32 devices in a mesh: dp: 16 (over z, y, x), tensor: 2 (over core).
Axes of the slice: x: 2, y: 2, z: 4, core: 2. Of those that a mesh axis runs over, the one named last changes fastest.
Arguments:
- tokens: bfloat16 [32, 1024, 512], P('dp', 'tensor'), may hold values from -6 to 6
- memory: bfloat16 [32, 1024, 512], P('dp', 'tensor'), may hold values from -6 to 6
- dec_segment: int32 [32, 1024], P('dp'), may hold values from 0 to 3, as said below
- enc_segment: int32 [32, 1024], P('dp'), may hold values from 0 to 3, as said below
- slot_left: int32 [32, 512], P('dp'), may hold values from 0 to 1022
- self_qkv: bfloat16 [3, 512, 512], P(None, None, 'tensor'), may hold values from -0.25 to 0.25
- self_bias: bfloat16 [2, 512], P(None, 'tensor'), may hold values from -3 to 3
- self_out: bfloat16 [512, 512], P('tensor'), may hold values from -4 to 4
- self_out_bias: bfloat16 [512], replicated, may hold values from -3 to 3
- cross_qkv: bfloat16 [3, 512, 512], P(None, None, 'tensor'), may hold values from -0.25 to 0.25
- cross_bias: bfloat16 [2, 512], P(None, 'tensor'), may hold values from -3 to 3
- cross_out: bfloat16 [512, 512], P('tensor'), may hold values from -4 to 4
- cross_out_bias: bfloat16 [512], replicated, may hold values from -3 to 3
- ffn_in: bfloat16 [512, 2048], P(None, 'tensor'), may hold values from -0.25 to 0.25
- ffn_in_bias: bfloat16 [2048], P('tensor'), may hold values from -3 to 3
- ffn_out: bfloat16 [2048, 512], P('tensor'), may hold values from -0.125 to 0.125
- ffn_out_bias: bfloat16 [512], replicated, may hold values from -3 to 3
- norm_gain: bfloat16 [3, 512], replicated, may hold values from 0.5 to 1.5
- norm_bias: bfloat16 [3, 512], replicated, may hold values from -2 to 2
- slot_weight: bfloat16 [1024, 512], P(None, 'tensor'), may hold values from -0.1875 to 0.1875
- slot_bias: bfloat16 [512], P('tensor'), may hold values from -3 to 3
- grad_output: bfloat16 [32, 1024, 512], P('dp', 'tensor'), may hold values from -6 to 6
- grad_slots: bfloat16 [32, 512, 512], P('dp', None, 'tensor'), may hold values from -6 to 6
Outputs:
- output: bfloat16 [32, 1024, 512], P('dp', 'tensor')
- slot_states: bfloat16 [32, 512, 512], P('dp', None, 'tensor')
- grad_input: bfloat16 [32, 1024, 512], P('dp', 'tensor')
- grad_memory: bfloat16 [32, 1024, 512], P('dp', 'tensor')
- grad_self_qkv: float32 [3, 512, 512], P(None, None, 'tensor')
- grad_self_bias: float32 [2, 512], P(None, 'tensor')
- grad_self_out: float32 [512, 512], P('tensor')
- grad_self_out_bias: float32 [512], replicated
- grad_cross_qkv: float32 [3, 512, 512], P(None, None, 'tensor')
- grad_cross_bias: float32 [2, 512], P(None, 'tensor')
- grad_cross_out: float32 [512, 512], P('tensor')
- grad_cross_out_bias: float32 [512], replicated
- grad_ffn_in: float32 [512, 2048], P(None, 'tensor')
- grad_ffn_in_bias: float32 [2048], P('tensor')
- grad_ffn_out: float32 [2048, 512], P('tensor')
- grad_ffn_out_bias: float32 [512], replicated
- grad_norm_gain: float32 [3, 512], replicated
- grad_norm_bias: float32 [3, 512], replicated
- grad_slot_weight: float32 [1024, 512], P(None, 'tensor')
- grad_slot_bias: float32 [512], P('tensor')
The draws below stay inside these ranges and needn't reach their ends.
Inputs may be any that keep to these rules, and one draw needn't show every extreme that they name: `dec_segment`: within a row the ids never fall, and each of the 4 documents has at least one decoder token and at least one encoder token in that row. `enc_segment`: within a row the ids never fall; the documents are those of dec_segment in the same row. Slot j of row r pairs the states at positions slot_left[r, j] and slot_left[r, j] + 1 of that row.
All inputs are finite; a program needn't handle non-finite values.
Results may differ from the reference program's by a relative error of at most 0.023.
Values may be sent and summed in bfloat16 or wider, within the bound.
No kernel may reach another device: no remote copies, remote signals or barrier semaphores. Data moves between devices by JAX's collectives and lax.ppermute only.
A program may use at most 192 MiB of HBM per device.

```python
import jax
import jax.numpy as jnp
from jax import lax

D = 512
HEADS = 8
HEAD_DIM = 64
FF = 2048
SEQ = 1024
MEM = 1024
SLOTS = 512
DOCS = 4
ROWS = 32
DEC_SHARD = 512
MEM_SHARD = 512


def long_document(key):
    return jax.random.randint(key, (ROWS, 1), 0, DOCS)


def document_ids(key, longest, length, shard_len):
    doc_sizes = jax.random.randint(key, (ROWS, DOCS), 1, shard_len // DOCS + 1)
    numbers = jnp.arange(DOCS)[None, :]
    doc_sizes = jnp.where(numbers == longest, 0, doc_sizes)
    doc_sizes = jnp.where(numbers == longest, length - jnp.sum(doc_sizes, axis=1, keepdims=True), doc_sizes)
    doc_ends = jnp.cumsum(doc_sizes, axis=1)
    places = jnp.arange(length)[None, :, None]
    return jnp.sum((places >= doc_ends[:, None, :]).astype(jnp.int32), axis=2).astype(jnp.int32)


def draw_dec_segment(key, part):
    longest = long_document(key)
    key = jax.random.fold_in(key, 11)
    return document_ids(key, longest, SEQ, DEC_SHARD)


def draw_enc_segment(key, part):
    longest = long_document(key)
    key = jax.random.fold_in(key, 12)
    return document_ids(key, longest, MEM, MEM_SHARD)


def touch_ends(values, rng, smallest, top_value):
    longest = values.shape.index(max(values.shape))
    spots = []
    for shift in (0, 1):
        where = [jax.random.randint(jax.random.fold_in(rng, axis), (), 0, length) for axis, length in enumerate(values.shape)]
        where[longest] = (where[longest] + shift) % values.shape[longest]
        spots.append(tuple(where))
    return values.at[spots[0]].set(smallest).at[spots[1]].set(top_value)


def level_of(stream_key, extent, split, smallest, high):
    gain = 1.0
    for dim, parts in split:
        steps = jax.random.uniform(jax.random.fold_in(jax.random.fold_in(stream_key, 6), dim), (parts,), jnp.float32, smallest / len(split), high / len(split))
        gain = gain * jnp.repeat(jnp.exp(steps), extent[dim] // parts).reshape((-1,) + (1,) * (len(extent) - 1 - dim))
    return gain


def scatter_about(stream_key, extent, scale, reach, split=(), held_as=jnp.bfloat16):
    factor_of = level_of(stream_key, extent, split, -0.22, 0.18) if split else 1.0
    array = jax.random.normal(stream_key, extent, jnp.float32) * scale * factor_of
    return jnp.minimum(jnp.maximum(array, -reach), reach).astype(held_as)


def setup_inputs(seed: int = 0) -> dict:
    splits = jax.random.split(jax.random.key(seed), 24)
    tokens = scatter_about(splits[0], (ROWS, SEQ, D), 1.0, 6.0, ((0, 16), (1, 2)))
    memory = scatter_about(splits[1], (ROWS, MEM, D), 1.0, 6.0, ((0, 16), (1, 2)))
    dec_segment = draw_dec_segment(jax.random.fold_in(splits[23], 71), 0)
    enc_segment = draw_enc_segment(jax.random.fold_in(splits[23], 71), 0)
    slot_left = touch_ends(jax.random.randint(splits[4], (ROWS, SLOTS), 0, SEQ - 1), jax.random.fold_in(splits[4], 1), 0, (SEQ - 1) - 1).astype(jnp.int32)
    self_qkv = scatter_about(splits[5], (3, D, D), D ** -0.5, 0.25, ((2, 2),))
    self_bias = scatter_about(splits[6], (2, D), 0.5, 3.0, ((1, 2),))
    self_out = scatter_about(splits[7], (D, D), 2 ** -0.5, 4.0, ((0, 2),))
    self_out_bias = scatter_about(splits[8], (D,), 0.5, 3.0)
    cross_qkv = scatter_about(splits[9], (3, D, D), D ** -0.5, 0.25, ((2, 2),))
    cross_bias = scatter_about(splits[10], (2, D), 0.5, 3.0, ((1, 2),))
    cross_out = scatter_about(splits[11], (D, D), 2 ** -0.5, 4.0, ((0, 2),))
    cross_out_bias = scatter_about(splits[12], (D,), 0.5, 3.0)
    ffn_in = scatter_about(splits[13], (D, FF), D ** -0.5, 0.25, ((1, 2),))
    ffn_in_bias = scatter_about(splits[14], (FF,), 0.5, 3.0, ((0, 2),))
    ffn_out = scatter_about(splits[15], (FF, D), FF ** -0.5, 0.125, ((0, 2),))
    ffn_out_bias = scatter_about(splits[16], (D,), 0.5, 3.0)
    norm_gain = jnp.clip(1.0 + 0.1 * jax.random.normal(splits[17], (3, D), jnp.float32), 0.5, 1.5).astype(jnp.bfloat16)
    norm_bias = scatter_about(splits[18], (3, D), 0.3, 2.0)
    slot_weight = scatter_about(splits[19], (2 * D, D), (2 * D) ** -0.5, 0.1875, ((1, 2),))
    slot_bias = scatter_about(splits[20], (D,), 0.5, 3.0, ((0, 2),))
    grad_output = scatter_about(splits[21], (ROWS, SEQ, D), 1.0, 6.0, ((0, 16), (1, 2)))
    grad_slots = scatter_about(splits[22], (ROWS, SLOTS, D), 1.0, 6.0, ((0, 16), (2, 2)))
    return dict(tokens=tokens, memory=memory, dec_segment=dec_segment, enc_segment=enc_segment, slot_left=slot_left, self_qkv=self_qkv, self_bias=self_bias, self_out=self_out, self_out_bias=self_out_bias, cross_qkv=cross_qkv, cross_bias=cross_bias, cross_out=cross_out, cross_out_bias=cross_out_bias, ffn_in=ffn_in, ffn_in_bias=ffn_in_bias, ffn_out=ffn_out, ffn_out_bias=ffn_out_bias, norm_gain=norm_gain, norm_bias=norm_bias, slot_weight=slot_weight, slot_bias=slot_bias, grad_output=grad_output, grad_slots=grad_slots)


@jax.custom_vjp
def low(v):
    return lax.optimization_barrier(v.astype(jnp.bfloat16)).astype(jnp.float32)

@jax.custom_vjp
def low_back(v):
    return v

def low_keep(v):
    return (low(v), None)

def low_pass(kept, grad):
    return (grad,)

def back_keep(v):
    return (v, None)

def back_low(kept, grad):
    return (low(grad),)
low.defvjp(low_keep, low_pass)
low_back.defvjp(back_keep, back_low)
EPSILON = 1e-05
MASKED = -1e+30
GELU_C = 0.7978845608028654

def gelu(inputs):
    return 0.5 * inputs * (1.0 + jnp.tanh(GELU_C * (inputs + 0.044715 * inputs * inputs * inputs)))

def layer_norm(values, scaling, offset):
    centre = values - lax.optimization_barrier(jnp.mean(values, axis=-1, keepdims=True))
    spread = lax.optimization_barrier(jnp.mean(centre * centre, axis=-1, keepdims=True))
    return centre * lax.rsqrt(spread + EPSILON) * scaling + offset

def matmul(left_side, right_side):
    return jnp.dot(left_side, right_side, precision=lax.Precision.HIGHEST, preferred_element_type=jnp.float32)

def attention(queries, keys_in, values_in, left_segment, right_segment):
    query_heads = queries.reshape(queries.shape[0], HEADS, HEAD_DIM)
    key_heads = keys_in.reshape(keys_in.shape[0], HEADS, HEAD_DIM)
    value_heads = values_in.reshape(values_in.shape[0], HEADS, HEAD_DIM)
    scores = jnp.einsum('qhd,khd->hqk', query_heads, key_heads, precision=lax.Precision.HIGHEST) * HEAD_DIM ** (-0.5)
    scores = low_back(scores)
    allowed = left_segment[:, None] == right_segment[None, :]
    scores = jnp.where(allowed[None], scores, MASKED)
    row_max = lax.optimization_barrier(jnp.max(scores, axis=-1, keepdims=True))
    weights = jnp.exp(scores - row_max)
    probabilities = low(weights / lax.optimization_barrier(jnp.sum(weights, axis=-1, keepdims=True)))
    context = jnp.einsum('hqk,khd->qhd', probabilities, value_heads, precision=lax.Precision.HIGHEST)
    return low(low_back(context.reshape(queries.shape[0], HEADS * HEAD_DIM)))

def forward_row(params, row_tokens, row_memory, dec_row, enc_row, left_row):
    self_qkv, self_bias, self_out, self_out_bias, cross_qkv, cross_bias, cross_out, cross_out_bias, ffn_in, ffn_in_bias, ffn_out, ffn_out_bias, norm_gain, norm_bias, slot_weight, slot_bias = params
    self_query = low(low_back(matmul(row_tokens, self_qkv[0]) + self_bias[0]))
    self_key = low(low_back(matmul(row_tokens, self_qkv[1])))
    self_value = low(low_back(matmul(row_tokens, self_qkv[2]) + self_bias[1]))
    context = attention(self_query, self_key, self_value, dec_row, dec_row)
    branch = low_back(matmul(context, self_out) + self_out_bias)
    first_norm = low(layer_norm(row_tokens + branch, norm_gain[0], norm_bias[0]))
    cross_query = low(low_back(matmul(first_norm, cross_qkv[0]) + cross_bias[0]))
    cross_key = low(low_back(matmul(row_memory, cross_qkv[1])))
    cross_value = low(low_back(matmul(row_memory, cross_qkv[2]) + cross_bias[1]))
    cross_context = attention(cross_query, cross_key, cross_value, dec_row, enc_row)
    cross_branch = low_back(matmul(cross_context, cross_out) + cross_out_bias)
    second_norm = low(layer_norm(first_norm + cross_branch, norm_gain[1], norm_bias[1]))
    inner_pre = low_back(matmul(second_norm, ffn_in) + ffn_in_bias)
    hidden = low(gelu(inner_pre))
    ffn_branch = low_back(matmul(hidden, ffn_out) + ffn_out_bias)
    output = low(layer_norm(second_norm + ffn_branch, norm_gain[2], norm_bias[2]))
    slot_pair = jnp.concatenate([output[left_row], output[left_row + 1]], axis=-1)
    slot_states = matmul(slot_pair, slot_weight) + slot_bias
    return (output, slot_states)

def reference(tokens, memory, dec_segment, enc_segment, slot_left, self_qkv, self_bias, self_out, self_out_bias, cross_qkv, cross_bias, cross_out, cross_out_bias, ffn_in, ffn_in_bias, ffn_out, ffn_out_bias, norm_gain, norm_bias, slot_weight, slot_bias, grad_output, grad_slots):
    params = tuple((weight_arg.astype(jnp.float32) for weight_arg in (self_qkv, self_bias, self_out, self_out_bias, cross_qkv, cross_bias, cross_out, cross_out_bias, ffn_in, ffn_in_bias, ffn_out, ffn_out_bias, norm_gain, norm_bias, slot_weight, slot_bias)))

    def one_row(totals, row_data):
        row_tokens, row_memory, dec_row, enc_row, left_row, out_cot, slot_cot = row_data

        def local_forward(weights_all, tokens_in, memory_in):
            return forward_row(weights_all, tokens_in, memory_in, dec_row, enc_row, left_row)
        results, pullback = jax.vjp(local_forward, params, row_tokens.astype(jnp.float32), row_memory.astype(jnp.float32))
        param_grads, tokens_grad, memory_grad = pullback((out_cot.astype(jnp.float32), slot_cot.astype(jnp.float32)))
        totals = jax.tree.map(lambda first, second: first + second, totals, param_grads)
        return (totals, (results[0].astype(jnp.bfloat16), results[1].astype(jnp.bfloat16), tokens_grad.astype(jnp.bfloat16), memory_grad.astype(jnp.bfloat16)))
    zero_grads = jax.tree.map(jnp.zeros_like, params)
    totals, (output, slot_states, grad_input, grad_memory) = lax.scan(one_row, zero_grads, (tokens, memory, dec_segment, enc_segment, slot_left, grad_output, grad_slots))
    grad_self_qkv, grad_self_bias, grad_self_out, grad_self_out_bias, grad_cross_qkv, grad_cross_bias, grad_cross_out, grad_cross_out_bias, grad_ffn_in, grad_ffn_in_bias, grad_ffn_out, grad_ffn_out_bias, grad_norm_gain, grad_norm_bias, grad_slot_weight, grad_slot_bias = totals
    return (output, slot_states, grad_input, grad_memory, grad_self_qkv, grad_self_bias, grad_self_out, grad_self_out_bias, grad_cross_qkv, grad_cross_bias, grad_cross_out, grad_cross_out_bias, grad_ffn_in, grad_ffn_in_bias, grad_ffn_out, grad_ffn_out_bias, grad_norm_gain, grad_norm_bias, grad_slot_weight, grad_slot_bias)
```

```python
import functools

import jax
import jax.numpy as jnp
from jax import lax
from jax.experimental import pallas as pl
from jax.experimental.pallas import tpu as pltpu
from jax.sharding import PartitionSpec as P

HEAD_DIM = 64
EPSILON = 1e-05
MASKED = -1e30
GELU_C = 0.7978845608028654
GELU_A = 0.044715
LOG2E = 1.4426950408889634
LN2 = 0.6931471805599453
SCALE = HEAD_DIM ** (-0.5)
AUG = 80
QB = 256
TB = 256
VMEM_LIMIT = 56 * 2**20

bf16 = jnp.bfloat16
f32 = jnp.float32


def dg(a, b, ca, cb):
    return lax.dot_general(a, b, (((ca,), (cb,)), ((), ())), preferred_element_type=f32)


def column_of(row):
    return jnp.broadcast_to(row.astype(f32), (8, row.shape[1])).T[:, 0:1]


def three_parts(row):
    high = row.astype(bf16).astype(f32)
    rest = row - high
    middle = rest.astype(bf16).astype(f32)
    return high, middle, (rest - middle)


def tall(shape, rows):
    index = lax.broadcasted_iota(jnp.int32, shape, 0)
    block = jnp.zeros(shape, f32)
    for at, row in rows.items():
        block = jnp.where(index == at, jnp.broadcast_to(row, shape), block)
    return block


def norm_parts(y):
    centre = y - jnp.mean(y, axis=-1, keepdims=True)
    spread = lax.rsqrt(jnp.mean(centre * centre, axis=-1, keepdims=True) + EPSILON)
    return centre * spread, spread


def norm_back(xhat, spread, gain, e):
    a = e * gain
    dy = (a - jnp.mean(a, axis=-1, keepdims=True) - xhat * jnp.mean(a * xhat, axis=-1, keepdims=True)) * spread
    return dy, jnp.sum(e * xhat, axis=0, keepdims=True), jnp.sum(e, axis=0, keepdims=True)


def vmem_call(body, outs, scratch=(), cost=None):
    vm = pl.BlockSpec(memory_space=pltpu.VMEM)

    def call(*args):
        return pl.pallas_call(
            body,
            out_shape=[jax.ShapeDtypeStruct(s, d) for s, d in outs],
            in_specs=[vm] * len(args),
            out_specs=[vm] * len(outs),
            scratch_shapes=list(scratch),
            compiler_params=pltpu.CompilerParams(vmem_limit_bytes=VMEM_LIMIT),
            cost_estimate=cost,
        )(*args)

    return call


def attend_forward(cross, *refs):
    if cross:
        (src, mem_m, mem_t, seg_q, seg_k, w_m, w_t, b_m, b_t, wo_m, wo_t, ob, gain, shift, qa, ka, va, ctx, y_out, h_out) = refs
        length = src.shape[0]
        half = length // 2
        src_q = [src[0:half, :], src[half:length, :]]
        src_k = [mem_m[...], mem_t[...]]
    else:
        (x_m, x_t, seg_q, w_m, w_t, b_m, b_t, wo_m, wo_t, ob, gain, shift, qa, ka, va, ctx, y_out, h_out) = refs
        seg_k = seg_q
        half = x_m.shape[0]
        length = 2 * half
        src_q = src_k = [x_m[...], x_t[...]]
    heads_half = w_m.shape[2] // HEAD_DIM
    heads = 2 * heads_half
    shape16 = (16, length)
    index = lax.broadcasted_iota(jnp.int32, shape16, 0)
    same_q = index == jnp.broadcast_to(seg_q[...], shape16)
    same_k = index == jnp.broadcast_to(seg_k[...], shape16)
    q_extra = jnp.where(index < 4, jnp.where(same_q, 0.0, MASKED), 0.0).astype(bf16)
    k_extra = jnp.where(index < 4, jnp.where(same_k, 1.0, 0.0), jnp.where(index < 7, 1.0, 0.0)).astype(bf16)
    v_extra = jnp.where(index < 3, 1.0, 0.0).astype(bf16)
    for h in range(heads):
        qa[h, 64:80, :] = q_extra
        ka[h, 64:80, :] = k_extra
        va[h, 64:80, :] = v_extra
    for side, (w, b) in enumerate(((w_m, b_m), (w_t, b_t))):
        bias_q = column_of(b[0:1, :])
        bias_v = column_of(b[1:2, :])
        for piece in range(2):
            at = slice(piece * half, (piece + 1) * half)
            q = ((dg(w[0], src_q[piece], 0, 1) + bias_q) * (SCALE * LOG2E)).astype(bf16)
            k = dg(w[1], src_k[piece], 0, 1).astype(bf16)
            v = (dg(w[2], src_k[piece], 0, 1) + bias_v).astype(bf16)
            for i in range(heads_half):
                h = side * heads_half + i
                rows = slice(i * HEAD_DIM, (i + 1) * HEAD_DIM)
                qa[h, 0:64, at] = q[rows]
                ka[h, 0:64, at] = k[rows]
                va[h, 0:64, at] = v[rows]

    def one_head(h, _):
        keys = ka[h]
        values = va[h]
        for i in range(length // QB):
            at = slice(i * QB, (i + 1) * QB)
            scores = dg(keys, qa[h, :, at], 0, 0)
            top = jnp.max(scores, axis=0, keepdims=True)
            weights = jnp.exp2(scores - top).astype(bf16)
            out = dg(values, weights, 1, 0)
            total = out[64:65, :]
            ctx[pl.ds(pl.multiple_of(h * HEAD_DIM, HEAD_DIM), HEAD_DIM), at] = (out[0:64, :] * (1.0 / total)).astype(bf16)
            high, middle, low = three_parts(-(top + jnp.log2(total)))
            extra = tall((16, QB), {4: high, 5: middle, 6: low})
            qa[h, 64:80, at] = qa[h, 64:80, at] + extra.astype(bf16)
        return 0

    lax.fori_loop(0, heads, one_head, 0)
    hw = w_m.shape[2]
    for i in range(length // TB):
        at = slice(i * TB, (i + 1) * TB)
        y = dg(ctx[0:hw, at], wo_m[...], 0, 0) + dg(ctx[hw:, at], wo_t[...], 0, 0) + ob[...].astype(f32)
        piece, inner = divmod(i * TB, half)
        y = y + src_q[piece][inner : inner + TB, :].astype(f32)
        y_out[at, :] = y
        xhat, _ = norm_parts(y)
        h_out[at, :] = (xhat * gain[...].astype(f32) + shift[...].astype(f32)).astype(bf16)


def attend_backward(cross, *refs):
    if cross:
        (dy, qa, ka, va, ctx, src, mem_m, mem_t, w_m, w_t, wo_m, wo_t, y_prev, gain,
         g_m, g_t, small, dprev, dmem_m, dmem_t, da, dq, dk, dv) = refs
        length = src.shape[0]
        half = length // 2
        src_q = [src[0:half, :], src[half:length, :]]
        src_k = [mem_m[...], mem_t[...]]
        mem_outs = (dmem_m, dmem_t)
    else:
        (dy, qa, ka, va, ctx, x_m, x_t, w_m, w_t, wo_m, wo_t,
         g_m, g_t, small, dx_m, dx_t, da, dq, dk, dv) = refs
        half = x_m.shape[0]
        length = 2 * half
        src_q = src_k = [x_m[...], x_t[...]]
    hw = w_m.shape[2]
    heads = 2 * hw // HEAD_DIM
    width = dy.shape[1]
    dout = dy[...].astype(bf16)
    for side, (wo, g) in enumerate(((wo_m, g_m), (wo_t, g_t))):
        dctx = dg(wo[...], dout, 1, 1).astype(bf16)
        g[3 * hw : 4 * hw, :] = dg(ctx[side * hw : (side + 1) * hw, :], dout, 1, 0).astype(g.dtype)
        for i in range(hw // HEAD_DIM):
            da[side * (hw // HEAD_DIM) + i, 0:64, :] = dctx[i * HEAD_DIM : (i + 1) * HEAD_DIM]

    def one_head(h, _):
        rows = pl.ds(pl.multiple_of(h * HEAD_DIM, HEAD_DIM), HEAD_DIM)
        keys = ka[h]
        values = va[h]
        grads = da[h, 0:64, :]
        inner = jnp.sum(grads.astype(f32) * ctx[rows, :].astype(f32), axis=0, keepdims=True)
        high, middle, low = three_parts(-inner)
        da[h, 64:80, :] = tall((16, length), {0: high, 1: middle, 2: low}).astype(bf16)
        dv_sum = jnp.zeros((HEAD_DIM, length), f32)
        dk_sum = jnp.zeros((HEAD_DIM, length), f32)
        for i in range(length // QB):
            at = slice(i * QB, (i + 1) * QB)
            weights = jnp.exp2(dg(qa[h, :, at], keys, 0, 0))
            spread = dg(da[h, :, at], values, 0, 0)
            ds = (weights * spread).astype(bf16)
            dv_sum = dv_sum + dg(da[h, 0:64, at], weights.astype(bf16), 1, 0)
            dk_sum = dk_sum + dg(qa[h, 0:64, at], ds, 1, 0)
            dq[rows, at] = (dg(keys[0:64], ds, 1, 1) * SCALE).astype(bf16)
        dk[rows, :] = (dk_sum * LN2).astype(bf16)
        dv[rows, :] = dv_sum.astype(bf16)
        return 0

    lax.fori_loop(0, heads, one_head, 0)

    for side, (w, g) in enumerate(((w_m, g_m), (w_t, g_t))):
        rows = slice(side * hw, (side + 1) * hw)
        for j, (grad, src_pair) in enumerate(((dq, src_q), (dk, src_k), (dv, src_k))):
            total = dg(src_pair[0], grad[rows, 0:half], 0, 1) + dg(src_pair[1], grad[rows, half:length], 0, 1)
            g[j * hw : (j + 1) * hw, 0:hw] = total[0 : width // 2].astype(g.dtype)
            g[j * hw : (j + 1) * hw, hw : 2 * hw] = total[width // 2 :].astype(g.dtype)
    ones = jnp.ones((8, length), bf16)
    small[...] = jnp.zeros(small.shape, f32)
    small[0:1, :] = dg(ones, dq[...], 1, 1)[0:1]
    small[1:2, :] = dg(ones, dv[...], 1, 1)[0:1]
    gain_sum = jnp.zeros((1, width), f32)
    shift_sum = jnp.zeros((1, width), f32)
    out_sum = jnp.zeros((1, width), f32)
    for i in range(length // TB):
        at = slice(i * TB, (i + 1) * TB)
        piece, inner = divmod(i * TB, half)
        there = slice(inner, inner + TB)
        e = dy[at, :] + dg(dq[0:hw, at], w_m[0], 0, 1) + dg(dq[hw:, at], w_t[0], 0, 1)
        rest = (
            dg(dk[0:hw, at], w_m[1], 0, 1)
            + dg(dk[hw:, at], w_t[1], 0, 1)
            + dg(dv[0:hw, at], w_m[2], 0, 1)
            + dg(dv[hw:, at], w_t[2], 0, 1)
        )
        if cross:
            mem_outs[piece][there, :] = rest.astype(bf16)
            xhat, spread = norm_parts(y_prev[at, :])
            back, d_gain, d_shift = norm_back(xhat, spread, gain[...].astype(f32), e)
            dprev[at, :] = back
            gain_sum += d_gain
            shift_sum += d_shift
            out_sum += jnp.sum(back.astype(bf16).astype(f32), axis=0, keepdims=True)
        else:
            (dx_m, dx_t)[piece][there, :] = (e + rest).astype(bf16)
    if cross:
        small[2:3, :] = gain_sum
        small[3:4, :] = shift_sum
        small[4:5, :] = out_sum


def feed_forward(*refs):
    (h2, y2, go_m, go_t, slot, gs_m, gs_t, ws_m, ws_t, bs_m, bs_t, wi_m, wi_t, bi_m, bi_t, wo_m, wo_t, ob,
     gain2, gain3, shift3,
     out_m, out_t, st_m, st_t, dy2, g_m, g_t, small, small_t,
     onehot, tl, tr, e3, outs, hid, dpre, slope, df_all) = refs
    length, width = h2.shape
    half = length // 2
    fw = wi_m.shape[1]
    sw = ws_m.shape[1]
    slots = gs_m.shape[0]
    place = lax.broadcasted_iota(jnp.int32, (length, slots), 0)
    onehot[...] = jnp.where(place == jnp.broadcast_to(slot[...], (length, slots)), 1.0, 0.0).astype(bf16)
    small[...] = jnp.zeros(small.shape, f32)
    small_t[...] = jnp.zeros(small_t.shape, f32)
    e3[0:half, :] = go_m[...].astype(f32)
    e3[half:length, :] = go_t[...].astype(f32)
    for side, (gs, ws) in enumerate(((gs_m, ws_m), (gs_t, ws_t))):
        cols = slice(side * sw, (side + 1) * sw)
        left = dg(onehot[...], gs[...], 1, 0)
        tl[:, cols] = left.astype(bf16)
        tr[:, cols] = pltpu.roll(left, 1, 0).astype(bf16)
        for i in range(length // TB):
            at = slice(i * TB, (i + 1) * TB)
            e3[at, :] += dg(tl[at, cols], ws[0:width, :], 1, 1) + dg(tr[at, cols], ws[width : 2 * width, :], 1, 1)

    def one_block(i, sums):
        gain3_sum, shift3_sum, gain2_sum, shift2_sum, ffn_out_sum, cross_out_sum, in_m_sum, in_t_sum = sums
        at = pl.ds(pl.multiple_of(i * TB, TB), TB)
        hb = h2[at, :]
        y3 = hb.astype(f32) + ob[...].astype(f32)
        for side, (wi, bi, wo) in enumerate(((wi_m, bi_m, wo_m), (wi_t, bi_t, wo_t))):
            cols = slice(side * fw, (side + 1) * fw)
            pre = dg(hb, wi[...], 1, 0) + bi[...].astype(f32)
            square = pre * pre
            tanh = jnp.tanh(pre * (GELU_C + GELU_C * GELU_A * square))
            gate = 0.5 + 0.5 * tanh
            hidden = (pre * gate).astype(bf16)
            hid[at, cols] = hidden
            slope[:, cols] = gate + (0.5 * pre) * (1.0 - tanh * tanh) * (GELU_C + 3.0 * GELU_C * GELU_A * square)
            y3 = y3 + dg(hidden, wo[...], 1, 0)
        xhat, spread = norm_parts(y3)
        outs[at, :] = (xhat * gain3[...].astype(f32) + shift3[...].astype(f32)).astype(bf16)
        dy3, d_gain, d_shift = norm_back(xhat, spread, gain3[...].astype(f32), e3[at, :])
        gain3_sum += d_gain
        shift3_sum += d_shift
        df = dy3.astype(bf16)
        df_all[at, :] = df
        ffn_out_sum += jnp.sum(df.astype(f32), axis=0, keepdims=True)
        e2 = dy3
        in_sums = []
        for side, (wi, wo, in_sum) in enumerate(((wi_m, wo_m, in_m_sum), (wi_t, wo_t, in_t_sum))):
            cols = slice(side * fw, (side + 1) * fw)
            back = (dg(df, wo[...], 1, 1) * slope[:, cols]).astype(bf16)
            dpre[at, cols] = back
            in_sums.append(in_sum + jnp.sum(back.astype(f32), axis=0, keepdims=True))
            e2 = e2 + dg(back, wi[...], 1, 1)
        xhat, spread = norm_parts(y2[at, :])
        back2, d_gain, d_shift = norm_back(xhat, spread, gain2[...].astype(f32), e2)
        dy2[at, :] = back2
        gain2_sum += d_gain
        shift2_sum += d_shift
        cross_out_sum += jnp.sum(back2.astype(bf16).astype(f32), axis=0, keepdims=True)
        return gain3_sum, shift3_sum, gain2_sum, shift2_sum, ffn_out_sum, cross_out_sum, in_sums[0], in_sums[1]

    row = jnp.zeros((1, width), f32)
    wide = jnp.zeros((1, fw), f32)
    sums = lax.fori_loop(0, length // TB, one_block, (row, row, row, row, row, row, wide, wide))
    for at, total in enumerate(sums[0:6]):
        small[at : at + 1, :] = total
    for ref, total, gs in ((small, sums[6], gs_m), (small_t, sums[7], gs_t)):
        for i in range(fw // width):
            ref[6 + i : 7 + i, :] = total[:, i * width : (i + 1) * width]
        ref[6 + fw // width : 7 + fw // width, 0:sw] = jnp.sum(gs[...].astype(f32), axis=0, keepdims=True)
    out_m[...] = outs[0:half, :]
    out_t[...] = outs[half:length, :]

    for side, (g, ws, bs, st) in enumerate(((g_m, ws_m, bs_m, st_m), (g_t, ws_t, bs_t, st_t))):
        cols = slice(side * sw, (side + 1) * sw)
        top = dg(outs[...], ws[0:width, :], 1, 0)
        low = dg(outs[...], ws[width : 2 * width, :], 1, 0)
        state = (top + pltpu.roll(low, length - 1, 0) + bs[...].astype(f32)).astype(bf16)
        st[...] = dg(onehot[...], state, 0, 0).astype(bf16)
        g[0:width, 0:sw] = dg(outs[...], tl[:, cols], 0, 0).astype(g.dtype)
        g[0:width, sw : 2 * sw] = dg(outs[...], tr[:, cols], 0, 0).astype(g.dtype)
        for i in range(fw // width):
            block = slice(side * fw + i * width, side * fw + (i + 1) * width)
            rows = slice(width + i * width, 2 * width + i * width)
            g[rows, :] = dg(h2[...], dpre[:, block], 0, 0).astype(g.dtype)
            rows = slice(width + fw + i * width, 2 * width + fw + i * width)
            g[rows, :] = dg(hid[:, block], df_all[...], 0, 0).astype(g.dtype)


def swap(x):
    return lax.ppermute(x, "tensor", [(0, 1), (1, 0)])


def sum_rows(x, dp_size, dp_index, core):
    bits = dp_size.bit_length() - 1
    orders = [list(range(bits)), list(range(bits))]
    if bits > 2:
        orders[1] = [1, 2, 0] + list(range(3, bits))
    plan = []
    for step in range(bits):
        pairs = []
        for device in range(dp_size):
            for c in range(2):
                pairs.append((device * 2 + c, (device ^ (1 << orders[c][step])) * 2 + c))
        bit = jnp.where(core == 0, (dp_index >> orders[0][step]) & 1, (dp_index >> orders[1][step]) & 1)
        plan.append((pairs, bit))
    for pairs, bit in plan:
        count = x.shape[0] // 2
        away = lax.dynamic_slice_in_dim(x, (1 - bit) * count, count, 0)
        kept = lax.dynamic_slice_in_dim(x, bit * count, count, 0)
        got = lax.ppermute(away.astype(bf16), ("dp", "tensor"), pairs)
        x = kept.astype(f32) + got.astype(f32)
    x = x.astype(bf16)
    for pairs, bit in reversed(plan):
        got = lax.ppermute(x, ("dp", "tensor"), pairs)
        first = jnp.where(bit == 0, x, got)
        second = jnp.where(bit == 0, got, x)
        x = jnp.concatenate([first, second], axis=0)
    return x


def shards(dp_size, *args):
    (tokens, memory, dec_segment, enc_segment, slot_left, self_qkv, self_bias, self_out, self_out_bias,
     cross_qkv, cross_bias, cross_out, cross_out_bias, ffn_in, ffn_in_bias, ffn_out, ffn_out_bias,
     norm_gain, norm_bias, slot_weight, slot_bias, grad_output, grad_slots) = args
    core = lax.axis_index("tensor")
    dp_index = lax.axis_index("dp")
    half, width = tokens.shape[1], tokens.shape[2]
    length = 2 * half
    heads_w = self_qkv.shape[2]
    heads = 2 * heads_w // HEAD_DIM
    fw = ffn_in.shape[1]
    sw = slot_weight.shape[1]
    slots = slot_left.shape[1]

    def mine(x):
        return lax.dynamic_index_in_dim(x, core, 0, keepdims=False)

    def theirs(x):
        return lax.dynamic_index_in_dim(x, 1 - core, 0, keepdims=False)

    x_m, x_t = mine(tokens), swap(theirs(tokens))
    self_qkv_t = swap(self_qkv)
    biases = jnp.concatenate([self_bias.reshape(-1), cross_bias.reshape(-1), ffn_in_bias, slot_bias])
    biases_t = swap(biases)
    self_out_t = swap(self_out)
    mem_m, mem_t = mine(memory), swap(theirs(memory))
    cross_qkv_t = swap(cross_qkv)
    cross_out_t = swap(cross_out)
    ffn_in_t = swap(ffn_in)
    ffn_out_t = swap(ffn_out)
    slot_weight_t = swap(slot_weight)
    gs_m, gs_t = mine(grad_slots), swap(theirs(grad_slots))
    go_m, go_t = mine(grad_output), swap(theirs(grad_output))
    n1 = 2 * heads_w
    self_bias_t = biases_t[0:n1].reshape(2, heads_w)
    cross_bias_t = biases_t[n1 : 2 * n1].reshape(2, heads_w)
    ffn_in_bias_t = biases_t[2 * n1 : 2 * n1 + fw].reshape(1, fw)
    slot_bias_t = biases_t[2 * n1 + fw :].reshape(1, sw)
    seg_d = mine(dec_segment).reshape(2, half)
    seg_e = mine(enc_segment).reshape(2, half)
    seg_d = jnp.where(core == 0, seg_d, seg_d[::-1]).reshape(1, length)
    seg_e = jnp.where(core == 0, seg_e, seg_e[::-1]).reshape(1, length)
    place = mine(slot_left)
    place = jnp.where(core == 0, place, jnp.where(place >= half, place - half, place + half)).reshape(1, slots)

    aug = (heads, AUG, length)
    fwd_outs = [(aug, bf16), (aug, bf16), (aug, bf16), ((2 * heads_w, length), bf16), ((length, width), f32), ((length, width), bf16)]
    qa, ka, va, ctx, y1, h1 = vmem_call(functools.partial(attend_forward, False), fwd_outs)(
        x_m, x_t, seg_d, self_qkv, self_qkv_t, self_bias, self_bias_t, self_out, self_out_t,
        self_out_bias.reshape(1, width), norm_gain[0:1], norm_bias[0:1])
    qa2, ka2, va2, ctx2, y2, h2 = vmem_call(functools.partial(attend_forward, True), fwd_outs)(
        h1, mem_m, mem_t, seg_d, seg_e, cross_qkv, cross_qkv_t, cross_bias, cross_bias_t, cross_out, cross_out_t,
        cross_out_bias.reshape(1, width), norm_gain[1:2], norm_bias[1:2])
    g1_rows = width + 2 * fw
    (out_m, out_t, st_m, st_t, dy2, g1_m, g1_t, small1, small1_t) = vmem_call(
        feed_forward,
        [((half, width), bf16), ((half, width), bf16), ((slots, sw), bf16), ((slots, sw), bf16), ((length, width), f32),
         ((g1_rows, width), f32), ((g1_rows, width), bf16), ((16, width), f32), ((16, width), f32)],
        [pltpu.VMEM((length, slots), bf16), pltpu.VMEM((length, 2 * sw), bf16), pltpu.VMEM((length, 2 * sw), bf16),
         pltpu.VMEM((length, width), f32), pltpu.VMEM((length, width), bf16), pltpu.VMEM((length, 2 * fw), bf16),
         pltpu.VMEM((length, 2 * fw), bf16), pltpu.VMEM((TB, 2 * fw), f32), pltpu.VMEM((length, width), bf16)],
    )(h2, y2, go_m, go_t, place, gs_m, gs_t, slot_weight, slot_weight_t, slot_bias.reshape(1, sw), slot_bias_t,
      ffn_in, ffn_in_t, ffn_in_bias.reshape(1, fw), ffn_in_bias_t, ffn_out, ffn_out_t, ffn_out_bias.reshape(1, width),
      norm_gain[1:2], norm_gain[2:3], norm_bias[2:3])
    g2_rows = 4 * heads_w
    bwd_scratch = [pltpu.VMEM(aug, bf16)] + [pltpu.VMEM((2 * heads_w, length), bf16)] * 3
    g_outs = [((g2_rows, width), f32), ((g2_rows, width), bf16), ((8, width), f32)]
    g2_m, g2_t, small2, dy1, dmem_m, dmem_t = vmem_call(
        functools.partial(attend_backward, True),
        g_outs + [((length, width), f32), ((half, width), bf16), ((half, width), bf16)], bwd_scratch,
    )(dy2, qa2, ka2, va2, ctx2, h1, mem_m, mem_t, cross_qkv, cross_qkv_t, cross_out, cross_out_t, y1, norm_gain[0:1])
    g3_m, g3_t, small3, dx_m, dx_t = vmem_call(
        functools.partial(attend_backward, False),
        g_outs + [((half, width), bf16), ((half, width), bf16)], bwd_scratch,
    )(dy1, qa, ka, va, ctx, x_m, x_t, self_qkv, self_qkv_t, self_out, self_out_t)

    def together(kept, sent):
        got = swap(sent)
        first = jnp.where(core == 0, kept, got)
        second = jnp.where(core == 0, got, kept)
        return jnp.stack([first, second])

    output = together(out_m, out_t)
    slot_states = together(st_m, st_t)
    grad_memory = together(dmem_m, dmem_t)
    grad_input = together(dx_m, dx_t)

    def summed(g_m, g_t):
        total = g_m + swap(g_t).astype(f32)
        rows = total.shape[0]
        return sum_rows(total.reshape(dp_size, rows // dp_size, width), dp_size, dp_index, core).reshape(rows, width).astype(f32)

    g1 = summed(g1_m, g1_t)
    g2 = summed(g2_m, g2_t)
    gains = [small2[2:3], small1[2:3], small1[0:1]]
    shifts = [small2[3:4], small1[3:4], small1[1:2]]
    outs_b = [small2[4:5], small1[5:6], small1[4:5]]
    both = gains + shifts + outs_b
    wide = fw // width
    def own(lo, ref):
        cut = slice(lo * heads_w, (lo + 1) * heads_w)
        return [jnp.concatenate([small3[0:1, cut], small3[1:2, cut]], axis=1),
                jnp.concatenate([small2[0:1, cut], small2[1:2, cut]], axis=1)] + [ref[6 : 7 + wide]]
    rows_m = jnp.concatenate(both + own(0, small1), axis=0)
    rows_t = jnp.concatenate(both + own(1, small1_t), axis=0)
    extra = -rows_m.shape[0] % dp_size
    rows_m = jnp.pad(rows_m, ((0, extra), (0, 0)))
    rows_t = jnp.pad(rows_t, ((0, extra), (0, 0)))
    rest = rows_m + swap(rows_t.astype(bf16)).astype(f32)
    tail = g3_m + swap(g3_t).astype(f32)
    rows = tail.shape[0] // dp_size
    more = rest.shape[0] // dp_size
    tail = jnp.concatenate([tail.reshape(dp_size, rows, width), rest.reshape(dp_size, more, width)], axis=1)
    tail = sum_rows(tail, dp_size, dp_index, core).astype(f32)
    g3 = tail[:, 0:rows].reshape(-1, width)
    rest = tail[:, rows:].reshape(-1, width)

    def qkv_of(g):
        cut = g[0 : 3 * heads_w].reshape(3, heads_w, 2, heads_w)
        return jnp.concatenate([cut[:, :, 0], cut[:, :, 1]], axis=1)

    grad_slot_weight = jnp.concatenate([g1[0:width, 0:sw], g1[0:width, sw : 2 * sw]], axis=0)
    grad_ffn_in = jnp.concatenate([g1[width + i * width : 2 * width + i * width] for i in range(wide)], axis=1)
    grad_ffn_out = g1[width + fw :]
    return (
        output,
        slot_states,
        grad_input,
        grad_memory,
        qkv_of(g3),
        rest[9].reshape(2, heads_w),
        g3[3 * heads_w :],
        rest[6],
        qkv_of(g2),
        rest[10].reshape(2, heads_w),
        g2[3 * heads_w :],
        rest[7],
        grad_ffn_in,
        rest[11 : 11 + wide].reshape(fw),
        grad_ffn_out,
        rest[8],
        rest[0:3],
        rest[3:6],
        grad_slot_weight,
        rest[11 + wide, 0:sw],
    )


def solution(mesh):
    row3 = P("dp", "tensor", None)
    seg = P("dp", None)
    col3 = P(None, None, "tensor")
    col2 = P(None, "tensor")
    out2 = P("tensor", None)
    one = P("tensor")
    in_specs = (row3, row3, seg, seg, seg, col3, col2, out2, P(), col3, col2, out2, P(), col2, one, out2, P(), P(), P(),
                col2, one, row3, P("dp", None, "tensor"))
    out_specs = (row3, P("dp", None, "tensor"), row3, row3, col3, col2, out2, P(), col3, col2, out2, P(), col2, one, out2,
                 P(), P(), P(), col2, one)
    body = functools.partial(shards, mesh.shape["dp"])
    return jax.shard_map(body, mesh=mesh, in_specs=in_specs, out_specs=out_specs, check_vma=False)
```

```python
import functools

import jax
import jax.numpy as jnp
from jax import lax
from jax.experimental import pallas as pl
from jax.experimental.pallas import tpu as pltpu
from jax.sharding import PartitionSpec as P

HEAD_DIM = 64
EPSILON = 1e-05
MASKED = -1e30
GELU_C = 0.7978845608028654
GELU_A = 0.044715
LOG2E = 1.4426950408889634
LN2 = 0.6931471805599453
SCALE = HEAD_DIM ** (-0.5)
AUG = 80
QB = 256
FWD_QB = 1024
FWD_HEADS = 2
PAIR_ROWS = 512
SELF_GROUPS = ((1,), (0,))
TB = 256
VMEM_LIMIT = 63 * 2**20

bf16 = jnp.bfloat16
f32 = jnp.float32


def dg(a, b, ca, cb):
    return lax.dot_general(a, b, (((ca,), (cb,)), ((), ())), preferred_element_type=f32)


def column_of(row):
    return jnp.broadcast_to(row.astype(f32), (8, row.shape[1])).T[:, 0:1]


def three_parts(row):
    high = row.astype(bf16).astype(f32)
    rest = row - high
    middle = rest.astype(bf16).astype(f32)
    return high, middle, (rest - middle)


def tall(shape, rows):
    index = lax.broadcasted_iota(jnp.int32, shape, 0)
    block = jnp.zeros(shape, f32)
    for at, row in rows.items():
        block = jnp.where(index == at, jnp.broadcast_to(row, shape), block)
    return block


def norm_parts(y):
    centre = y - jnp.mean(y, axis=-1, keepdims=True)
    spread = lax.rsqrt(jnp.mean(centre * centre, axis=-1, keepdims=True) + EPSILON)
    return centre * spread, spread


def norm_back(xhat, spread, gain, e):
    a = e * gain
    dy = (a - jnp.mean(a, axis=-1, keepdims=True) - xhat * jnp.mean(a * xhat, axis=-1, keepdims=True)) * spread
    return dy, jnp.sum(e * xhat, axis=0, keepdims=True), jnp.sum(e, axis=0, keepdims=True)


ANY = pl.BlockSpec(memory_space=pl.ANY)
HBM = pl.BlockSpec(memory_space=pltpu.HBM)
VMEM = pl.BlockSpec(memory_space=pltpu.VMEM)
SMEM = pl.BlockSpec(memory_space=pltpu.SMEM)


class Staged:
    def __init__(self, far, near, sems, first, pick=None):
        self.far, self.near, self.sems, self.next, self.pending, self.pick = far, near, sems, first, [], pick

    def load(self):
        source = self.far if self.pick is None else self.far.at[self.pick]
        copy = pltpu.make_async_copy(source, self.near, self.sems.at[self.next])
        copy.start()
        self.pending.append(copy)

    def store(self, rows=None):
        near, far = (self.near, self.far) if rows is None else (self.near.at[rows], self.far.at[rows])
        copy = pltpu.make_async_copy(near, far, self.sems.at[self.next])
        self.next += 1
        copy.start()
        self.pending.append(copy)

    def wait(self):
        for copy in self.pending:
            copy.wait()
        self.pending = []
        return self.near


def staged_call(body, scalars, big_ins, small_ins, outs, small_outs=(), scratch=(), after=(), micros=10.0):
    def shape_of(a, part):
        if part is None:
            return a.shape
        return a.shape[1:] if part == "core" else (part.stop - part.start,) + a.shape[1:]

    def kernel(*refs):
        refs = list(refs)
        take = lambda n: [refs.pop(0) for _ in range(n)]
        (scalar_ref,) = take(1)
        far_in, smalls, _, far_out = take(len(big_ins)), take(len(small_ins)), take(len(after)), take(len(outs))
        short_out, buf_in, buf_out = take(len(small_outs)), take(len(big_ins)), take(len(outs))
        sem_in, sem_out = take(2)
        me = [scalar_ref[i] for i in range(scalars.shape[0])]
        ins = [
            Staged(far, near, sem_in, i, me[0] if part == "core" else part)
            for i, (far, near, (_, part)) in enumerate(zip(far_in, buf_in, big_ins))
        ]
        for one in ins:
            one.load()
        first = 0
        results = []
        for far, near, (_, _, n) in zip(far_out, buf_out, outs):
            results.append(Staged(far, near, sem_out, first))
            first += n
        body(me if len(me) > 1 else me[0], ins, smalls, results, short_out, refs)
        for one in ins + results:
            one.wait()

    return pl.pallas_call(
        kernel,
        out_shape=[jax.ShapeDtypeStruct(s, d) for s, d, _ in outs] + [jax.ShapeDtypeStruct(s, d) for s, d in small_outs],
        in_specs=[SMEM] + [HBM] * len(big_ins) + [VMEM] * len(small_ins) + [ANY] * len(after),
        out_specs=[HBM] * len(outs) + [VMEM] * len(small_outs),
        scratch_shapes=[pltpu.VMEM(shape_of(a, part), a.dtype) for a, part in big_ins]
        + [pltpu.VMEM(s, d) for s, d, _ in outs]
        + [pltpu.SemaphoreType.DMA((len(big_ins),)), pltpu.SemaphoreType.DMA((max(1, sum(o[2] for o in outs)),))]
        + list(scratch),
        compiler_params=pltpu.CompilerParams(vmem_limit_bytes=VMEM_LIMIT),
        cost_estimate=pl.CostEstimate(flops=int(micros * 1.1e9), bytes_accessed=1024, transcendentals=0),
    )(scalars, *[a for a, _ in big_ins], *small_ins, *after)


def row_of(ref):
    return ref[...].astype(f32).reshape(1, ref.shape[0])


S_GAIN, S_SHIFT, S_SELF_OB, S_CROSS_OB, S_FFN_OB, S_SELF_B, S_CROSS_B, S_FFN_B, S_SLOT_B = 0, 3, 6, 7, 8, 9, 10, 11, 13


def own_first(row, core):
    half = row.shape[1] // 2
    return jnp.where(core == 0, row, jnp.concatenate([row[:, half:], row[:, :half]], axis=1))


def attend_forward(cross, core, ins, smalls, outs, _, scratch):
    qa_s, ka_s, va_s, ctx_s, y_s, h_s = outs
    qa, ka, va, ctx, y_out, h_out = [o.near for o in outs]
    if cross:
        src_s, k_m, k_t, w_m, w_t, wo_m, wo_t = ins
        bias_m, bias_t, out_bias, gains, shifts, seg_d, seg_e = smalls
    else:
        k_m, k_t, w_m, w_t, wo_m, wo_t = ins
        bias_m, bias_t, out_bias, gains, shifts, seg_d = smalls
        seg_e = seg_d
    heads, _, length = qa.shape
    half = length // 2
    hw = w_m.near.shape[2]
    heads_half = heads // 2
    seg_q = own_first(seg_d[pl.ds(core, 1), :], core)
    seg_k = own_first(seg_e[pl.ds(core, 1), :], core)
    shape16 = (16, length)
    index = lax.broadcasted_iota(jnp.int32, shape16, 0)
    same_q = index == jnp.broadcast_to(seg_q, shape16)
    same_k = index == jnp.broadcast_to(seg_k, shape16)
    q_extra = jnp.where(index < 4, jnp.where(same_q, 0.0, MASKED), 0.0).astype(bf16)
    k_extra = jnp.where(index < 4, jnp.where(same_k, 1.0, 0.0), jnp.where(index < 7, 1.0, 0.0)).astype(bf16)
    v_extra = jnp.where(index < 3, 1.0, 0.0).astype(bf16)
    for h in range(heads):
        qa[h, 64:80, :] = q_extra
        ka[h, 64:80, :] = k_extra
        va[h, 64:80, :] = v_extra
    src_k = [k_m.wait(), k_t.wait()]
    if cross:
        src = src_s.wait()
        src_q = [src.at[0:half], src.at[half:length]]
    else:
        src_q = src_k
    for side, (w_s, short) in enumerate(((w_m, bias_m), (w_t, bias_t))):
        w = w_s.wait()
        bias_q = column_of(short[0:1, :])
        bias_v = column_of(short[1:2, :])
        for piece in range(2):
            at = slice(piece * half, (piece + 1) * half)
            q = ((dg(w[0], src_q[piece][...], 0, 1) + bias_q) * (SCALE * LOG2E)).astype(bf16)
            k = dg(w[1], src_k[piece][...], 0, 1).astype(bf16)
            v = (dg(w[2], src_k[piece][...], 0, 1) + bias_v).astype(bf16)
            for i in range(heads_half):
                h = side * heads_half + i
                rows = slice(i * HEAD_DIM, (i + 1) * HEAD_DIM)
                qa[h, 0:64, at] = q[rows]
                ka[h, 0:64, at] = k[rows]
                va[h, 0:64, at] = v[rows]
    ka_s.store()
    va_s.store()

    def some_heads(step, _):
        items = [(step * FWD_HEADS + j, slice(i, i + FWD_QB)) for j in range(FWD_HEADS) for i in range(0, length, FWD_QB)]

        def scores_of(item):
            h, at = item
            return dg(ka[h], qa[h, :, at], 0, 0)

        scores = scores_of(items[0])
        for n, (h, at) in enumerate(items):
            following = scores_of(items[n + 1]) if n + 1 < len(items) else None
            top = jnp.max(scores, axis=0, keepdims=True)
            weights = jnp.exp2(scores - top).astype(bf16)
            out = dg(va[h], weights, 1, 0)
            total = out[64:65, :]
            ctx[pl.ds(pl.multiple_of(h * HEAD_DIM, HEAD_DIM), HEAD_DIM), at] = (out[0:64, :] * (1.0 / total)).astype(bf16)
            high, middle, low = three_parts(-(top + jnp.log2(total)))
            extra = tall((16, FWD_QB), {4: high, 5: middle, 6: low})
            qa[h, 64:80, at] = qa[h, 64:80, at] + extra.astype(bf16)
            scores = following
        return 0

    lax.fori_loop(0, heads // FWD_HEADS, some_heads, 0)
    qa_s.store()
    ctx_s.store()
    norm = 1 if cross else 0
    bias = row_of(out_bias)
    gain = gains[norm : norm + 1, :].astype(f32)
    shift = shifts[norm : norm + 1, :].astype(f32)
    wo = [wo_m.wait(), wo_t.wait()]
    for i in range(length // TB):
        at = slice(i * TB, (i + 1) * TB)
        y = dg(ctx[0:hw, at], wo[0][...], 0, 0) + dg(ctx[hw:, at], wo[1][...], 0, 0) + bias
        piece, inner = divmod(i * TB, half)
        y = y + src_q[piece][inner : inner + TB, :].astype(f32)
        y_out[at, :] = y
        y_s.store(at)
        xhat, _ = norm_parts(y)
        h_out[at, :] = (xhat * gain + shift).astype(bf16)
        h_s.store(at)


def back_heads(count, qa, ka, va, da, ctx, dq, dk, dv):
    length = qa.shape[2]

    def one_head(h, _):
        rows = pl.ds(pl.multiple_of(h * HEAD_DIM, HEAD_DIM), HEAD_DIM)
        keys = ka[h]
        values = va[h]
        inner = jnp.sum(da[h, 0:64, :].astype(f32) * ctx[rows, :].astype(f32), axis=0, keepdims=True)
        high, middle, low = three_parts(-inner)
        da[h, 64:80, :] = tall((16, length), {0: high, 1: middle, 2: low}).astype(bf16)
        cuts = [slice(i * QB, (i + 1) * QB) for i in range(length // QB)]

        def products(at):
            return dg(qa[h, :, at], keys, 0, 0), dg(da[h, :, at], values, 0, 0)

        ahead = products(cuts[0])
        for n, at in enumerate(cuts):
            scores, spread = ahead
            if n + 1 < len(cuts):
                ahead = products(cuts[n + 1])
            weights = jnp.exp2(scores)
            ds = (weights * spread).astype(bf16)
            dv_part = dg(da[h, 0:64, at], weights.astype(bf16), 1, 0)
            dk_part = dg(qa[h, 0:64, at], ds, 1, 0)
            dv_sum = dv_part if n == 0 else dv_sum + dv_part
            dk_sum = dk_part if n == 0 else dk_sum + dk_part
            dq[rows, at] = (dg(keys[0:64], ds, 1, 1) * SCALE).astype(bf16)
        dk[rows, :] = (dk_sum * LN2).astype(bf16)
        dv[rows, :] = dv_sum.astype(bf16)
        return 0

    lax.fori_loop(0, count, one_head, 0)


def weight_rows(g, grads, sources):
    for j, (grad, pair) in enumerate(zip(grads, sources)):
        hw, length = grad.shape
        half = length // 2
        total = dg(pair[0][...], grad[:, 0:half], 0, 1) + dg(pair[1][...], grad[:, half:length], 0, 1)
        put = slice(j * hw, (j + 1) * hw)
        inner = total.shape[0] // 2
        g.near[put, 0:hw] = total[0:inner].astype(bf16)
        g.near[put, hw : 2 * hw] = total[inner:].astype(bf16)
        g.store(put)


def position_sums(dq, dv):
    ones = jnp.ones((8, dq.shape[1]), bf16)
    return dg(ones, dq[...], 1, 1)[0:1], dg(ones, dv[...], 1, 1)[0:1]


def cross_backward(core, ins, smalls, outs, _, scratch):
    dy_s, wo_m, wo_t, ctx_s, va_s, qa_s, ka_s, src_s, k_m, k_t, w_m, w_t, y_s, ctx1_s = ins
    gains, short_m, short_t = smalls
    g_m, g_t, dk_s, dv_s, dprev_s, do_s, ns_m, ns_t = outs
    da, dq = scratch
    dk, dv = dk_s.near, dv_s.near
    length, width = dy_s.near.shape
    half = length // 2
    hw = wo_m.near.shape[0]
    each = hw // HEAD_DIM
    dout = dy_s.wait()[...].astype(bf16)
    ctx = ctx_s.near
    for side, wo in enumerate((wo_m, wo_t)):
        dctx = dg(wo.wait()[...], dout, 1, 1).astype(bf16)
        for i in range(each):
            da[side * each + i, 0:64, :] = dctx[i * HEAD_DIM : (i + 1) * HEAD_DIM]
    ctx_s.wait()
    for side, g in enumerate((g_m, g_t)):
        rows = slice(3 * hw, 4 * hw)
        g.near[rows, :] = dg(ctx[side * hw : (side + 1) * hw, :], dout, 1, 0).astype(bf16)
        g.store(rows)
    va, qa, ka = va_s.wait(), qa_s.wait(), ka_s.wait()
    back_heads(2 * each, qa, ka, va, da, ctx, dq, dk, dv)
    dk_s.store()
    dv_s.store()
    src = src_s.wait()
    src_q = [src.at[0:half], src.at[half:length]]
    src_k = [k_m.wait(), k_t.wait()]
    w = [w_m.wait(), w_t.wait()]
    y_prev = y_s.wait()
    dy = dy_s.near
    dprev = dprev_s.near
    dout1 = do_s.near
    gain = gains[0:1, :].astype(f32)
    gain_sum = jnp.zeros((1, width), f32)
    shift_sum = jnp.zeros((1, width), f32)
    out_sum = jnp.zeros((1, width), f32)
    for i in range(length // TB):
        at = slice(i * TB, (i + 1) * TB)
        e = dy[at, :] + dg(dq[0:hw, at], w[0][0], 0, 1) + dg(dq[hw:, at], w[1][0], 0, 1)
        xhat, spread = norm_parts(y_prev[at, :])
        back, d_gain, d_shift = norm_back(xhat, spread, gain, e)
        dprev[at, :] = back
        dprev_s.store(at)
        rounded = back.astype(bf16)
        dout1[at, :] = rounded
        gain_sum += d_gain
        shift_sum += d_shift
        out_sum += jnp.sum(rounded.astype(f32), axis=0, keepdims=True)
    do_s.store()
    ctx1 = ctx1_s.wait()
    q_sum, v_sum = position_sums(dq, dv)
    for side, g, short, ns in ((1, g_t, short_t, ns_t), (0, g_m, short_m, ns_m)):
        rows = slice(side * hw, (side + 1) * hw)
        weight_rows(g, [dq.at[rows], dk.at[rows], dv.at[rows]], [src_q, src_k, src_k])
        put = slice(4 * hw, 5 * hw)
        g.near[put, :] = dg(ctx1[rows, :], dout1[...], 1, 0).astype(bf16)
        g.store(put)
        own = jnp.concatenate([q_sum[:, rows], v_sum[:, rows]], axis=1)
        ns.near[...] = short[...]
        ns.near[S_GAIN : S_GAIN + 1, :] = gain_sum
        ns.near[S_SHIFT : S_SHIFT + 1, :] = shift_sum
        ns.near[S_SELF_OB : S_SELF_OB + 1, :] = out_sum
        ns.near[S_CROSS_B : S_CROSS_B + 1, :] = own
        ns.store()


def self_backward(sides, core, ins, smalls, outs, _, scratch):
    do_s, x_m, x_t = ins[0:3]
    dout = do_s.wait()
    for n in range(sides):
        wo, da = ins[3 + 5 * n], scratch[n]
        dctx = dg(wo.wait()[...], dout[...], 1, 1).astype(bf16)
        for i in range(da.shape[0]):
            da[i, 0:64, :] = dctx[i * HEAD_DIM : (i + 1) * HEAD_DIM]
    for n in range(sides):
        ctx, va, qa, ka = [one.wait() for one in ins[4 + 5 * n : 8 + 5 * n]]
        g = outs[4 * n]
        grads = [one.near for one in outs[4 * n + 1 : 4 * n + 4]]
        back_heads(qa.shape[0], qa, ka, va, scratch[n], ctx, *grads)
        for one in outs[4 * n + 1 : 4 * n + 4]:
            one.store()
        src = [x_m.wait(), x_t.wait()]
        weight_rows(g, grads, [src] * 3)
        short = smalls[n]
        q_sum, v_sum = position_sums(grads[0], grads[2])
        own = jnp.concatenate([q_sum, v_sum], axis=1)
        index = lax.broadcasted_iota(jnp.int32, short.shape, 0)
        rows = jnp.where(index == S_SELF_B, jnp.broadcast_to(own, short.shape), short[...])
        start = 3 * grads[0].shape[0]
        stop, end = start + short.shape[0], g.near.shape[0]
        g.near[start:stop, :] = rows.astype(bf16)
        if stop < end:
            g.near[stop:end, :] = jnp.zeros((end - stop, g.near.shape[1]), bf16)
        g.store(slice(start, end))


def memory_gradient(core, ins, smalls, outs, _, scratch):
    dk_s, dv_s, w_m, w_t = ins
    out_m, out_t = outs
    dk, dv, w0, w1 = dk_s.wait(), dv_s.wait(), w_m.wait(), w_t.wait()
    hw = w0.shape[2]
    half = out_m.near.shape[0]
    for piece, out in ((1, out_t), (0, out_m)):
        at = slice(piece * half, (piece + 1) * half)
        total = dg(dk[0:hw, at], w0[1], 0, 1) + dg(dk[hw:, at], w1[1], 0, 1)
        total = total + dg(dv[0:hw, at], w0[2], 0, 1) + dg(dv[hw:, at], w1[2], 0, 1)
        out.near[...] = total.astype(bf16)
        out.store()


def input_gradient(core, ins, smalls, outs, _, scratch):
    dy_s = ins[-1]
    out_m, out_t = outs
    sides = [[one.wait() for one in ins[0:4]], [one.wait() for one in ins[4:8]]]
    dy = dy_s.wait()
    half = out_m.near.shape[0]
    for piece, out in ((1, out_t), (0, out_m)):
        at = slice(piece * half, (piece + 1) * half)
        total = dy[at, :]
        for grads in sides:
            for j in range(3):
                total = total + dg(grads[j][:, at], grads[3][j], 0, 1)
        out.near[...] = total.astype(bf16)
        out.store()


def place_of(slot, core, length):
    place = slot[pl.ds(core, 1), :]
    half = length // 2
    return jnp.where(core == 0, place, jnp.where(place >= half, place - half, place + half))


def slot_matrix(slot, core, length):
    row = place_of(slot, core, length)
    shape = (length, row.shape[1])
    return jnp.where(lax.broadcasted_iota(jnp.int32, shape, 0) == jnp.broadcast_to(row, shape), 1.0, 0.0).astype(bf16)


def feed_forward(core, ins, smalls, outs, _, scratch):
    gs_m, gs_t, ws_m, ws_t, go_m, go_t, h2_s, wi_m, wi_t, wo_m, wo_t, y2_s = ins
    bi_m, bi_t, ob, gains, shifts, slot = smalls
    out_m, out_t, dy2_s, g_m, g_t, small_m, small_t = outs
    onehot, tl, tr, e3, hid, dpre, slope, df_all, states = scratch
    length, width = h2_s.near.shape
    half = length // 2
    fw = wi_m.near.shape[1]
    sw = ws_m.near.shape[1]
    onehot[...] = slot_matrix(slot, core, length)
    for side, (gs, ws) in enumerate(((gs_m, ws_m), (gs_t, ws_t))):
        cols = slice(side * sw, (side + 1) * sw)
        left = dg(onehot[...], gs.wait()[...], 1, 0)
        tl[:, cols] = left.astype(bf16)
        tr[:, cols] = pltpu.roll(left, 1, 0).astype(bf16)
    ws = [ws_m.wait(), ws_t.wait()]
    go = [go_m.wait(), go_t.wait()]
    for i in range(length // TB):
        at = slice(i * TB, (i + 1) * TB)
        piece, inner = divmod(i * TB, half)
        total = go[piece][inner : inner + TB, :].astype(f32)
        for side in range(2):
            cols = slice(side * sw, (side + 1) * sw)
            total = total + dg(tl[at, cols], ws[side][0:width, :], 1, 1) + dg(tr[at, cols], ws[side][width : 2 * width, :], 1, 1)
        e3[at, :] = total
    h2, y2 = h2_s.wait(), y2_s.wait()
    wi = [wi_m.wait(), wi_t.wait()]
    wo = [wo_m.wait(), wo_t.wait()]
    dy2 = dy2_s.near
    bias_in = [row_of(bi_m), row_of(bi_t)]
    bias_out = row_of(ob)
    gain2 = gains[1:2, :].astype(f32)
    gain3 = gains[2:3, :].astype(f32)
    shift3 = shifts[2:3, :].astype(f32)

    def one_block(i, sums):
        gain3_sum, shift3_sum, gain2_sum, shift2_sum, ffn_out_sum, cross_out_sum, in_m_sum, in_t_sum = sums
        at = pl.ds(pl.multiple_of(i * TB, TB), TB)
        hb = h2[at, :]
        y3 = hb.astype(f32) + bias_out
        for side in range(2):
            cols = slice(side * fw, (side + 1) * fw)
            pre = dg(hb, wi[side][...], 1, 0) + bias_in[side]
            square = pre * pre
            tanh = jnp.tanh(pre * (GELU_C + GELU_C * GELU_A * square))
            gate = 0.5 + 0.5 * tanh
            hidden = (pre * gate).astype(bf16)
            hid[at, cols] = hidden
            slope[:, cols] = gate + (0.5 * pre) * (1.0 - tanh * tanh) * (GELU_C + 3.0 * GELU_C * GELU_A * square)
            y3 = y3 + dg(hidden, wo[side][...], 1, 0)
        xhat, spread = norm_parts(y3)
        states[at, :] = (xhat * gain3 + shift3).astype(bf16)
        dy3, d_gain, d_shift = norm_back(xhat, spread, gain3, e3[at, :])
        gain3_sum += d_gain
        shift3_sum += d_shift
        df = dy3.astype(bf16)
        df_all[at, :] = df
        ffn_out_sum += jnp.sum(df.astype(f32), axis=0, keepdims=True)
        e2 = dy3
        in_sums = []
        for side, in_sum in enumerate((in_m_sum, in_t_sum)):
            cols = slice(side * fw, (side + 1) * fw)
            back = (dg(df, wo[side][...], 1, 1) * slope[:, cols]).astype(bf16)
            dpre[at, cols] = back
            in_sums.append(in_sum + jnp.sum(back.astype(f32), axis=0, keepdims=True))
            e2 = e2 + dg(back, wi[side][...], 1, 1)
        xhat, spread = norm_parts(y2[at, :])
        back2, d_gain, d_shift = norm_back(xhat, spread, gain2, e2)
        dy2[at, :] = back2
        gain2_sum += d_gain
        shift2_sum += d_shift
        cross_out_sum += jnp.sum(back2.astype(bf16).astype(f32), axis=0, keepdims=True)
        return gain3_sum, shift3_sum, gain2_sum, shift2_sum, ffn_out_sum, cross_out_sum, in_sums[0], in_sums[1]

    row = jnp.zeros((1, width), f32)
    wide = jnp.zeros((1, fw), f32)
    sums = lax.fori_loop(0, length // TB, one_block, (row, row, row, row, row, row, wide, wide))
    dy2_s.store()
    for piece, out in ((1, out_t), (0, out_m)):
        out.near[...] = states[piece * half : (piece + 1) * half, :]
        out.store()
    for side, g in ((1, g_t), (0, g_m)):
        for i in range(fw // width):
            block = slice(side * fw + i * width, side * fw + (i + 1) * width)
            rows = slice(width + i * width, 2 * width + i * width)
            g.near[rows, :] = dg(h2[...], dpre[:, block], 0, 0).astype(bf16)
            g.store(rows)
            rows = slice(width + fw + i * width, 2 * width + fw + i * width)
            g.near[rows, :] = dg(hid[:, block], df_all[...], 0, 0).astype(bf16)
            g.store(rows)
        cols = slice(side * sw, (side + 1) * sw)
        rows = slice(0, width)
        g.near[rows, 0:sw] = dg(states[...], tl[:, cols], 0, 0).astype(bf16)
        g.near[rows, sw : 2 * sw] = dg(states[...], tr[:, cols], 0, 0).astype(bf16)
        g.store(rows)
    for short, total, gs in ((small_m, sums[6], gs_m), (small_t, sums[7], gs_t)):
        short.near[...] = jnp.zeros(short.near.shape, f32)
        for at, one in ((S_GAIN + 2, 0), (S_SHIFT + 2, 1), (S_GAIN + 1, 2), (S_SHIFT + 1, 3), (S_FFN_OB, 4), (S_CROSS_OB, 5)):
            short.near[at : at + 1, :] = sums[one]
        for i in range(fw // width):
            short.near[S_FFN_B + i : S_FFN_B + i + 1, :] = total[:, i * width : (i + 1) * width]
        short.near[S_SLOT_B : S_SLOT_B + 1, 0:sw] = jnp.sum(gs.near[...].astype(f32), axis=0, keepdims=True)
        short.store()


def slot_forward(core, ins, smalls, outs, _, scratch):
    out_m, out_t, ws_m, ws_t = ins
    bs_m, bs_t, slot = smalls
    onehot, states = scratch
    length, width = states.shape
    half = length // 2
    onehot[...] = slot_matrix(slot, core, length)
    states[0:half, :] = out_m.wait()[...]
    states[half:length, :] = out_t.wait()[...]
    for ws_s, short, out in ((ws_t, bs_t, outs[1]), (ws_m, bs_m, outs[0])):
        ws = ws_s.wait()
        top = dg(states[...], ws[0:width, :], 1, 0)
        low = dg(states[...], ws[width : 2 * width, :], 1, 0)
        total = (top + pltpu.roll(low, length - 1, 0) + row_of(short)).astype(bf16)
        out.near[...] = dg(onehot[...], total, 0, 0).astype(bf16)
        out.store()


def joined(scalars, ins):
    bit = scalars[1]
    own, got = ins[0].wait(), ins[1].wait()
    return jnp.where(bit == 0, own[...], got[...]), jnp.where(bit == 0, got[...], own[...])


def put_qkv(out, buf, hw):
    for j in range(3):
        out.near[j, 0:hw, :] = buf[j * hw : (j + 1) * hw, 0:hw].astype(f32)
        out.near[j, hw : 2 * hw, :] = buf[j * hw : (j + 1) * hw, hw : 2 * hw].astype(f32)
    out.store()


def unpack_cross(scalars, ins, smalls, outs, _, scratch):
    (buf,) = scratch
    count = buf.shape[0] // 2
    buf[0:count, :], buf[count:, :] = joined(scalars, ins)
    qkv, cross_out, self_out = outs
    hw = cross_out.near.shape[0]
    put_qkv(qkv, buf, hw)
    cross_out.near[...] = buf[3 * hw : 4 * hw, :].astype(f32)
    cross_out.store()
    self_out.near[...] = buf[4 * hw : 5 * hw, :].astype(f32)
    self_out.store()


def unpack_self(scalars, ins, smalls, outs, small_outs, scratch):
    (buf,) = scratch
    count = buf.shape[0] // 2
    buf[0:count, :], buf[count:, :] = joined(scalars, ins)
    (qkv,) = outs
    hw = qkv.near.shape[2]
    put_qkv(qkv, buf, hw)
    self_b, self_ob, cross_b, cross_ob, ffn_b, ffn_ob, gains, shifts, slot_b = small_outs
    short = buf[3 * hw : 3 * hw + 16, :].astype(f32)
    width = short.shape[1]
    for ref, at in ((self_b, S_SELF_B), (cross_b, S_CROSS_B)):
        ref[0:1, :] = short[at : at + 1, 0:hw]
        ref[1:2, :] = short[at : at + 1, hw : 2 * hw]
    for ref, at in ((self_ob, S_SELF_OB), (cross_ob, S_CROSS_OB), (ffn_ob, S_FFN_OB)):
        ref[...] = short[at : at + 1, :].reshape(width)
    wide = ffn_b.shape[0] // width
    ffn_b[...] = jnp.concatenate([short[S_FFN_B + i : S_FFN_B + i + 1, :] for i in range(wide)], axis=1).reshape(wide * width)
    gains[...] = short[S_GAIN : S_GAIN + 3, :]
    shifts[...] = short[S_SHIFT : S_SHIFT + 3, :]
    slot_b[...] = short[S_SLOT_B : S_SLOT_B + 1, 0 : slot_b.shape[0]].reshape(slot_b.shape[0])


def unpack_ffn(core, ins, smalls, outs, _, scratch):
    slot, into, back = ins
    slot_w, ffn_in, ffn_out = outs
    buf = slot.wait()
    width = buf.shape[0]
    sw = slot_w.near.shape[1]
    slot_w.near[0:width, :] = buf[:, 0:sw].astype(f32)
    slot_w.near[width:, :] = buf[:, sw : 2 * sw].astype(f32)
    slot_w.store()
    buf = into.wait()
    for i in range(ffn_in.near.shape[1] // width):
        ffn_in.near[:, i * width : (i + 1) * width] = buf[i * width : (i + 1) * width, :].astype(f32)
    ffn_in.store()
    ffn_out.near[...] = back.wait()[...].astype(f32)
    ffn_out.store()


def swap(x):
    return lax.ppermute(x, "tensor", [(0, 1), (1, 0)])


def pair_add(core, ins, smalls, outs, _, scratch):
    (out,) = outs
    count = len(ins) // 2
    for i in range(count):
        kept, got = ins[i].wait(), ins[count + i].wait()
        rows = slice(i * kept.shape[0], (i + 1) * kept.shape[0])
        out.near[rows, :] = (kept[...].astype(f32) + got[...].astype(f32)).astype(bf16)
        out.store(rows)


def pair_sum(core, kept, got, after):
    cuts = [slice(i, i + PAIR_ROWS) for i in range(0, kept.shape[0], PAIR_ROWS)]
    return staged_call(pair_add, core, [(kept, cut) for cut in cuts] + [(got, cut) for cut in cuts], [],
                       [(kept.shape, bf16, len(cuts))], after=after, micros=3)[0]


class RowSum:
    def __init__(self, x, dp_size, dp_index, core):
        bits = dp_size.bit_length() - 1
        orders = [list(range(bits)), list(range(bits))]
        if bits > 2:
            orders[1] = [1, 2, 0] + list(range(3, bits))
        self.plan = []
        for step in range(bits):
            pairs = []
            for device in range(dp_size):
                for c in range(2):
                    pairs.append((device * 2 + c, (device ^ (1 << orders[c][step])) * 2 + c))
            bit = jnp.where(core == 0, (dp_index >> orders[0][step]) & 1, (dp_index >> orders[1][step]) & 1)
            self.plan.append((pairs, bit))
        self.x = x
        self.step = 0
        self.cut()

    def cut(self):
        if self.step == len(self.plan):
            self.x = self.x.astype(bf16)
            self.away = self.x
            return
        bit = self.plan[self.step][1]
        count = self.x.shape[0] // 2
        self.away = lax.dynamic_slice_in_dim(self.x, (1 - bit) * count, count, 0).astype(bf16)
        self.kept = lax.dynamic_slice_in_dim(self.x, bit * count, count, 0)

    def scatter(self):
        got = lax.ppermute(self.away, ("dp", "tensor"), self.plan[self.step][0])
        self.x = self.kept.astype(f32) + got.astype(f32)
        self.step += 1
        self.cut()

    def gather(self):
        x = self.x
        for step in reversed(range(len(self.plan))):
            pairs, bit = self.plan[step]
            got = lax.ppermute(x, ("dp", "tensor"), pairs)
            if step == 0:
                return x, got, bit
            first = lax.broadcasted_iota(jnp.int32, (2,) + x.shape, 0) == bit
            x = jnp.where(first, x[None], got[None]).reshape((2 * x.shape[0],) + x.shape[1:])


def shards(dp_size, *args):
    (tokens, memory, dec_segment, enc_segment, slot_left, self_qkv, self_bias, self_out, self_out_bias,
     cross_qkv, cross_bias, cross_out, cross_out_bias, ffn_in, ffn_in_bias, ffn_out, ffn_out_bias,
     norm_gain, norm_bias, slot_weight, slot_bias, grad_output, grad_slots) = args
    core_index = lax.axis_index("tensor")
    dp_index = lax.axis_index("dp")
    core = core_index.astype(jnp.int32).reshape(1)
    half, width = tokens.shape[1], tokens.shape[2]
    length = 2 * half
    hw = self_qkv.shape[2]
    heads = 2 * hw // HEAD_DIM
    fw = ffn_in.shape[1]
    wide = fw // width
    sw = slot_weight.shape[1]
    slots = slot_left.shape[1]

    tokens_t = swap(tokens)
    self_qkv_t = swap(self_qkv)
    self_bias_t = swap(self_bias)
    self_out_t = swap(self_out)
    memory_t = swap(memory)
    cross_qkv_t = swap(cross_qkv)
    cross_bias_t = swap(cross_bias)
    cross_out_t = swap(cross_out)
    grad_slots_t = swap(grad_slots)
    slot_weight_t = swap(slot_weight)
    grad_output_t = swap(grad_output)
    ffn_in_t = swap(ffn_in)
    ffn_in_bias_t = swap(ffn_in_bias)
    ffn_out_t = swap(ffn_out)
    slot_bias_t = swap(slot_bias)

    aug = (heads, AUG, length)
    blocks = length // TB
    forward_outs = [(aug, bf16, 1), (aug, bf16, 1), (aug, bf16, 1), ((2 * hw, length), bf16, 1),
                    ((length, width), f32, blocks), ((length, width), bf16, blocks)]
    qa, ka, va, ctx, y1, h1 = staged_call(
        functools.partial(attend_forward, False), core,
        [(tokens, "core"), (tokens_t, "core"), (self_qkv, None), (self_qkv_t, None), (self_out, None), (self_out_t, None)],
        [self_bias, self_bias_t, self_out_bias, norm_gain, norm_bias, dec_segment], forward_outs, micros=18)
    qa2, ka2, va2, ctx2, y2, h2 = staged_call(
        functools.partial(attend_forward, True), core,
        [(h1, None), (memory, "core"), (memory_t, "core"), (cross_qkv, None), (cross_qkv_t, None), (cross_out, None),
         (cross_out_t, None)],
        [cross_bias, cross_bias_t, cross_out_bias, norm_gain, norm_bias, dec_segment, enc_segment], forward_outs, micros=18)
    g1_rows = width + 2 * fw
    half_out = ((half, width), bf16, 1)
    out_m, out_t, dy2, g1_m, g1_t, short1_m, short1_t = staged_call(
        feed_forward, core,
        [(grad_slots, "core"), (grad_slots_t, "core"), (slot_weight, None), (slot_weight_t, None), (grad_output, "core"),
         (grad_output_t, "core"), (h2, None), (ffn_in, None), (ffn_in_t, None), (ffn_out, None), (ffn_out_t, None),
         (y2, None)],
        [ffn_in_bias, ffn_in_bias_t, ffn_out_bias, norm_gain, norm_bias, slot_left],
        [half_out, half_out, ((length, width), f32, 1), ((g1_rows, width), bf16, 1 + 2 * wide),
         ((g1_rows, width), bf16, 1 + 2 * wide), ((16, width), f32, 1), ((16, width), f32, 1)],
        scratch=[pltpu.VMEM((length, slots), bf16), pltpu.VMEM((length, 2 * sw), bf16), pltpu.VMEM((length, 2 * sw), bf16),
                 pltpu.VMEM((length, width), f32), pltpu.VMEM((length, 2 * fw), bf16), pltpu.VMEM((length, 2 * fw), bf16),
                 pltpu.VMEM((TB, 2 * fw), f32), pltpu.VMEM((length, width), bf16), pltpu.VMEM((length, width), bf16)],
        after=[slot_bias_t], micros=25)
    st_m, st_t = staged_call(
        slot_forward, core, [(out_m, None), (out_t, None), (slot_weight, None), (slot_weight_t, None)],
        [slot_bias, slot_bias_t, slot_left], [((slots, sw), bf16, 1), ((slots, sw), bf16, 1)],
        scratch=[pltpu.VMEM((length, slots), bf16), pltpu.VMEM((length, width), bf16)], micros=4)
    g1 = pair_sum(core, g1_m, swap(g1_t), [st_m])
    g1_sum = lax.psum(g1, "dp")
    def attention_part():
        g2_m, g2_t, dk2, dv2, dy1, do1, short2_m, short2_t = staged_call(
            cross_backward, core,
            [(dy2, None), (cross_out, None), (cross_out_t, None), (ctx2, None), (va2, None), (qa2, None), (ka2, None),
             (h1, None), (memory, "core"), (memory_t, "core"), (cross_qkv, None), (cross_qkv_t, None), (y1, None), (ctx, None)],
            [norm_gain, short1_m, short1_t],
            [((5 * hw, width), bf16, 5), ((5 * hw, width), bf16, 5), ((2 * hw, length), bf16, 1), ((2 * hw, length), bf16, 1),
             ((length, width), f32, blocks), ((length, width), bf16, 1), ((16, width), f32, 1), ((16, width), f32, 1)],
            scratch=[pltpu.VMEM(aug, bf16), pltpu.VMEM((2 * hw, length), bf16)], after=[g1], micros=30)
        dmem_m, dmem_t = staged_call(
            memory_gradient, core, [(dk2, None), (dv2, None), (cross_qkv, None), (cross_qkv_t, None)], [],
            [half_out, half_out], micros=4)

        def packed(total):
            return total.reshape(dp_size, total.shape[0] // dp_size, width)

        sum2 = RowSum(packed(g2_m.astype(f32) + swap(g2_t).astype(f32)), dp_size, dp_index, core_index)
        g3_rows = 3 * hw + 16 + (-(3 * hw + 16)) % 128
        g3_rows += -g3_rows % dp_size
        count = heads // 2
        side_outs = [((g3_rows, width), bf16, 4)] + [((hw, length), bf16, 1)] * 3
        sides = {}
        held = [dmem_m]
        for group in SELF_GROUPS:
            inputs, shorts = [], []
            for side in group:
                of = slice(side * count, (side + 1) * count)
                inputs += [((self_out, self_out_t)[side], None), (ctx, slice(side * hw, (side + 1) * hw)), (va, of), (qa, of), (ka, of)]
                shorts.append((short2_m, short2_t)[side])
            found = staged_call(
                functools.partial(self_backward, len(group)), core,
                [(do1, None), (tokens, "core"), (tokens_t, "core")] + inputs, shorts, side_outs * len(group),
                scratch=[pltpu.VMEM((count, AUG, length), bf16)] * len(group), after=held + [sum2.away], micros=14 * len(group))
            sum2.scatter()
            held = []
            for n, side in enumerate(group):
                w = (self_qkv, self_qkv_t)[side]
                sides[side] = (found[4 * n], [(g, None) for g in found[4 * n + 1 : 4 * n + 4]] + [(w, None)])
        while sum2.step < len(sum2.plan):
            sum2.scatter()
        sum3 = RowSum(packed(sides[0][0].astype(f32) + swap(sides[1][0]).astype(f32)), dp_size, dp_index, core_index)
        dx_m, dx_t = staged_call(input_gradient, core, sides[0][1] + sides[1][1] + [(dy1, None)], [], [half_out, half_out], micros=5)
        while sum3.step < len(sum3.plan):
            sum3.scatter()

        def together(kept, sent):
            got = swap(sent)
            return jnp.where(lax.broadcasted_iota(jnp.int32, (2,) + kept.shape, 0) == core_index, kept[None], got[None])

        output = together(out_m, out_t)
        slot_states = together(st_m, st_t)
        grad_memory = together(dmem_m, dmem_t)
        grad_input = together(dx_m, dx_t)

        def ends(total):
            own, got, bit = total.gather()
            flat = lambda x: x.reshape(-1, width)
            return jnp.stack([core_index, bit]).astype(jnp.int32), [(flat(own), None), (flat(got), None)]

        qkv_out = ((3, 2 * hw, hw), f32, 1)
        scalars, halves = ends(sum2)
        grad_cross_qkv, grad_cross_out, grad_self_out = staged_call(
            unpack_cross, scalars, halves, [], [qkv_out, ((hw, width), f32, 1), ((hw, width), f32, 1)],
            scratch=[pltpu.VMEM((5 * hw, width), bf16)], micros=3)
        scalars, halves = ends(sum3)
        (grad_self_qkv, grad_self_bias, grad_self_out_bias, grad_cross_bias, grad_cross_out_bias, grad_ffn_in_bias,
         grad_ffn_out_bias, grad_norm_gain, grad_norm_bias, grad_slot_bias) = staged_call(
            unpack_self, scalars, halves, [], [qkv_out],
            [((2, hw), f32), ((width,), f32), ((2, hw), f32), ((width,), f32), ((fw,), f32), ((width,), f32), ((3, width), f32),
             ((3, width), f32), ((sw,), f32)],
            scratch=[pltpu.VMEM((g3_rows, width), bf16)], micros=3)
        return (output, slot_states, grad_input, grad_memory, grad_self_qkv, grad_self_bias, grad_self_out, grad_self_out_bias,
                grad_cross_qkv, grad_cross_bias, grad_cross_out, grad_cross_out_bias, grad_ffn_in_bias, grad_ffn_out_bias,
                grad_norm_gain, grad_norm_bias, grad_slot_bias)

    shapes = jax.eval_shape(attention_part)
    nothing = lambda: tuple(jnp.zeros(one.shape, one.dtype) for one in shapes)
    (output, slot_states, grad_input, grad_memory, grad_self_qkv, grad_self_bias, grad_self_out, grad_self_out_bias,
     grad_cross_qkv, grad_cross_bias, grad_cross_out, grad_cross_out_bias, grad_ffn_in_bias, grad_ffn_out_bias,
     grad_norm_gain, grad_norm_bias, grad_slot_bias) = lax.cond(core_index < 2, attention_part, nothing)
    grad_slot_weight, grad_ffn_in, grad_ffn_out = staged_call(
        unpack_ffn, core, [(g1_sum, slice(0, width)), (g1_sum, slice(width, width + fw)), (g1_sum, slice(width + fw, g1_rows))],
        [], [((2 * width, sw), f32, 1), ((width, fw), f32, 1), ((fw, width), f32, 1)], micros=4)
    return (
        output, slot_states, grad_input, grad_memory, grad_self_qkv, grad_self_bias, grad_self_out, grad_self_out_bias,
        grad_cross_qkv, grad_cross_bias, grad_cross_out, grad_cross_out_bias, grad_ffn_in, grad_ffn_in_bias, grad_ffn_out,
        grad_ffn_out_bias, grad_norm_gain, grad_norm_bias, grad_slot_weight, grad_slot_bias,
    )


def solution(mesh):
    row3 = P("dp", "tensor", None)
    seg = P("dp", None)
    col3 = P(None, None, "tensor")
    col2 = P(None, "tensor")
    out2 = P("tensor", None)
    one = P("tensor")
    in_specs = (row3, row3, seg, seg, seg, col3, col2, out2, P(), col3, col2, out2, P(), col2, one, out2, P(), P(), P(),
                col2, one, row3, P("dp", None, "tensor"))
    out_specs = (row3, P("dp", None, "tensor"), row3, row3, col3, col2, out2, P(), col3, col2, out2, P(), col2, one, out2,
                 P(), P(), P(), col2, one)
    body = functools.partial(shards, mesh.shape["dp"])
    return jax.shard_map(body, mesh=mesh, in_specs=in_specs, out_specs=out_specs, check_vma=False)
```

```python
import functools

import jax
import jax.numpy as jnp
from jax import lax
from jax.experimental import pallas as pl
from jax.experimental.pallas import tpu as pltpu
from jax.sharding import PartitionSpec as P

HEAD_DIM = 64
EPSILON = 1e-05
MASKED = -1e30
GELU_C = 0.7978845608028654
GELU_A = 0.044715
LOG2E = 1.4426950408889634
LN2 = 0.6931471805599453
SCALE = HEAD_DIM ** (-0.5)
AUG = 80
QB = 256
FWD_QB = 1024
FWD_HEADS = 4
FFN_TB = 512
PAIR_ROWS = 512
SELF_GROUPS = ((1,), (0,))
TB = 256
VMEM_LIMIT = 63 * 2**20

bf16 = jnp.bfloat16
f32 = jnp.float32


def dg(a, b, ca, cb):
    return lax.dot_general(a, b, (((ca,), (cb,)), ((), ())), preferred_element_type=f32)


def column_of(row):
    return jnp.broadcast_to(row.astype(f32), (8, row.shape[1])).T[:, 0:1]


def three_parts(row):
    high = row.astype(bf16).astype(f32)
    rest = row - high
    middle = rest.astype(bf16).astype(f32)
    return high, middle, (rest - middle)


def tall(shape, rows):
    index = lax.broadcasted_iota(jnp.int32, shape, 0)
    block = jnp.zeros(shape, f32)
    for at, row in rows.items():
        block = jnp.where(index == at, jnp.broadcast_to(row, shape), block)
    return block


def norm_parts(y):
    centre = y - jnp.mean(y, axis=-1, keepdims=True)
    spread = lax.rsqrt(jnp.mean(centre * centre, axis=-1, keepdims=True) + EPSILON)
    return centre * spread, spread


def norm_back(xhat, spread, gain, e):
    a = e * gain
    dy = (a - jnp.mean(a, axis=-1, keepdims=True) - xhat * jnp.mean(a * xhat, axis=-1, keepdims=True)) * spread
    return dy, jnp.sum(e * xhat, axis=0, keepdims=True), jnp.sum(e, axis=0, keepdims=True)


ANY = pl.BlockSpec(memory_space=pl.ANY)
HBM = pl.BlockSpec(memory_space=pltpu.HBM)
VMEM = pl.BlockSpec(memory_space=pltpu.VMEM)
SMEM = pl.BlockSpec(memory_space=pltpu.SMEM)


class Staged:
    def __init__(self, far, near, sems, first, pick=None):
        self.far, self.near, self.sems, self.next, self.pending, self.pick = far, near, sems, first, [], pick

    def load(self):
        source = self.far if self.pick is None else self.far.at[self.pick]
        copy = pltpu.make_async_copy(source, self.near, self.sems.at[self.next])
        copy.start()
        self.pending.append(copy)

    def store(self, rows=None):
        near, far = (self.near, self.far) if rows is None else (self.near.at[rows], self.far.at[rows])
        copy = pltpu.make_async_copy(near, far, self.sems.at[self.next])
        self.next += 1
        copy.start()
        self.pending.append(copy)

    def wait(self):
        for copy in self.pending:
            copy.wait()
        self.pending = []
        return self.near


def staged_call(body, scalars, big_ins, small_ins, outs, small_outs=(), scratch=(), after=(), micros=10.0):
    def shape_of(a, part):
        if part is None:
            return a.shape
        return a.shape[1:] if part == "core" else (part.stop - part.start,) + a.shape[1:]

    def kernel(*refs):
        refs = list(refs)
        take = lambda n: [refs.pop(0) for _ in range(n)]
        (scalar_ref,) = take(1)
        far_in, smalls, _, far_out = take(len(big_ins)), take(len(small_ins)), take(len(after)), take(len(outs))
        short_out, buf_in, buf_out = take(len(small_outs)), take(len(big_ins)), take(len(outs))
        sem_in, sem_out = take(2)
        me = [scalar_ref[i] for i in range(scalars.shape[0])]
        ins = [
            Staged(far, near, sem_in, i, me[0] if part == "core" else part)
            for i, (far, near, (_, part)) in enumerate(zip(far_in, buf_in, big_ins))
        ]
        for one in ins:
            one.load()
        first = 0
        results = []
        for far, near, (_, _, n) in zip(far_out, buf_out, outs):
            results.append(Staged(far, near, sem_out, first))
            first += n
        body(me if len(me) > 1 else me[0], ins, smalls, results, short_out, refs)
        for one in ins + results:
            one.wait()

    return pl.pallas_call(
        kernel,
        out_shape=[jax.ShapeDtypeStruct(s, d) for s, d, _ in outs] + [jax.ShapeDtypeStruct(s, d) for s, d in small_outs],
        in_specs=[SMEM] + [HBM] * len(big_ins) + [VMEM] * len(small_ins) + [ANY] * len(after),
        out_specs=[HBM] * len(outs) + [VMEM] * len(small_outs),
        scratch_shapes=[pltpu.VMEM(shape_of(a, part), a.dtype) for a, part in big_ins]
        + [pltpu.VMEM(s, d) for s, d, _ in outs]
        + [pltpu.SemaphoreType.DMA((len(big_ins),)), pltpu.SemaphoreType.DMA((max(1, sum(o[2] for o in outs)),))]
        + list(scratch),
        compiler_params=pltpu.CompilerParams(vmem_limit_bytes=VMEM_LIMIT),
        cost_estimate=pl.CostEstimate(flops=int(micros * 1.1e9), bytes_accessed=1024, transcendentals=0),
    )(scalars, *[a for a, _ in big_ins], *small_ins, *after)


def row_of(ref):
    return ref[...].astype(f32).reshape(1, ref.shape[0])


S_GAIN, S_SHIFT, S_SELF_OB, S_CROSS_OB, S_FFN_OB, S_SELF_B, S_CROSS_B, S_FFN_B, S_SLOT_B = 0, 3, 6, 7, 8, 9, 10, 11, 13


def own_first(row, core):
    half = row.shape[1] // 2
    return jnp.where(core == 0, row, jnp.concatenate([row[:, half:], row[:, :half]], axis=1))


def attend_forward(cross, core, ins, smalls, outs, _, scratch):
    qa_s, ka_s, va_s, ctx_s, y_s, h_s = outs
    qa, ka, va, ctx, y_out, h_out = [o.near for o in outs]
    if cross:
        src_s, k_m, k_t, w_m, w_t, wo_m, wo_t = ins
        bias_m, bias_t, out_bias, gains, shifts, seg_d, seg_e = smalls
    else:
        k_m, k_t, w_m, w_t, wo_m, wo_t = ins
        bias_m, bias_t, out_bias, gains, shifts, seg_d = smalls
        seg_e = seg_d
    heads, _, length = qa.shape
    half = length // 2
    hw = w_m.near.shape[2]
    heads_half = heads // 2
    seg_q = own_first(seg_d[pl.ds(core, 1), :], core)
    seg_k = own_first(seg_e[pl.ds(core, 1), :], core)
    shape16 = (16, length)
    index = lax.broadcasted_iota(jnp.int32, shape16, 0)
    same_q = index == jnp.broadcast_to(seg_q, shape16)
    same_k = index == jnp.broadcast_to(seg_k, shape16)
    q_extra = jnp.where(index < 4, jnp.where(same_q, 0.0, MASKED), 0.0).astype(bf16)
    k_extra = jnp.where(index < 4, jnp.where(same_k, 1.0, 0.0), jnp.where(index < 7, 1.0, 0.0)).astype(bf16)
    v_extra = jnp.where(index < 3, 1.0, 0.0).astype(bf16)
    for h in range(heads):
        qa[h, 64:80, :] = q_extra
        ka[h, 64:80, :] = k_extra
        va[h, 64:80, :] = v_extra
    src_k = [k_m.wait(), k_t.wait()]
    if cross:
        src = src_s.wait()
        src_q = [src.at[0:half], src.at[half:length]]
    else:
        src_q = src_k
    for side, (w_s, short) in enumerate(((w_m, bias_m), (w_t, bias_t))):
        w = w_s.wait()
        bias_q = column_of(short[0:1, :])
        bias_v = column_of(short[1:2, :])
        for piece in range(2):
            at = slice(piece * half, (piece + 1) * half)
            q = ((dg(w[0], src_q[piece][...], 0, 1) + bias_q) * (SCALE * LOG2E)).astype(bf16)
            k = dg(w[1], src_k[piece][...], 0, 1).astype(bf16)
            v = (dg(w[2], src_k[piece][...], 0, 1) + bias_v).astype(bf16)
            for i in range(heads_half):
                h = side * heads_half + i
                rows = slice(i * HEAD_DIM, (i + 1) * HEAD_DIM)
                qa[h, 0:64, at] = q[rows]
                ka[h, 0:64, at] = k[rows]
                va[h, 0:64, at] = v[rows]
    ka_s.store()
    va_s.store()

    def some_heads(step, _):
        items = [(step * FWD_HEADS + j, slice(i, i + FWD_QB)) for j in range(FWD_HEADS) for i in range(0, length, FWD_QB)]

        def scores_of(item):
            h, at = item
            return dg(ka[h], qa[h, :, at], 0, 0)

        scores = scores_of(items[0])
        for n, (h, at) in enumerate(items):
            following = scores_of(items[n + 1]) if n + 1 < len(items) else None
            top = jnp.max(scores, axis=0, keepdims=True)
            weights = jnp.exp2(scores - top).astype(bf16)
            out = dg(va[h], weights, 1, 0)
            total = out[64:65, :]
            ctx[pl.ds(pl.multiple_of(h * HEAD_DIM, HEAD_DIM), HEAD_DIM), at] = (out[0:64, :] * (1.0 / total)).astype(bf16)
            high, middle, low = three_parts(-(top + jnp.log2(total)))
            extra = tall((16, FWD_QB), {4: high, 5: middle, 6: low})
            qa[h, 64:80, at] = qa[h, 64:80, at] + extra.astype(bf16)
            scores = following
        return 0

    lax.fori_loop(0, heads // FWD_HEADS, some_heads, 0)
    qa_s.store()
    ctx_s.store()
    norm = 1 if cross else 0
    bias = row_of(out_bias)
    gain = gains[norm : norm + 1, :].astype(f32)
    shift = shifts[norm : norm + 1, :].astype(f32)
    wo = [wo_m.wait(), wo_t.wait()]
    for i in range(length // TB):
        at = slice(i * TB, (i + 1) * TB)
        y = dg(ctx[0:hw, at], wo[0][...], 0, 0) + dg(ctx[hw:, at], wo[1][...], 0, 0) + bias
        piece, inner = divmod(i * TB, half)
        y = y + src_q[piece][inner : inner + TB, :].astype(f32)
        y_out[at, :] = y
        y_s.store(at)
        xhat, _ = norm_parts(y)
        h_out[at, :] = (xhat * gain + shift).astype(bf16)
        h_s.store(at)


def back_heads(count, qa, ka, va, da, ctx, dq, dk, dv):
    length = qa.shape[2]

    def one_head(h, _):
        rows = pl.ds(pl.multiple_of(h * HEAD_DIM, HEAD_DIM), HEAD_DIM)
        keys = ka[h]
        values = va[h]
        inner = jnp.sum(da[h, 0:64, :].astype(f32) * ctx[rows, :].astype(f32), axis=0, keepdims=True)
        high, middle, low = three_parts(-inner)
        da[h, 64:80, :] = tall((16, length), {0: high, 1: middle, 2: low}).astype(bf16)
        cuts = [slice(i * QB, (i + 1) * QB) for i in range(length // QB)]

        def products(at):
            return dg(qa[h, :, at], keys, 0, 0), dg(da[h, :, at], values, 0, 0)

        ahead = products(cuts[0])
        for n, at in enumerate(cuts):
            scores, spread = ahead
            if n + 1 < len(cuts):
                ahead = products(cuts[n + 1])
            weights = jnp.exp2(scores)
            ds = (weights * spread).astype(bf16)
            dv_part = dg(da[h, 0:64, at], weights.astype(bf16), 1, 0)
            dk_part = dg(qa[h, 0:64, at], ds, 1, 0)
            dv_sum = dv_part if n == 0 else dv_sum + dv_part
            dk_sum = dk_part if n == 0 else dk_sum + dk_part
            dq[rows, at] = (dg(keys[0:64], ds, 1, 1) * SCALE).astype(bf16)
        dk[rows, :] = (dk_sum * LN2).astype(bf16)
        dv[rows, :] = dv_sum.astype(bf16)
        return 0

    lax.fori_loop(0, count, one_head, 0)


def weight_rows(g, grads, sources):
    for j, (grad, pair) in enumerate(zip(grads, sources)):
        hw, length = grad.shape
        half = length // 2
        total = dg(pair[0][...], grad[:, 0:half], 0, 1) + dg(pair[1][...], grad[:, half:length], 0, 1)
        put = slice(j * hw, (j + 1) * hw)
        inner = total.shape[0] // 2
        g.near[put, 0:hw] = total[0:inner].astype(bf16)
        g.near[put, hw : 2 * hw] = total[inner:].astype(bf16)
        g.store(put)


def position_sums(dq, dv):
    ones = jnp.ones((8, dq.shape[1]), bf16)
    return dg(ones, dq[...], 1, 1)[0:1], dg(ones, dv[...], 1, 1)[0:1]


def cross_backward(core, ins, smalls, outs, _, scratch):
    dy_s, wo_m, wo_t, ctx_s, va_s, qa_s, ka_s, src_s, k_m, k_t, w_m, w_t, y_s, ctx1_s = ins
    gains, short_m, short_t = smalls
    g_m, g_t, dk_s, dv_s, dprev_s, do_s, ns_m, ns_t = outs
    da, dq = scratch
    dk, dv = dk_s.near, dv_s.near
    length, width = dy_s.near.shape
    half = length // 2
    hw = wo_m.near.shape[0]
    each = hw // HEAD_DIM
    dout = dy_s.wait()[...].astype(bf16)
    ctx = ctx_s.near
    for side, wo in enumerate((wo_m, wo_t)):
        dctx = dg(wo.wait()[...], dout, 1, 1).astype(bf16)
        for i in range(each):
            da[side * each + i, 0:64, :] = dctx[i * HEAD_DIM : (i + 1) * HEAD_DIM]
    ctx_s.wait()
    for side, g in enumerate((g_m, g_t)):
        rows = slice(3 * hw, 4 * hw)
        g.near[rows, :] = dg(ctx[side * hw : (side + 1) * hw, :], dout, 1, 0).astype(bf16)
        g.store(rows)
    va, qa, ka = va_s.wait(), qa_s.wait(), ka_s.wait()
    back_heads(2 * each, qa, ka, va, da, ctx, dq, dk, dv)
    dk_s.store()
    dv_s.store()
    src = src_s.wait()
    src_q = [src.at[0:half], src.at[half:length]]
    src_k = [k_m.wait(), k_t.wait()]
    w = [w_m.wait(), w_t.wait()]
    y_prev = y_s.wait()
    dy = dy_s.near
    dprev = dprev_s.near
    dout1 = do_s.near
    gain = gains[0:1, :].astype(f32)
    gain_sum = jnp.zeros((1, width), f32)
    shift_sum = jnp.zeros((1, width), f32)
    out_sum = jnp.zeros((1, width), f32)
    for i in range(length // TB):
        at = slice(i * TB, (i + 1) * TB)
        e = dy[at, :] + dg(dq[0:hw, at], w[0][0], 0, 1) + dg(dq[hw:, at], w[1][0], 0, 1)
        xhat, spread = norm_parts(y_prev[at, :])
        back, d_gain, d_shift = norm_back(xhat, spread, gain, e)
        dprev[at, :] = back
        dprev_s.store(at)
        rounded = back.astype(bf16)
        dout1[at, :] = rounded
        gain_sum += d_gain
        shift_sum += d_shift
        out_sum += jnp.sum(rounded.astype(f32), axis=0, keepdims=True)
    do_s.store()
    ctx1 = ctx1_s.wait()
    q_sum, v_sum = position_sums(dq, dv)
    for side, g, short, ns in ((1, g_t, short_t, ns_t), (0, g_m, short_m, ns_m)):
        rows = slice(side * hw, (side + 1) * hw)
        weight_rows(g, [dq.at[rows], dk.at[rows], dv.at[rows]], [src_q, src_k, src_k])
        put = slice(4 * hw, 5 * hw)
        g.near[put, :] = dg(ctx1[rows, :], dout1[...], 1, 0).astype(bf16)
        g.store(put)
        own = jnp.concatenate([q_sum[:, rows], v_sum[:, rows]], axis=1)
        ns.near[...] = short[...]
        ns.near[S_GAIN : S_GAIN + 1, :] = gain_sum
        ns.near[S_SHIFT : S_SHIFT + 1, :] = shift_sum
        ns.near[S_SELF_OB : S_SELF_OB + 1, :] = out_sum
        ns.near[S_CROSS_B : S_CROSS_B + 1, :] = own
        ns.store()


def self_backward(sides, core, ins, smalls, outs, _, scratch):
    do_s, x_m, x_t = ins[0:3]
    dout = do_s.wait()
    for n in range(sides):
        wo, da = ins[3 + 5 * n], scratch[n]
        dctx = dg(wo.wait()[...], dout[...], 1, 1).astype(bf16)
        for i in range(da.shape[0]):
            da[i, 0:64, :] = dctx[i * HEAD_DIM : (i + 1) * HEAD_DIM]
    for n in range(sides):
        ctx, va, qa, ka = [one.wait() for one in ins[4 + 5 * n : 8 + 5 * n]]
        g = outs[4 * n]
        grads = [one.near for one in outs[4 * n + 1 : 4 * n + 4]]
        back_heads(qa.shape[0], qa, ka, va, scratch[n], ctx, *grads)
        for one in outs[4 * n + 1 : 4 * n + 4]:
            one.store()
        src = [x_m.wait(), x_t.wait()]
        weight_rows(g, grads, [src] * 3)
        short = smalls[n]
        q_sum, v_sum = position_sums(grads[0], grads[2])
        own = jnp.concatenate([q_sum, v_sum], axis=1)
        index = lax.broadcasted_iota(jnp.int32, short.shape, 0)
        rows = jnp.where(index == S_SELF_B, jnp.broadcast_to(own, short.shape), short[...])
        start = 3 * grads[0].shape[0]
        stop, end = start + short.shape[0], g.near.shape[0]
        g.near[start:stop, :] = rows.astype(bf16)
        if stop < end:
            g.near[stop:end, :] = jnp.zeros((end - stop, g.near.shape[1]), bf16)
        g.store(slice(start, end))


def memory_gradient(core, ins, smalls, outs, _, scratch):
    dk_s, dv_s, w_m, w_t = ins
    out_m, out_t = outs
    dk, dv, w0, w1 = dk_s.wait(), dv_s.wait(), w_m.wait(), w_t.wait()
    hw = w0.shape[2]
    half = out_m.near.shape[0]
    for piece, out in ((1, out_t), (0, out_m)):
        at = slice(piece * half, (piece + 1) * half)
        total = dg(dk[0:hw, at], w0[1], 0, 1) + dg(dk[hw:, at], w1[1], 0, 1)
        total = total + dg(dv[0:hw, at], w0[2], 0, 1) + dg(dv[hw:, at], w1[2], 0, 1)
        out.near[...] = total.astype(bf16)
        out.store()


def input_gradient(core, ins, smalls, outs, _, scratch):
    dy_s = ins[-1]
    out_m, out_t = outs
    sides = [[one.wait() for one in ins[0:4]], [one.wait() for one in ins[4:8]]]
    dy = dy_s.wait()
    half = out_m.near.shape[0]
    for piece, out in ((1, out_t), (0, out_m)):
        at = slice(piece * half, (piece + 1) * half)
        total = dy[at, :]
        for grads in sides:
            for j in range(3):
                total = total + dg(grads[j][:, at], grads[3][j], 0, 1)
        out.near[...] = total.astype(bf16)
        out.store()


def place_of(slot, core, length):
    place = slot[pl.ds(core, 1), :]
    half = length // 2
    return jnp.where(core == 0, place, jnp.where(place >= half, place - half, place + half))


def slot_matrix(slot, core, length):
    row = place_of(slot, core, length)
    shape = (length, row.shape[1])
    return jnp.where(lax.broadcasted_iota(jnp.int32, shape, 0) == jnp.broadcast_to(row, shape), 1.0, 0.0).astype(bf16)


def feed_forward(core, ins, smalls, outs, _, scratch):
    gs_m, gs_t, ws_m, ws_t, go_m, go_t, h2_s, wi_m, wi_t, wo_m, wo_t, y2_s = ins
    bi_m, bi_t, ob, gains, shifts, slot = smalls
    out_m, out_t, dy2_s, g_m, g_t, small_m, small_t = outs
    onehot, tl, tr, e3, hid, dpre, slope, df_all, states = scratch
    length, width = h2_s.near.shape
    half = length // 2
    fw = wi_m.near.shape[1]
    sw = ws_m.near.shape[1]
    onehot[...] = slot_matrix(slot, core, length)
    for side, (gs, ws) in enumerate(((gs_m, ws_m), (gs_t, ws_t))):
        cols = slice(side * sw, (side + 1) * sw)
        left = dg(onehot[...], gs.wait()[...], 1, 0)
        tl[:, cols] = left.astype(bf16)
        tr[:, cols] = pltpu.roll(left, 1, 0).astype(bf16)
    ws = [ws_m.wait(), ws_t.wait()]
    go = [go_m.wait(), go_t.wait()]
    for i in range(length // TB):
        at = slice(i * TB, (i + 1) * TB)
        piece, inner = divmod(i * TB, half)
        total = go[piece][inner : inner + TB, :].astype(f32)
        for side in range(2):
            cols = slice(side * sw, (side + 1) * sw)
            total = total + dg(tl[at, cols], ws[side][0:width, :], 1, 1) + dg(tr[at, cols], ws[side][width : 2 * width, :], 1, 1)
        e3[at, :] = total
    h2, y2 = h2_s.wait(), y2_s.wait()
    wi = [wi_m.wait(), wi_t.wait()]
    wo = [wo_m.wait(), wo_t.wait()]
    dy2 = dy2_s.near
    bias_in = [row_of(bi_m), row_of(bi_t)]
    bias_out = row_of(ob)
    gain2 = gains[1:2, :].astype(f32)
    gain3 = gains[2:3, :].astype(f32)
    shift3 = shifts[2:3, :].astype(f32)

    def one_block(i, sums):
        gain3_sum, shift3_sum, gain2_sum, shift2_sum, ffn_out_sum, cross_out_sum, in_m_sum, in_t_sum = sums
        at = pl.ds(pl.multiple_of(i * FFN_TB, FFN_TB), FFN_TB)
        hb = h2[at, :]
        y3 = hb.astype(f32) + bias_out
        for side in range(2):
            cols = slice(side * fw, (side + 1) * fw)
            pre = dg(hb, wi[side][...], 1, 0) + bias_in[side]
            square = pre * pre
            tanh = jnp.tanh(pre * (GELU_C + GELU_C * GELU_A * square))
            gate = 0.5 + 0.5 * tanh
            hidden = (pre * gate).astype(bf16)
            hid[at, cols] = hidden
            slope[:, cols] = gate + (0.5 * pre) * (1.0 - tanh * tanh) * (GELU_C + 3.0 * GELU_C * GELU_A * square)
            y3 = y3 + dg(hidden, wo[side][...], 1, 0)
        xhat, spread = norm_parts(y3)
        states[at, :] = (xhat * gain3 + shift3).astype(bf16)
        dy3, d_gain, d_shift = norm_back(xhat, spread, gain3, e3[at, :])
        gain3_sum += d_gain
        shift3_sum += d_shift
        df = dy3.astype(bf16)
        df_all[at, :] = df
        ffn_out_sum += jnp.sum(df.astype(f32), axis=0, keepdims=True)
        e2 = dy3
        in_sums = []
        for side, in_sum in enumerate((in_m_sum, in_t_sum)):
            cols = slice(side * fw, (side + 1) * fw)
            back = (dg(df, wo[side][...], 1, 1) * slope[:, cols]).astype(bf16)
            dpre[at, cols] = back
            in_sums.append(in_sum + jnp.sum(back.astype(f32), axis=0, keepdims=True))
            e2 = e2 + dg(back, wi[side][...], 1, 1)
        xhat, spread = norm_parts(y2[at, :])
        back2, d_gain, d_shift = norm_back(xhat, spread, gain2, e2)
        dy2[at, :] = back2
        gain2_sum += d_gain
        shift2_sum += d_shift
        cross_out_sum += jnp.sum(back2.astype(bf16).astype(f32), axis=0, keepdims=True)
        return gain3_sum, shift3_sum, gain2_sum, shift2_sum, ffn_out_sum, cross_out_sum, in_sums[0], in_sums[1]

    row = jnp.zeros((1, width), f32)
    wide = jnp.zeros((1, fw), f32)
    sums = lax.fori_loop(0, length // FFN_TB, one_block, (row, row, row, row, row, row, wide, wide))
    dy2_s.store()
    for piece, out in ((1, out_t), (0, out_m)):
        out.near[...] = states[piece * half : (piece + 1) * half, :]
        out.store()
    for side, g in ((1, g_t), (0, g_m)):
        for i in range(fw // width):
            block = slice(side * fw + i * width, side * fw + (i + 1) * width)
            rows = slice(width + i * width, 2 * width + i * width)
            g.near[rows, :] = dg(h2[...], dpre[:, block], 0, 0).astype(bf16)
            g.store(rows)
            rows = slice(width + fw + i * width, 2 * width + fw + i * width)
            g.near[rows, :] = dg(hid[:, block], df_all[...], 0, 0).astype(bf16)
            g.store(rows)
        cols = slice(side * sw, (side + 1) * sw)
        rows = slice(0, width)
        g.near[rows, 0:sw] = dg(states[...], tl[:, cols], 0, 0).astype(bf16)
        g.near[rows, sw : 2 * sw] = dg(states[...], tr[:, cols], 0, 0).astype(bf16)
        g.store(rows)
    for short, total, gs in ((small_m, sums[6], gs_m), (small_t, sums[7], gs_t)):
        short.near[...] = jnp.zeros(short.near.shape, f32)
        for at, one in ((S_GAIN + 2, 0), (S_SHIFT + 2, 1), (S_GAIN + 1, 2), (S_SHIFT + 1, 3), (S_FFN_OB, 4), (S_CROSS_OB, 5)):
            short.near[at : at + 1, :] = sums[one]
        for i in range(fw // width):
            short.near[S_FFN_B + i : S_FFN_B + i + 1, :] = total[:, i * width : (i + 1) * width]
        short.near[S_SLOT_B : S_SLOT_B + 1, 0:sw] = jnp.sum(gs.near[...].astype(f32), axis=0, keepdims=True)
        short.store()


def slot_forward(core, ins, smalls, outs, _, scratch):
    out_m, out_t, ws_m, ws_t = ins
    bs_m, bs_t, slot = smalls
    onehot, states = scratch
    length, width = states.shape
    half = length // 2
    onehot[...] = slot_matrix(slot, core, length)
    states[0:half, :] = out_m.wait()[...]
    states[half:length, :] = out_t.wait()[...]
    for ws_s, short, out in ((ws_t, bs_t, outs[1]), (ws_m, bs_m, outs[0])):
        ws = ws_s.wait()
        top = dg(states[...], ws[0:width, :], 1, 0)
        low = dg(states[...], ws[width : 2 * width, :], 1, 0)
        total = (top + pltpu.roll(low, length - 1, 0) + row_of(short)).astype(bf16)
        out.near[...] = dg(onehot[...], total, 0, 0).astype(bf16)
        out.store()


def joined(scalars, ins):
    bit = scalars[1]
    own, got = ins[0].wait(), ins[1].wait()
    return jnp.where(bit == 0, own[...], got[...]), jnp.where(bit == 0, got[...], own[...])


def put_qkv(out, buf, hw):
    for j in range(3):
        out.near[j, 0:hw, :] = buf[j * hw : (j + 1) * hw, 0:hw].astype(f32)
        out.near[j, hw : 2 * hw, :] = buf[j * hw : (j + 1) * hw, hw : 2 * hw].astype(f32)
    out.store()


def unpack_cross(scalars, ins, smalls, outs, small_outs, scratch):
    (buf,) = scratch
    count = buf.shape[0] // 2
    buf[0:count, :], buf[count:, :] = joined(scalars, ins)
    qkv, cross_out, self_out = outs
    hw = cross_out.near.shape[0]
    put_qkv(qkv, buf, hw)
    cross_out.near[...] = buf[3 * hw : 4 * hw, :].astype(f32)
    cross_out.store()
    self_out.near[...] = buf[4 * hw : 5 * hw, :].astype(f32)
    self_out.store()


def unpack_self(scalars, ins, smalls, outs, small_outs, scratch):
    (buf,) = scratch
    count = buf.shape[0] // 2
    buf[0:count, :], buf[count:, :] = joined(scalars, ins)
    (qkv,) = outs
    hw = qkv.near.shape[2]
    put_qkv(qkv, buf, hw)
    self_b, self_ob, cross_b, cross_ob, ffn_b, ffn_ob, gains, shifts, slot_b = small_outs
    short = buf[3 * hw : 3 * hw + 16, :].astype(f32)
    width = short.shape[1]
    for ref, at in ((self_b, S_SELF_B), (cross_b, S_CROSS_B)):
        ref[0:1, :] = short[at : at + 1, 0:hw]
        ref[1:2, :] = short[at : at + 1, hw : 2 * hw]
    for ref, at in ((self_ob, S_SELF_OB), (cross_ob, S_CROSS_OB), (ffn_ob, S_FFN_OB)):
        ref[...] = short[at : at + 1, :].reshape(width)
    wide = ffn_b.shape[0] // width
    ffn_b[...] = jnp.concatenate([short[S_FFN_B + i : S_FFN_B + i + 1, :] for i in range(wide)], axis=1).reshape(wide * width)
    gains[...] = short[S_GAIN : S_GAIN + 3, :]
    shifts[...] = short[S_SHIFT : S_SHIFT + 3, :]
    slot_b[...] = short[S_SLOT_B : S_SLOT_B + 1, 0 : slot_b.shape[0]].reshape(slot_b.shape[0])


def unpack_ffn(core, ins, smalls, outs, _, scratch):
    slot, into, back = ins
    slot_w, ffn_in, ffn_out = outs
    buf = slot.wait()
    width = buf.shape[0]
    sw = slot_w.near.shape[1]
    slot_w.near[0:width, :] = buf[:, 0:sw].astype(f32)
    slot_w.near[width:, :] = buf[:, sw : 2 * sw].astype(f32)
    slot_w.store()
    buf = into.wait()
    for i in range(ffn_in.near.shape[1] // width):
        ffn_in.near[:, i * width : (i + 1) * width] = buf[i * width : (i + 1) * width, :].astype(f32)
    ffn_in.store()
    ffn_out.near[...] = back.wait()[...].astype(f32)
    ffn_out.store()


def swap(x):
    return lax.ppermute(x, "tensor", [(0, 1), (1, 0)])


def pair_add(core, ins, smalls, outs, _, scratch):
    (out,) = outs
    count = len(ins) // 2
    for i in range(count):
        kept, got = ins[i].wait(), ins[count + i].wait()
        rows = slice(i * kept.shape[0], (i + 1) * kept.shape[0])
        out.near[rows, :] = (kept[...].astype(f32) + got[...].astype(f32)).astype(bf16)
        out.store(rows)


def pair_sum(core, kept, got, after):
    cuts = [slice(i, i + PAIR_ROWS) for i in range(0, kept.shape[0], PAIR_ROWS)]
    return staged_call(pair_add, core, [(kept, cut) for cut in cuts] + [(got, cut) for cut in cuts], [],
                       [(kept.shape, bf16, len(cuts))], after=after, micros=3)[0]


class RowSum:
    def __init__(self, x, dp_size, dp_index, core):
        bits = dp_size.bit_length() - 1
        orders = [list(range(bits)), list(range(bits))]
        if bits > 2:
            orders[1] = [1, 2, 0] + list(range(3, bits))
        self.plan = []
        for step in range(bits):
            pairs = []
            for device in range(dp_size):
                for c in range(2):
                    pairs.append((device * 2 + c, (device ^ (1 << orders[c][step])) * 2 + c))
            bit = jnp.where(core == 0, (dp_index >> orders[0][step]) & 1, (dp_index >> orders[1][step]) & 1)
            self.plan.append((pairs, bit.astype(jnp.int32)))
        self.x = x
        self.step = 0
        self.cut()

    def cut(self):
        if self.step >= len(self.plan) - 1:
            self.away = self.kept = self.x
            return
        bit = self.plan[self.step][1]
        count = self.x.shape[0] // 2
        self.away = lax.dynamic_slice_in_dim(self.x, (1 - bit) * count, count, 0)
        self.kept = lax.dynamic_slice_in_dim(self.x, bit * count, count, 0)

    def scatter(self, *beside):
        got = lax.ppermute(self.away, ("dp", "tensor"), self.plan[self.step][0])
        if beside:
            got = lax.optimization_barrier((got, *beside))[0]
        self.x = (self.kept.astype(f32) + got.astype(f32)).astype(bf16)
        self.step += 1
        self.cut()

    def gather(self):
        x = self.x
        for step in reversed(range(len(self.plan) - 1)):
            pairs, bit = self.plan[step]
            got = lax.ppermute(x, ("dp", "tensor"), pairs)
            if step == 0:
                return x, got
            first = lax.broadcasted_iota(jnp.int32, (2,) + x.shape, 0) == bit
            x = jnp.where(first, x[None], got[None]).reshape((2 * x.shape[0],) + x.shape[1:])


def shards(dp_size, *args):
    (tokens, memory, dec_segment, enc_segment, slot_left, self_qkv, self_bias, self_out, self_out_bias,
     cross_qkv, cross_bias, cross_out, cross_out_bias, ffn_in, ffn_in_bias, ffn_out, ffn_out_bias,
     norm_gain, norm_bias, slot_weight, slot_bias, grad_output, grad_slots) = args
    core_index = lax.axis_index("tensor")
    dp_index = lax.axis_index("dp")
    core = core_index.astype(jnp.int32).reshape(1)
    half, width = tokens.shape[1], tokens.shape[2]
    length = 2 * half
    hw = self_qkv.shape[2]
    heads = 2 * hw // HEAD_DIM
    fw = ffn_in.shape[1]
    wide = fw // width
    sw = slot_weight.shape[1]
    slots = slot_left.shape[1]

    tokens_t = swap(tokens)
    self_qkv_t = swap(self_qkv)
    self_bias_t = swap(self_bias)
    self_out_t = swap(self_out)
    memory_t = swap(memory)
    cross_qkv_t = swap(cross_qkv)
    cross_bias_t = swap(cross_bias)
    cross_out_t = swap(cross_out)
    grad_slots_t = swap(grad_slots)
    slot_weight_t = swap(slot_weight)
    grad_output_t = swap(grad_output)
    ffn_in_t = swap(ffn_in)
    ffn_in_bias_t = swap(ffn_in_bias)
    ffn_out_t = swap(ffn_out)
    slot_bias_t = swap(slot_bias)

    aug = (heads, AUG, length)
    blocks = length // TB
    forward_outs = [(aug, bf16, 1), (aug, bf16, 1), (aug, bf16, 1), ((2 * hw, length), bf16, 1),
                    ((length, width), f32, blocks), ((length, width), bf16, blocks)]
    qa, ka, va, ctx, y1, h1 = staged_call(
        functools.partial(attend_forward, False), core,
        [(tokens, "core"), (tokens_t, "core"), (self_qkv, None), (self_qkv_t, None), (self_out, None), (self_out_t, None)],
        [self_bias, self_bias_t, self_out_bias, norm_gain, norm_bias, dec_segment], forward_outs, micros=18)
    qa2, ka2, va2, ctx2, y2, h2 = staged_call(
        functools.partial(attend_forward, True), core,
        [(h1, None), (memory, "core"), (memory_t, "core"), (cross_qkv, None), (cross_qkv_t, None), (cross_out, None),
         (cross_out_t, None)],
        [cross_bias, cross_bias_t, cross_out_bias, norm_gain, norm_bias, dec_segment, enc_segment], forward_outs, micros=18)
    g1_rows = width + 2 * fw
    half_out = ((half, width), bf16, 1)
    out_m, out_t, dy2, g1_m, g1_t, short1_m, short1_t = staged_call(
        feed_forward, core,
        [(grad_slots, "core"), (grad_slots_t, "core"), (slot_weight, None), (slot_weight_t, None), (grad_output, "core"),
         (grad_output_t, "core"), (h2, None), (ffn_in, None), (ffn_in_t, None), (ffn_out, None), (ffn_out_t, None),
         (y2, None)],
        [ffn_in_bias, ffn_in_bias_t, ffn_out_bias, norm_gain, norm_bias, slot_left],
        [half_out, half_out, ((length, width), f32, 1), ((g1_rows, width), bf16, 1 + 2 * wide),
         ((g1_rows, width), bf16, 1 + 2 * wide), ((16, width), f32, 1), ((16, width), f32, 1)],
        scratch=[pltpu.VMEM((length, slots), bf16), pltpu.VMEM((length, 2 * sw), bf16), pltpu.VMEM((length, 2 * sw), bf16),
                 pltpu.VMEM((length, width), f32), pltpu.VMEM((length, 2 * fw), bf16), pltpu.VMEM((length, 2 * fw), bf16),
                 pltpu.VMEM((FFN_TB, 2 * fw), f32), pltpu.VMEM((length, width), bf16), pltpu.VMEM((length, width), bf16)],
        after=[slot_bias_t], micros=25)
    st_m, st_t = staged_call(
        slot_forward, core, [(out_m, None), (out_t, None), (slot_weight, None), (slot_weight_t, None)],
        [slot_bias, slot_bias_t, slot_left], [((slots, sw), bf16, 1), ((slots, sw), bf16, 1)],
        scratch=[pltpu.VMEM((length, slots), bf16), pltpu.VMEM((length, width), bf16)], micros=4)
    g1 = pair_sum(core, g1_m, swap(g1_t), [st_m])
    g1_sum = lax.psum(g1, "dp")
    def attention_part():
        g2_m, g2_t, dk2, dv2, dy1, do1, short2_m, short2_t = staged_call(
            cross_backward, core,
            [(dy2, None), (cross_out, None), (cross_out_t, None), (ctx2, None), (va2, None), (qa2, None), (ka2, None),
             (h1, None), (memory, "core"), (memory_t, "core"), (cross_qkv, None), (cross_qkv_t, None), (y1, None), (ctx, None)],
            [norm_gain, short1_m, short1_t],
            [((5 * hw, width), bf16, 5), ((5 * hw, width), bf16, 5), ((2 * hw, length), bf16, 1), ((2 * hw, length), bf16, 1),
             ((length, width), f32, blocks), ((length, width), bf16, 1), ((16, width), f32, 1), ((16, width), f32, 1)],
            scratch=[pltpu.VMEM(aug, bf16), pltpu.VMEM((2 * hw, length), bf16)], after=[g1], micros=30)
        dmem_m, dmem_t = staged_call(
            memory_gradient, core, [(dk2, None), (dv2, None), (cross_qkv, None), (cross_qkv_t, None)], [],
            [half_out, half_out], micros=4)

        def packed(total):
            return total.reshape(dp_size, total.shape[0] // dp_size, width)

        sum2 = RowSum(packed((g2_m.astype(f32) + swap(g2_t).astype(f32)).astype(bf16)), dp_size, dp_index, core_index)
        g3_rows = 3 * hw + 16 + (-(3 * hw + 16)) % 128
        g3_rows += -g3_rows % dp_size
        count = heads // 2
        side_outs = [((g3_rows, width), bf16, 4)] + [((hw, length), bf16, 1)] * 3
        sides = {}
        held = [dmem_m]
        for group in SELF_GROUPS:
            inputs, shorts = [], []
            for side in group:
                of = slice(side * count, (side + 1) * count)
                inputs += [((self_out, self_out_t)[side], None), (ctx, slice(side * hw, (side + 1) * hw)), (va, of), (qa, of), (ka, of)]
                shorts.append((short2_m, short2_t)[side])
            found = staged_call(
                functools.partial(self_backward, len(group)), core,
                [(do1, None), (tokens, "core"), (tokens_t, "core")] + inputs, shorts, side_outs * len(group),
                scratch=[pltpu.VMEM((count, AUG, length), bf16)] * len(group), after=held + [sum2.away], micros=14 * len(group))
            sum2.scatter()
            held = []
            for n, side in enumerate(group):
                w = (self_qkv, self_qkv_t)[side]
                sides[side] = (found[4 * n], [(g, None) for g in found[4 * n + 1 : 4 * n + 4]] + [(w, None)])
        while sum2.step < len(sum2.plan):
            sum2.scatter()
        sum3 = RowSum(packed((sides[0][0].astype(f32) + swap(sides[1][0]).astype(f32)).astype(bf16)), dp_size, dp_index, core_index)
        dx_m, dx_t = staged_call(input_gradient, core, sides[0][1] + sides[1][1] + [(dy1, None)], [], [half_out, half_out], micros=5)
        def together(kept, sent):
            got = swap(sent)
            return jnp.where(lax.broadcasted_iota(jnp.int32, (2,) + kept.shape, 0) == core_index, kept[None], got[None])

        output = together(out_m, out_t)
        slot_states = together(st_m, st_t)
        grad_memory = together(dmem_m, dmem_t)
        sum3.scatter(output, slot_states, grad_memory)
        while sum3.step < len(sum3.plan):
            sum3.scatter()

        grad_input = together(dx_m, dx_t)

        def ends(total):
            own, got = total.gather()
            flat = lambda x: x.reshape(-1, width)
            return jnp.stack([core_index.astype(jnp.int32), total.plan[0][1]]), [(flat(own), None), (flat(got), None)]

        qkv_out = ((3, 2 * hw, hw), f32, 1)
        scalars, halves = ends(sum2)
        grad_cross_qkv, grad_cross_out, grad_self_out = staged_call(
            unpack_cross, scalars, halves, [], [qkv_out, ((hw, width), f32, 1), ((hw, width), f32, 1)],
            scratch=[pltpu.VMEM((5 * hw, width), bf16)], micros=3)
        scalars, halves = ends(sum3)
        (grad_self_qkv, grad_self_bias, grad_self_out_bias, grad_cross_bias, grad_cross_out_bias, grad_ffn_in_bias,
         grad_ffn_out_bias, grad_norm_gain, grad_norm_bias, grad_slot_bias) = staged_call(
            unpack_self, scalars, halves, [], [qkv_out],
            [((2, hw), f32), ((width,), f32), ((2, hw), f32), ((width,), f32), ((fw,), f32), ((width,), f32), ((3, width), f32),
             ((3, width), f32), ((sw,), f32)],
            scratch=[pltpu.VMEM((g3_rows, width), bf16)], micros=3)
        return (output, slot_states, grad_input, grad_memory, grad_self_qkv, grad_self_bias, grad_self_out, grad_self_out_bias,
                grad_cross_qkv, grad_cross_bias, grad_cross_out, grad_cross_out_bias, grad_ffn_in_bias, grad_ffn_out_bias,
                grad_norm_gain, grad_norm_bias, grad_slot_bias)

    shapes = jax.eval_shape(attention_part)
    nothing = lambda: tuple(jnp.zeros(one.shape, one.dtype) for one in shapes)
    (output, slot_states, grad_input, grad_memory, grad_self_qkv, grad_self_bias, grad_self_out, grad_self_out_bias,
     grad_cross_qkv, grad_cross_bias, grad_cross_out, grad_cross_out_bias, grad_ffn_in_bias, grad_ffn_out_bias,
     grad_norm_gain, grad_norm_bias, grad_slot_bias) = lax.cond(core_index < 2, attention_part, nothing)
    grad_slot_weight, grad_ffn_in, grad_ffn_out = staged_call(
        unpack_ffn, core, [(g1_sum, slice(0, width)), (g1_sum, slice(width, width + fw)), (g1_sum, slice(width + fw, g1_rows))],
        [], [((2 * width, sw), f32, 1), ((width, fw), f32, 1), ((fw, width), f32, 1)], micros=4)
    return (
        output, slot_states, grad_input, grad_memory, grad_self_qkv, grad_self_bias, grad_self_out, grad_self_out_bias,
        grad_cross_qkv, grad_cross_bias, grad_cross_out, grad_cross_out_bias, grad_ffn_in, grad_ffn_in_bias, grad_ffn_out,
        grad_ffn_out_bias, grad_norm_gain, grad_norm_bias, grad_slot_weight, grad_slot_bias,
    )


def solution(mesh):
    row3 = P("dp", "tensor", None)
    seg = P("dp", None)
    col3 = P(None, None, "tensor")
    col2 = P(None, "tensor")
    out2 = P("tensor", None)
    one = P("tensor")
    in_specs = (row3, row3, seg, seg, seg, col3, col2, out2, P(), col3, col2, out2, P(), col2, one, out2, P(), P(), P(),
                col2, one, row3, P("dp", None, "tensor"))
    out_specs = (row3, P("dp", None, "tensor"), row3, row3, col3, col2, out2, P(), col3, col2, out2, P(), col2, one, out2,
                 P(), P(), P(), col2, one)
    body = functools.partial(shards, mesh.shape["dp"])
    return jax.shard_map(body, mesh=mesh, in_specs=in_specs, out_specs=out_specs, check_vma=False)
```

```python
import functools
import math

import jax
import jax.numpy as jnp
from jax import lax
from jax.experimental import pallas as pl
from jax.experimental.pallas import tpu as pltpu
from jax.sharding import PartitionSpec as P

HEAD_DIM = 64
EPSILON = 1e-05
MASKED = -1e30
GELU_C = 0.7978845608028654
GELU_A = 0.044715
LOG2E = 1.4426950408889634
LN2 = 0.6931471805599453
SCALE = HEAD_DIM ** (-0.5)
AUG = 80
QB = 256
FWD_QB = 1024
FWD_HEADS = 4
FFN_TB = 512
TB = 256
VMEM_LIMIT = 63 * 2**20
SPARE = 20 * 2**20

bf16 = jnp.bfloat16
f32 = jnp.float32


def dg(a, b, ca, cb):
    return lax.dot_general(a, b, (((ca,), (cb,)), ((), ())), preferred_element_type=f32)


def column_of(row):
    return jnp.broadcast_to(row.astype(f32), (8, row.shape[1])).T[:, 0:1]


def three_parts(row):
    high = row.astype(bf16).astype(f32)
    rest = row - high
    middle = rest.astype(bf16).astype(f32)
    return high, middle, (rest - middle)


def tall(shape, rows):
    index = lax.broadcasted_iota(jnp.int32, shape, 0)
    block = jnp.zeros(shape, f32)
    for at, row in rows.items():
        block = jnp.where(index == at, jnp.broadcast_to(row, shape), block)
    return block


def norm_parts(y):
    centre = y - jnp.mean(y, axis=-1, keepdims=True)
    spread = lax.rsqrt(jnp.mean(centre * centre, axis=-1, keepdims=True) + EPSILON)
    return centre * spread, spread


def norm_back(xhat, spread, gain, e):
    a = e * gain
    dy = (a - jnp.mean(a, axis=-1, keepdims=True) - xhat * jnp.mean(a * xhat, axis=-1, keepdims=True)) * spread
    return dy, jnp.sum(e * xhat, axis=0, keepdims=True), jnp.sum(e, axis=0, keepdims=True)


ANY = pl.BlockSpec(memory_space=pl.ANY)
HBM = pl.BlockSpec(memory_space=pltpu.HBM)
VMEM = pl.BlockSpec(memory_space=pltpu.VMEM)
SMEM = pl.BlockSpec(memory_space=pltpu.SMEM)


class Staged:
    def __init__(self, far, near, sems, first, pick=None):
        self.far, self.near, self.sems, self.next, self.pending, self.pick = far, near, sems, first, [], pick

    def load(self):
        source = self.far if self.pick is None else self.far.at[self.pick]
        copy = pltpu.make_async_copy(source, self.near, self.sems.at[self.next])
        copy.start()
        self.pending.append(copy)

    def store(self, rows=None):
        near, far = (self.near, self.far) if rows is None else (self.near.at[rows], self.far.at[rows])
        copy = pltpu.make_async_copy(near, far, self.sems.at[self.next])
        self.next += 1
        copy.start()
        self.pending.append(copy)

    def wait(self):
        for copy in self.pending:
            copy.wait()
        self.pending = []
        return self.near


def staged_call(body, scalars, big_ins, small_ins, outs, small_outs=(), scratch=(), after=(), micros=10.0):
    def shape_of(a, part):
        if part is None:
            return a.shape
        return a.shape[1:] if part == "core" else (part.stop - part.start,) + a.shape[1:]

    def kernel(*refs):
        refs = list(refs)
        take = lambda n: [refs.pop(0) for _ in range(n)]
        (scalar_ref,) = take(1)
        far_in, smalls, _, far_out = take(len(big_ins)), take(len(small_ins)), take(len(after)), take(len(outs))
        short_out, buf_in, buf_out = take(len(small_outs)), take(len(big_ins)), take(len(outs))
        sem_in, sem_out = take(2)
        me = [scalar_ref[i] for i in range(scalars.shape[0])]
        ins = [
            Staged(far, near, sem_in, i, me[0] if part == "core" else part)
            for i, (far, near, (_, part)) in enumerate(zip(far_in, buf_in, big_ins))
        ]
        for one in ins:
            one.load()
        first = 0
        results = []
        for far, near, (_, _, n) in zip(far_out, buf_out, outs):
            results.append(Staged(far, near, sem_out, first))
            first += n
        body(me if len(me) > 1 else me[0], ins, smalls, results, short_out, refs)
        for one in ins + results:
            one.wait()

    held = [(shape_of(a, part), a.dtype) for a, part in big_ins] + [(s, d) for s, d, _ in outs]
    held += [(one.shape, one.dtype) for one in scratch]
    size = sum(math.prod(s) * jnp.dtype(d).itemsize for s, d in held)
    far = [pltpu.with_memory_space_constraint(a, pltpu.HBM) for a, _ in big_ins]
    small_ins = [pltpu.with_memory_space_constraint(a, pltpu.HBM) for a in small_ins]
    return pl.pallas_call(
        kernel,
        out_shape=[pltpu.HBM(s, d) for s, d, _ in outs] + [jax.ShapeDtypeStruct(s, d) for s, d in small_outs],
        in_specs=[SMEM] + [HBM] * len(big_ins) + [VMEM] * len(small_ins) + [ANY] * len(after),
        out_specs=[HBM] * len(outs) + [VMEM] * len(small_outs),
        scratch_shapes=[pltpu.VMEM(shape_of(a, part), a.dtype) for a, part in big_ins]
        + [pltpu.VMEM(s, d) for s, d, _ in outs]
        + [pltpu.SemaphoreType.DMA((len(big_ins),)), pltpu.SemaphoreType.DMA((max(1, sum(o[2] for o in outs)),))]
        + list(scratch),
        compiler_params=pltpu.CompilerParams(vmem_limit_bytes=min(VMEM_LIMIT, size + SPARE)),
        cost_estimate=pl.CostEstimate(flops=int(micros * 1.1e9), bytes_accessed=1024, transcendentals=0),
    )(scalars, *far, *small_ins, *after)


def row_of(ref):
    return ref[...].astype(f32).reshape(1, ref.shape[0])


S_GAIN, S_SHIFT, S_SELF_OB, S_CROSS_OB, S_FFN_OB, S_SELF_B, S_CROSS_B, S_FFN_B, S_SLOT_B = 0, 3, 6, 7, 8, 9, 10, 11, 13


def own_first(row, core):
    half = row.shape[1] // 2
    return jnp.where(core == 0, row, jnp.concatenate([row[:, half:], row[:, :half]], axis=1))


def attend_forward(cross, core, ins, smalls, outs, _, scratch):
    qa_s, ka_s, va_s, ctx_s, y_s, h_s = outs
    qa, ka, va, ctx, y_out, h_out = [o.near for o in outs]
    if cross:
        src_s, k_m, k_t, w_m, w_t, wo_m, wo_t = ins
        bias_m, bias_t, out_bias, gains, shifts, seg_d, seg_e = smalls
    else:
        k_m, k_t, w_m, w_t, wo_m, wo_t = ins
        bias_m, bias_t, out_bias, gains, shifts, seg_d = smalls
        seg_e = seg_d
    heads, _, length = qa.shape
    half = length // 2
    hw = w_m.near.shape[2]
    heads_half = heads // 2
    seg_q = own_first(seg_d[pl.ds(core, 1), :], core)
    seg_k = own_first(seg_e[pl.ds(core, 1), :], core)
    shape16 = (16, length)
    index = lax.broadcasted_iota(jnp.int32, shape16, 0)
    same_q = index == jnp.broadcast_to(seg_q, shape16)
    same_k = index == jnp.broadcast_to(seg_k, shape16)
    q_extra = jnp.where(index < 4, jnp.where(same_q, 0.0, MASKED), 0.0).astype(bf16)
    k_extra = jnp.where(index < 4, jnp.where(same_k, 1.0, 0.0), jnp.where(index < 7, 1.0, 0.0)).astype(bf16)
    v_extra = jnp.where(index < 3, 1.0, 0.0).astype(bf16)
    for h in range(heads):
        qa[h, 64:80, :] = q_extra
        ka[h, 64:80, :] = k_extra
        va[h, 64:80, :] = v_extra
    src_k = [k_m.wait(), k_t.wait()]
    if cross:
        src = src_s.wait()
        src_q = [src.at[0:half], src.at[half:length]]
    else:
        src_q = src_k
    for side, (w_s, short) in enumerate(((w_m, bias_m), (w_t, bias_t))):
        w = w_s.wait()
        bias_q = column_of(short[0:1, :])
        bias_v = column_of(short[1:2, :])
        for piece in range(2):
            at = slice(piece * half, (piece + 1) * half)
            q = ((dg(w[0], src_q[piece][...], 0, 1) + bias_q) * (SCALE * LOG2E)).astype(bf16)
            k = dg(w[1], src_k[piece][...], 0, 1).astype(bf16)
            v = (dg(w[2], src_k[piece][...], 0, 1) + bias_v).astype(bf16)
            for i in range(heads_half):
                h = side * heads_half + i
                rows = slice(i * HEAD_DIM, (i + 1) * HEAD_DIM)
                qa[h, 0:64, at] = q[rows]
                ka[h, 0:64, at] = k[rows]
                va[h, 0:64, at] = v[rows]
    ka_s.store()
    va_s.store()

    def some_heads(step, _):
        items = [(step * FWD_HEADS + j, slice(i, i + FWD_QB)) for j in range(FWD_HEADS) for i in range(0, length, FWD_QB)]

        def scores_of(item):
            h, at = item
            return dg(ka[h], qa[h, :, at], 0, 0)

        scores = scores_of(items[0])
        for n, (h, at) in enumerate(items):
            following = scores_of(items[n + 1]) if n + 1 < len(items) else None
            top = jnp.max(scores, axis=0, keepdims=True)
            weights = jnp.exp2(scores - top).astype(bf16)
            out = dg(va[h], weights, 1, 0)
            total = out[64:65, :]
            ctx[pl.ds(pl.multiple_of(h * HEAD_DIM, HEAD_DIM), HEAD_DIM), at] = (out[0:64, :] * (1.0 / total)).astype(bf16)
            high, middle, low = three_parts(-(top + jnp.log2(total)))
            extra = tall((16, FWD_QB), {4: high, 5: middle, 6: low})
            qa[h, 64:80, at] = qa[h, 64:80, at] + extra.astype(bf16)
            scores = following
        return 0

    lax.fori_loop(0, heads // FWD_HEADS, some_heads, 0)
    qa_s.store()
    ctx_s.store()
    norm = 1 if cross else 0
    bias = row_of(out_bias)
    gain = gains[norm : norm + 1, :].astype(f32)
    shift = shifts[norm : norm + 1, :].astype(f32)
    wo = [wo_m.wait(), wo_t.wait()]
    for i in range(length // TB):
        at = slice(i * TB, (i + 1) * TB)
        y = dg(ctx[0:hw, at], wo[0][...], 0, 0) + dg(ctx[hw:, at], wo[1][...], 0, 0) + bias
        piece, inner = divmod(i * TB, half)
        y = y + src_q[piece][inner : inner + TB, :].astype(f32)
        y_out[at, :] = y
        y_s.store(at)
        xhat, _ = norm_parts(y)
        h_out[at, :] = (xhat * gain + shift).astype(bf16)
        h_s.store(at)


def back_heads(count, qa, ka, va, da, ctx, dq, dk, dv):
    length = qa.shape[2]

    def one_head(h, _):
        rows = pl.ds(pl.multiple_of(h * HEAD_DIM, HEAD_DIM), HEAD_DIM)
        keys = ka[h]
        values = va[h]
        inner = jnp.sum(da[h, 0:64, :].astype(f32) * ctx[rows, :].astype(f32), axis=0, keepdims=True)
        high, middle, low = three_parts(-inner)
        da[h, 64:80, :] = tall((16, length), {0: high, 1: middle, 2: low}).astype(bf16)
        cuts = [slice(i * QB, (i + 1) * QB) for i in range(length // QB)]

        def products(at):
            return dg(qa[h, :, at], keys, 0, 0), dg(da[h, :, at], values, 0, 0)

        ahead = products(cuts[0])
        for n, at in enumerate(cuts):
            scores, spread = ahead
            if n + 1 < len(cuts):
                ahead = products(cuts[n + 1])
            weights = jnp.exp2(scores)
            ds = (weights * spread).astype(bf16)
            dv_part = dg(da[h, 0:64, at], weights.astype(bf16), 1, 0)
            dk_part = dg(qa[h, 0:64, at], ds, 1, 0)
            dv_sum = dv_part if n == 0 else dv_sum + dv_part
            dk_sum = dk_part if n == 0 else dk_sum + dk_part
            dq[rows, at] = (dg(keys[0:64], ds, 1, 1) * SCALE).astype(bf16)
        dk[rows, :] = (dk_sum * LN2).astype(bf16)
        dv[rows, :] = dv_sum.astype(bf16)
        return 0

    lax.fori_loop(0, count, one_head, 0)


def weight_rows(g, grads, sources):
    for j, (grad, pair) in enumerate(zip(grads, sources)):
        hw, length = grad.shape
        half = length // 2
        total = dg(pair[0][...], grad[:, 0:half], 0, 1) + dg(pair[1][...], grad[:, half:length], 0, 1)
        put = slice(j * hw, (j + 1) * hw)
        inner = total.shape[0] // 2
        g.near[put, 0:hw] = total[0:inner].astype(bf16)
        g.near[put, hw : 2 * hw] = total[inner:].astype(bf16)
        g.store(put)


def position_sums(dq, dv):
    ones = jnp.ones((8, dq.shape[1]), bf16)
    return dg(ones, dq[...], 1, 1)[0:1], dg(ones, dv[...], 1, 1)[0:1]


def heads_backward(ins, outs, da, dout):
    wo, ctx, va, qa, ka = ins
    dctx = dg(wo.wait()[...], dout[...], 1, 1).astype(bf16)
    for i in range(da.shape[0]):
        da[i, 0:64, :] = dctx[i * HEAD_DIM : (i + 1) * HEAD_DIM]
    ctx, va, qa, ka = ctx.wait(), va.wait(), qa.wait(), ka.wait()
    grads = [one.near for one in outs]
    back_heads(qa.shape[0], qa, ka, va, da, ctx, *grads)
    for one in outs:
        one.store()
    return grads


def halves_of(staged):
    if len(staged) == 2:
        return [one.wait() for one in staged]
    whole = staged[0].wait()
    half = whole.shape[0] // 2
    return [whole.at[0:half], whole.at[half : 2 * half]]


def out_rows(g, ctx, dout):
    hw = ctx.shape[0]
    put = slice(3 * hw, 4 * hw)
    g.near[put, :] = dg(ctx[...], dout[...], 1, 0).astype(bf16)
    g.store(put)


def cross_backward_first(core, ins, smalls, outs, _, scratch):
    do_s, src_s, k_m, k_t = ins[0:4]
    short, = smalls
    g, ns = outs[0:2]
    dout = do_s.wait()
    grads = heads_backward(ins[4:9], outs[2:5], scratch[0], dout)
    out_rows(g, ins[5].near, dout)
    src_k = [k_m.wait(), k_t.wait()]
    weight_rows(g, grads, [halves_of([src_s]), src_k, src_k])
    q_sum, v_sum = position_sums(grads[0], grads[2])
    ns.near[...] = short[...]
    ns.near[S_CROSS_B : S_CROSS_B + 1, :] = jnp.concatenate([q_sum, v_sum], axis=1)
    ns.store()


def cross_backward_second(core, ins, smalls, outs, _, scratch):
    do_s, src_s, k_m, k_t = ins[0:4]
    dy_s, y_s, dqt_s, wq_m, wq_t, ctx1_s = ins[9:15]
    gains, short_m, short_t = smalls
    g, ns_m, ns_t = outs[0:3]
    dprev_s, do1_s, so_t = outs[6:9]
    dout = do_s.wait()
    grads = heads_backward(ins[4:9], outs[3:6], scratch[0], dout)
    dq_m = grads[0]
    dq_t = dqt_s.wait()
    w = [wq_m.wait(), wq_t.wait()]
    y_prev = y_s.wait()
    dy = dy_s.wait()
    length, width = dy.shape
    hw = dq_m.shape[0]
    dprev = dprev_s.near
    dout1 = do1_s.near
    gain = gains[0:1, :].astype(f32)
    gain_sum = jnp.zeros((1, width), f32)
    shift_sum = jnp.zeros((1, width), f32)
    out_sum = jnp.zeros((1, width), f32)
    for i in range(length // TB):
        at = slice(i * TB, (i + 1) * TB)
        e = dy[at, :] + dg(dq_m[:, at], w[0][0], 0, 1) + dg(dq_t[:, at], w[1][0], 0, 1)
        xhat, spread = norm_parts(y_prev[at, :])
        back, d_gain, d_shift = norm_back(xhat, spread, gain, e)
        dprev[at, :] = back
        dprev_s.store(at)
        rounded = back.astype(bf16)
        dout1[at, :] = rounded
        gain_sum += d_gain
        shift_sum += d_shift
        out_sum += jnp.sum(rounded.astype(f32), axis=0, keepdims=True)
    do1_s.store()
    ctx1 = ctx1_s.wait()
    so_t.near[...] = dg(ctx1[hw : 2 * hw, :], dout1[...], 1, 0).astype(bf16)
    so_t.store()
    out_rows(g, ins[5].near, dout)
    put = slice(4 * hw, 5 * hw)
    g.near[put, :] = dg(ctx1[0:hw, :], dout1[...], 1, 0).astype(bf16)
    g.store(put)
    src_k = [k_m.wait(), k_t.wait()]
    weight_rows(g, grads, [halves_of([src_s]), src_k, src_k])
    q_sum, v_sum = position_sums(grads[0], grads[2])
    for short, ns in ((short_m, ns_m), (short_t, ns_t)):
        ns.near[...] = short[...]
        ns.near[S_GAIN : S_GAIN + 1, :] = gain_sum
        ns.near[S_SHIFT : S_SHIFT + 1, :] = shift_sum
        ns.near[S_SELF_OB : S_SELF_OB + 1, :] = out_sum
    ns_m.near[S_CROSS_B : S_CROSS_B + 1, :] = jnp.concatenate([q_sum, v_sum], axis=1)
    ns_m.store()
    ns_t.store()


def self_backward(core, ins, smalls, outs, _, scratch):
    do_s, x_m, x_t = ins[0:3]
    (short,) = smalls
    g = outs[0]
    grads = heads_backward(ins[3:8], outs[1:4], scratch[0], do_s.wait())
    src = [x_m.wait(), x_t.wait()]
    weight_rows(g, grads, [src] * 3)
    q_sum, v_sum = position_sums(grads[0], grads[2])
    own = jnp.concatenate([q_sum, v_sum], axis=1)
    index = lax.broadcasted_iota(jnp.int32, short.shape, 0)
    rows = jnp.where(index == S_SELF_B, jnp.broadcast_to(own, short.shape), short[...])
    start = 3 * grads[0].shape[0]
    stop, end = start + short.shape[0], g.near.shape[0]
    g.near[start:stop, :] = rows.astype(bf16)
    if stop < end:
        g.near[stop:end, :] = jnp.zeros((end - stop, g.near.shape[1]), bf16)
    g.store(slice(start, end))


def memory_gradient(core, ins, smalls, outs, _, scratch):
    out_m, out_t = outs
    sides = [[one.wait() for one in ins[0:3]], [one.wait() for one in ins[3:6]]]
    half = out_m.near.shape[0]
    for piece, out in ((1, out_t), (0, out_m)):
        at = slice(piece * half, (piece + 1) * half)
        total = None
        for dk, dv, w in sides:
            part = dg(dk[:, at], w[1], 0, 1) + dg(dv[:, at], w[2], 0, 1)
            total = part if total is None else total + part
        out.near[...] = total.astype(bf16)
        out.store()


def input_gradient(core, ins, smalls, outs, _, scratch):
    dy_s = ins[-1]
    out_m, out_t = outs
    sides = [[one.wait() for one in ins[0:4]], [one.wait() for one in ins[4:8]]]
    dy = dy_s.wait()
    half = out_m.near.shape[0]
    for piece, out in ((1, out_t), (0, out_m)):
        at = slice(piece * half, (piece + 1) * half)
        total = dy[at, :]
        for grads in sides:
            for j in range(3):
                total = total + dg(grads[j][:, at], grads[3][j], 0, 1)
        out.near[...] = total.astype(bf16)
        out.store()


def place_of(slot, core, length):
    place = slot[pl.ds(core, 1), :]
    half = length // 2
    return jnp.where(core == 0, place, jnp.where(place >= half, place - half, place + half))


def slot_matrix(slot, core, length):
    row = place_of(slot, core, length)
    shape = (length, row.shape[1])
    return jnp.where(lax.broadcasted_iota(jnp.int32, shape, 0) == jnp.broadcast_to(row, shape), 1.0, 0.0).astype(bf16)


def feed_forward(core, ins, smalls, outs, _, scratch):
    gs_m, gs_t, ws_m, ws_t, go_m, go_t, h2_s, wi_m, wi_t, wo_m, wo_t, y2_s = ins
    bi_m, bi_t, ob, gains, shifts, slot = smalls
    out_m, out_t, dy2_s, dc_s, g_m, g_t, small_m, small_t = outs
    onehot, tl, tr, e3, hid, dpre, slope, df_all, states = scratch
    length, width = h2_s.near.shape
    half = length // 2
    fw = wi_m.near.shape[1]
    sw = ws_m.near.shape[1]
    onehot[...] = slot_matrix(slot, core, length)
    for side, (gs, ws) in enumerate(((gs_m, ws_m), (gs_t, ws_t))):
        cols = slice(side * sw, (side + 1) * sw)
        left = dg(onehot[...], gs.wait()[...], 1, 0)
        tl[:, cols] = left.astype(bf16)
        tr[:, cols] = pltpu.roll(left, 1, 0).astype(bf16)
    ws = [ws_m.wait(), ws_t.wait()]
    go = [go_m.wait(), go_t.wait()]
    for i in range(length // TB):
        at = slice(i * TB, (i + 1) * TB)
        piece, inner = divmod(i * TB, half)
        total = go[piece][inner : inner + TB, :].astype(f32)
        for side in range(2):
            cols = slice(side * sw, (side + 1) * sw)
            total = total + dg(tl[at, cols], ws[side][0:width, :], 1, 1) + dg(tr[at, cols], ws[side][width : 2 * width, :], 1, 1)
        e3[at, :] = total
    h2, y2 = h2_s.wait(), y2_s.wait()
    wi = [wi_m.wait(), wi_t.wait()]
    wo = [wo_m.wait(), wo_t.wait()]
    dy2 = dy2_s.near
    dc = dc_s.near
    bias_in = [row_of(bi_m), row_of(bi_t)]
    bias_out = row_of(ob)
    gain2 = gains[1:2, :].astype(f32)
    gain3 = gains[2:3, :].astype(f32)
    shift3 = shifts[2:3, :].astype(f32)

    def one_block(i, sums):
        gain3_sum, shift3_sum, gain2_sum, shift2_sum, ffn_out_sum, cross_out_sum, in_m_sum, in_t_sum = sums
        at = pl.ds(pl.multiple_of(i * FFN_TB, FFN_TB), FFN_TB)
        hb = h2[at, :]
        y3 = hb.astype(f32) + bias_out
        for side in range(2):
            cols = slice(side * fw, (side + 1) * fw)
            pre = dg(hb, wi[side][...], 1, 0) + bias_in[side]
            square = pre * pre
            tanh = jnp.tanh(pre * (GELU_C + GELU_C * GELU_A * square))
            gate = 0.5 + 0.5 * tanh
            hidden = (pre * gate).astype(bf16)
            hid[at, cols] = hidden
            slope[:, cols] = gate + (0.5 * pre) * (1.0 - tanh * tanh) * (GELU_C + 3.0 * GELU_C * GELU_A * square)
            y3 = y3 + dg(hidden, wo[side][...], 1, 0)
        xhat, spread = norm_parts(y3)
        states[at, :] = (xhat * gain3 + shift3).astype(bf16)
        dy3, d_gain, d_shift = norm_back(xhat, spread, gain3, e3[at, :])
        gain3_sum += d_gain
        shift3_sum += d_shift
        df = dy3.astype(bf16)
        df_all[at, :] = df
        ffn_out_sum += jnp.sum(df.astype(f32), axis=0, keepdims=True)
        e2 = dy3
        in_sums = []
        for side, in_sum in enumerate((in_m_sum, in_t_sum)):
            cols = slice(side * fw, (side + 1) * fw)
            back = (dg(df, wo[side][...], 1, 1) * slope[:, cols]).astype(bf16)
            dpre[at, cols] = back
            in_sums.append(in_sum + jnp.sum(back.astype(f32), axis=0, keepdims=True))
            e2 = e2 + dg(back, wi[side][...], 1, 1)
        xhat, spread = norm_parts(y2[at, :])
        back2, d_gain, d_shift = norm_back(xhat, spread, gain2, e2)
        dy2[at, :] = back2
        rounded = back2.astype(bf16)
        dc[at, :] = rounded
        gain2_sum += d_gain
        shift2_sum += d_shift
        cross_out_sum += jnp.sum(rounded.astype(f32), axis=0, keepdims=True)
        return gain3_sum, shift3_sum, gain2_sum, shift2_sum, ffn_out_sum, cross_out_sum, in_sums[0], in_sums[1]

    row = jnp.zeros((1, width), f32)
    wide = jnp.zeros((1, fw), f32)
    sums = lax.fori_loop(0, length // FFN_TB, one_block, (row, row, row, row, row, row, wide, wide))
    dc_s.store()
    dy2_s.store()
    for piece, out in ((1, out_t), (0, out_m)):
        out.near[...] = states[piece * half : (piece + 1) * half, :]
        out.store()
    for side, g in ((1, g_t), (0, g_m)):
        for i in range(fw // width):
            block = slice(side * fw + i * width, side * fw + (i + 1) * width)
            rows = slice(width + i * width, 2 * width + i * width)
            g.near[rows, :] = dg(h2[...], dpre[:, block], 0, 0).astype(bf16)
            g.store(rows)
            rows = slice(width + fw + i * width, 2 * width + fw + i * width)
            g.near[rows, :] = dg(hid[:, block], df_all[...], 0, 0).astype(bf16)
            g.store(rows)
        cols = slice(side * sw, (side + 1) * sw)
        rows = slice(0, width)
        g.near[rows, 0:sw] = dg(states[...], tl[:, cols], 0, 0).astype(bf16)
        g.near[rows, sw : 2 * sw] = dg(states[...], tr[:, cols], 0, 0).astype(bf16)
        g.store(rows)
    for short, total, gs in ((small_m, sums[6], gs_m), (small_t, sums[7], gs_t)):
        short.near[...] = jnp.zeros(short.near.shape, f32)
        for at, one in ((S_GAIN + 2, 0), (S_SHIFT + 2, 1), (S_GAIN + 1, 2), (S_SHIFT + 1, 3), (S_FFN_OB, 4), (S_CROSS_OB, 5)):
            short.near[at : at + 1, :] = sums[one]
        for i in range(fw // width):
            short.near[S_FFN_B + i : S_FFN_B + i + 1, :] = total[:, i * width : (i + 1) * width]
        short.near[S_SLOT_B : S_SLOT_B + 1, 0:sw] = jnp.sum(gs.near[...].astype(f32), axis=0, keepdims=True)
        short.store()


def slot_forward(core, ins, smalls, outs, _, scratch):
    out_m, out_t, ws_m, ws_t = ins
    bs_m, bs_t, slot = smalls
    onehot, states = scratch
    length, width = states.shape
    half = length // 2
    onehot[...] = slot_matrix(slot, core, length)
    states[0:half, :] = out_m.wait()[...]
    states[half:length, :] = out_t.wait()[...]
    for ws_s, short, out in ((ws_t, bs_t, outs[1]), (ws_m, bs_m, outs[0])):
        ws = ws_s.wait()
        top = dg(states[...], ws[0:width, :], 1, 0)
        low = dg(states[...], ws[width : 2 * width, :], 1, 0)
        total = (top + pltpu.roll(low, length - 1, 0) + row_of(short)).astype(bf16)
        out.near[...] = dg(onehot[...], total, 0, 0).astype(bf16)
        out.store()


def joined(scalars, ins):
    bit = scalars[1]
    own, got = ins[0].wait(), ins[1].wait()
    return jnp.where(bit == 0, own[...], got[...]), jnp.where(bit == 0, got[...], own[...])


def put_qkv(out, buf, hw):
    for j in range(3):
        out.near[j, 0:hw, :] = buf[j * hw : (j + 1) * hw, 0:hw].astype(f32)
        out.near[j, hw : 2 * hw, :] = buf[j * hw : (j + 1) * hw, hw : 2 * hw].astype(f32)
    out.store()


def unpack_cross(scalars, ins, smalls, outs, small_outs, scratch):
    (buf,) = scratch
    count = buf.shape[0] // 2
    buf[0:count, :], buf[count:, :] = joined(scalars, ins)
    qkv, cross_out, self_out = outs
    hw = cross_out.near.shape[0]
    put_qkv(qkv, buf, hw)
    cross_out.near[...] = buf[3 * hw : 4 * hw, :].astype(f32)
    cross_out.store()
    self_out.near[...] = buf[4 * hw : 5 * hw, :].astype(f32)
    self_out.store()


def unpack_self(scalars, ins, smalls, outs, small_outs, scratch):
    (buf,) = scratch
    count = buf.shape[0] // 2
    buf[0:count, :], buf[count:, :] = joined(scalars, ins)
    (qkv,) = outs
    hw = qkv.near.shape[2]
    put_qkv(qkv, buf, hw)
    self_b, self_ob, cross_b, cross_ob, ffn_b, ffn_ob, gains, shifts, slot_b = small_outs
    short = buf[3 * hw : 3 * hw + 16, :].astype(f32)
    width = short.shape[1]
    for ref, at in ((self_b, S_SELF_B), (cross_b, S_CROSS_B)):
        ref[0:1, :] = short[at : at + 1, 0:hw]
        ref[1:2, :] = short[at : at + 1, hw : 2 * hw]
    for ref, at in ((self_ob, S_SELF_OB), (cross_ob, S_CROSS_OB), (ffn_ob, S_FFN_OB)):
        ref[...] = short[at : at + 1, :].reshape(width)
    wide = ffn_b.shape[0] // width
    ffn_b[...] = jnp.concatenate([short[S_FFN_B + i : S_FFN_B + i + 1, :] for i in range(wide)], axis=1).reshape(wide * width)
    gains[...] = short[S_GAIN : S_GAIN + 3, :]
    shifts[...] = short[S_SHIFT : S_SHIFT + 3, :]
    slot_b[...] = short[S_SLOT_B : S_SLOT_B + 1, 0 : slot_b.shape[0]].reshape(slot_b.shape[0])


def unpack_ffn(scalars, ins, smalls, outs, _, scratch):
    (buf,) = scratch
    count = buf.shape[0] // 2
    buf[0:count, :], buf[count:, :] = joined(scalars, ins)
    slot_w, ffn_in, ffn_out = outs
    width = buf.shape[1]
    sw = slot_w.near.shape[1]
    slot_w.near[0:width, :] = buf[0:width, 0:sw].astype(f32)
    slot_w.near[width:, :] = buf[0:width, sw : 2 * sw].astype(f32)
    slot_w.store()
    fw = ffn_in.near.shape[1]
    for i in range(fw // width):
        ffn_in.near[:, i * width : (i + 1) * width] = buf[(i + 1) * width : (i + 2) * width, :].astype(f32)
    ffn_in.store()
    ffn_out.near[...] = buf[width + fw :, :].astype(f32)
    ffn_out.store()


def swap(x):
    return lax.ppermute(x, "tensor", [(0, 1), (1, 0)])


class RowSum:
    def __init__(self, x, dp_size, dp_index, core):
        bits = dp_size.bit_length() - 1
        orders = [list(range(bits)), list(range(bits))]
        if bits > 2:
            orders[1] = [1, 2, 0] + list(range(3, bits))
        self.plan = []
        for step in range(bits):
            pairs = []
            for device in range(dp_size):
                for c in range(2):
                    pairs.append((device * 2 + c, (device ^ (1 << orders[c][step])) * 2 + c))
            bit = jnp.where(core == 0, (dp_index >> orders[0][step]) & 1, (dp_index >> orders[1][step]) & 1)
            self.plan.append((pairs, bit.astype(jnp.int32)))
        self.x = x
        self.step = 0
        self.done = False
        self.cut()

    def cut(self):
        if self.step >= len(self.plan) - 1:
            self.away = self.kept = self.x
            return
        bit = self.plan[self.step][1]
        count = self.x.shape[0] // 2
        self.away = lax.dynamic_slice_in_dim(self.x, (1 - bit) * count, count, 0)
        self.kept = lax.dynamic_slice_in_dim(self.x, bit * count, count, 0)

    def scatter(self, *beside):
        got = lax.ppermute(self.away, ("dp", "tensor"), self.plan[self.step][0])
        if beside:
            got = lax.optimization_barrier((got, *beside))[0]
        self.x = (self.kept.astype(f32) + got.astype(f32)).astype(bf16)
        self.step += 1
        self.done = self.step == len(self.plan)
        self.cut()
        if self.done:
            self.step -= 1

    def gather(self, last):
        while self.step > last:
            pairs, bit = self.plan[self.step - 1]
            got = lax.ppermute(self.x, ("dp", "tensor"), pairs)
            self.step -= 1
            if self.step == 0:
                return self.x, got
            first = lax.broadcasted_iota(jnp.int32, (2,) + self.x.shape, 0) == bit
            self.x = jnp.where(first, self.x[None], got[None]).reshape((2 * self.x.shape[0],) + self.x.shape[1:])


def shards(dp_size, *args):
    (tokens, memory, dec_segment, enc_segment, slot_left, self_qkv, self_bias, self_out, self_out_bias,
     cross_qkv, cross_bias, cross_out, cross_out_bias, ffn_in, ffn_in_bias, ffn_out, ffn_out_bias,
     norm_gain, norm_bias, slot_weight, slot_bias, grad_output, grad_slots) = args
    core_index = lax.axis_index("tensor")
    dp_index = lax.axis_index("dp")
    core = core_index.astype(jnp.int32).reshape(1)
    half, width = tokens.shape[1], tokens.shape[2]
    length = 2 * half
    hw = self_qkv.shape[2]
    heads = 2 * hw // HEAD_DIM
    fw = ffn_in.shape[1]
    wide = fw // width
    sw = slot_weight.shape[1]
    slots = slot_left.shape[1]

    tokens_t = swap(tokens)
    self_qkv_t = swap(self_qkv)
    self_bias_t = swap(self_bias)
    self_out_t = swap(self_out)
    memory_t = swap(memory)
    cross_qkv_t = swap(cross_qkv)
    cross_bias_t = swap(cross_bias)
    cross_out_t = swap(cross_out)
    grad_slots_t = swap(grad_slots)
    slot_weight_t = swap(slot_weight)
    grad_output_t = swap(grad_output)
    ffn_in_t = swap(ffn_in)
    ffn_in_bias_t = swap(ffn_in_bias)
    ffn_out_t = swap(ffn_out)
    slot_bias_t = swap(slot_bias)

    aug = (heads, AUG, length)
    blocks = length // TB
    forward_outs = [(aug, bf16, 1), (aug, bf16, 1), (aug, bf16, 1), ((2 * hw, length), bf16, 1),
                    ((length, width), f32, blocks), ((length, width), bf16, blocks)]
    qa, ka, va, ctx, y1, h1 = staged_call(
        functools.partial(attend_forward, False), core,
        [(tokens, "core"), (tokens_t, "core"), (self_qkv, None), (self_qkv_t, None), (self_out, None), (self_out_t, None)],
        [self_bias, self_bias_t, self_out_bias, norm_gain, norm_bias, dec_segment], forward_outs, micros=18)
    qa2, ka2, va2, ctx2, y2, h2 = staged_call(
        functools.partial(attend_forward, True), core,
        [(h1, None), (memory, "core"), (memory_t, "core"), (cross_qkv, None), (cross_qkv_t, None), (cross_out, None),
         (cross_out_t, None)],
        [cross_bias, cross_bias_t, cross_out_bias, norm_gain, norm_bias, dec_segment, enc_segment], forward_outs, micros=18)
    g1_rows = width + 2 * fw
    half_out = ((half, width), bf16, 1)
    out_m, out_t, dy2, dc, g1_m, g1_t, short1_m, short1_t = staged_call(
        feed_forward, core,
        [(grad_slots, "core"), (grad_slots_t, "core"), (slot_weight, None), (slot_weight_t, None), (grad_output, "core"),
         (grad_output_t, "core"), (h2, None), (ffn_in, None), (ffn_in_t, None), (ffn_out, None), (ffn_out_t, None),
         (y2, None)],
        [ffn_in_bias, ffn_in_bias_t, ffn_out_bias, norm_gain, norm_bias, slot_left],
        [half_out, half_out, ((length, width), f32, 1), ((length, width), bf16, 1), ((g1_rows, width), bf16, 1 + 2 * wide),
         ((g1_rows, width), bf16, 1 + 2 * wide), ((16, width), f32, 1), ((16, width), f32, 1)],
        scratch=[pltpu.VMEM((length, slots), bf16), pltpu.VMEM((length, 2 * sw), bf16), pltpu.VMEM((length, 2 * sw), bf16),
                 pltpu.VMEM((length, width), f32), pltpu.VMEM((length, 2 * fw), bf16), pltpu.VMEM((length, 2 * fw), bf16),
                 pltpu.VMEM((FFN_TB, 2 * fw), f32), pltpu.VMEM((length, width), bf16), pltpu.VMEM((length, width), bf16)],
        after=[slot_bias_t], micros=25)
    st_m, st_t = staged_call(
        slot_forward, core, [(out_m, None), (out_t, None), (slot_weight, None), (slot_weight_t, None)],
        [slot_bias, slot_bias_t, slot_left], [((slots, sw), bf16, 1), ((slots, sw), bf16, 1)],
        scratch=[pltpu.VMEM((length, slots), bf16), pltpu.VMEM((length, width), bf16)], micros=4)
    g1_got = lax.optimization_barrier((swap(g1_t), st_m))[0]
    g1 = (g1_m.astype(f32) + g1_got.astype(f32)).astype(bf16)

    def packed(total):
        return total.reshape(dp_size, total.shape[0] // dp_size, width)

    def added(kept, got):
        return (kept.astype(f32) + got.astype(f32)).astype(bf16)

    sum1 = RowSum(packed(g1), dp_size, dp_index, core_index)
    count = heads // 2
    grad_out = ((hw, length), bf16, 1)
    wide_f32 = ((length, width), f32, blocks)
    short_out = ((16, width), f32, 1)
    da_scratch = [pltpu.VMEM((count, AUG, length), bf16)]

    def head_inputs(side, wo, c, v, q, k):
        of = slice(side * count, (side + 1) * count)
        return [(wo[side], None), (c, slice(side * hw, (side + 1) * hw)), (v, of), (q, of), (k, of)]

    cross_inputs = [(dc, None), (h1, None), (memory, "core"), (memory_t, "core")]
    cross_wo = (cross_out, cross_out_t)
    g2_t, short_t, *cross_t = staged_call(
        cross_backward_first, core, cross_inputs + head_inputs(1, cross_wo, ctx2, va2, qa2, ka2), [short1_t],
        [((4 * hw, width), bf16, 4), short_out] + [grad_out] * 3, scratch=da_scratch, after=[sum1.away], micros=15)
    sum1.scatter()
    g2_m, short2_m, short2_t, *cross_m, dy1, do1, so_t = staged_call(
        cross_backward_second, core,
        cross_inputs + head_inputs(0, cross_wo, ctx2, va2, qa2, ka2)
        + [(dy2, None), (y1, None), (cross_t[0], None), (cross_qkv, slice(0, 1)), (cross_qkv_t, slice(0, 1)), (ctx, None)],
        [norm_gain, short1_m, short_t],
        [((5 * hw, width), bf16, 5), short_out, short_out] + [grad_out] * 3
        + [wide_f32, ((length, width), bf16, 1), ((hw, width), bf16, 1)],
        scratch=da_scratch, after=[sum1.away], micros=17)
    sum1.scatter()
    dmem_m, dmem_t = staged_call(
        memory_gradient, core,
        [(cross_m[1], None), (cross_m[2], None), (cross_qkv, None), (cross_t[1], None), (cross_t[2], None), (cross_qkv_t, None)],
        [], [half_out, half_out], after=[sum1.away], micros=4)
    so_got = lax.optimization_barrier((swap(so_t), dmem_m))[0]
    sum2 = RowSum(packed(added(g2_m, jnp.concatenate([swap(g2_t), so_got], axis=0))), dp_size, dp_index, core_index)
    sum1.scatter()
    g3_rows = 3 * hw + 16 + (-(3 * hw + 16)) % 128
    g3_rows += -g3_rows % dp_size
    sides = {}
    held = [dmem_m]
    for side in (1, 0):
        g3, *grads = staged_call(
            self_backward, core,
            [(do1, None), (tokens, "core"), (tokens_t, "core")] + head_inputs(side, (self_out, self_out_t), ctx, va, qa, ka),
            [(short2_m, short2_t)[side]], [((g3_rows, width), bf16, 4)] + [grad_out] * 3, scratch=da_scratch,
            after=held + [sum1.away, sum2.away], micros=15)
        if not sum1.done:
            sum1.scatter()
        sum2.scatter()
        held = []
        sides[side] = (g3, [(g, None) for g in grads] + [((self_qkv, self_qkv_t)[side], None)])
    while not sum1.done:
        sum1.scatter()
    sum1.gather(len(sum1.plan) - 2)

    def together(kept, sent):
        got = swap(sent)
        return jnp.where(lax.broadcasted_iota(jnp.int32, (2,) + kept.shape, 0) == core_index, kept[None], got[None])

    output = together(out_m, out_t)
    slot_states = together(st_m, st_t)
    grad_memory = together(dmem_m, dmem_t)
    g3_got = lax.optimization_barrier((swap(sides[1][0]), sum1.x, sum2.away))[0]
    sum3 = RowSum(packed(added(sides[0][0], g3_got)), dp_size, dp_index, core_index)
    dx_m, dx_t = staged_call(input_gradient, core, sides[0][1] + sides[1][1] + [(dy1, None)], [], [half_out, half_out], micros=5)
    sum3.scatter(output, slot_states, grad_memory)
    while not sum2.done:
        sum2.scatter()
    while not sum3.done:
        sum3.scatter()
    grad_input = together(dx_m, dx_t)

    def ends(total):
        own, got = total.gather(0)
        flat = lambda x: x.reshape(-1, width)
        return jnp.stack([core_index.astype(jnp.int32), total.plan[0][1]]), [(flat(own), None), (flat(got), None)]

    qkv_out = ((3, 2 * hw, hw), f32, 1)
    scalars, halves = ends(sum1)
    grad_slot_weight, grad_ffn_in, grad_ffn_out = staged_call(
        unpack_ffn, scalars, halves, [], [((2 * width, sw), f32, 1), ((width, fw), f32, 1), ((fw, width), f32, 1)],
        scratch=[pltpu.VMEM((g1_rows, width), bf16)], micros=4)
    scalars, halves = ends(sum2)
    grad_cross_qkv, grad_cross_out, grad_self_out = staged_call(
        unpack_cross, scalars, halves, [], [qkv_out, ((hw, width), f32, 1), ((hw, width), f32, 1)],
        scratch=[pltpu.VMEM((5 * hw, width), bf16)], micros=3)
    scalars, halves = ends(sum3)
    (grad_self_qkv, grad_self_bias, grad_self_out_bias, grad_cross_bias, grad_cross_out_bias, grad_ffn_in_bias,
     grad_ffn_out_bias, grad_norm_gain, grad_norm_bias, grad_slot_bias) = staged_call(
        unpack_self, scalars, halves, [], [qkv_out],
        [((2, hw), f32), ((width,), f32), ((2, hw), f32), ((width,), f32), ((fw,), f32), ((width,), f32), ((3, width), f32),
         ((3, width), f32), ((sw,), f32)],
        scratch=[pltpu.VMEM((g3_rows, width), bf16)], micros=3)
    return (
        output, slot_states, grad_input, grad_memory, grad_self_qkv, grad_self_bias, grad_self_out, grad_self_out_bias,
        grad_cross_qkv, grad_cross_bias, grad_cross_out, grad_cross_out_bias, grad_ffn_in, grad_ffn_in_bias, grad_ffn_out,
        grad_ffn_out_bias, grad_norm_gain, grad_norm_bias, grad_slot_weight, grad_slot_bias,
    )


def solution(mesh):
    row3 = P("dp", "tensor", None)
    seg = P("dp", None)
    col3 = P(None, None, "tensor")
    col2 = P(None, "tensor")
    out2 = P("tensor", None)
    one = P("tensor")
    in_specs = (row3, row3, seg, seg, seg, col3, col2, out2, P(), col3, col2, out2, P(), col2, one, out2, P(), P(), P(),
                col2, one, row3, P("dp", None, "tensor"))
    out_specs = (row3, P("dp", None, "tensor"), row3, row3, col3, col2, out2, P(), col3, col2, out2, P(), col2, one, out2,
                 P(), P(), P(), col2, one)
    body = functools.partial(shards, mesh.shape["dp"])
    return jax.shard_map(body, mesh=mesh, in_specs=in_specs, out_specs=out_specs, check_vma=False)
```

```python
import functools
import math

import jax
import jax.numpy as jnp
from jax import lax
from jax.experimental import pallas as pl
from jax.experimental.pallas import tpu as pltpu
from jax.sharding import PartitionSpec as P

HEAD_DIM = 64
EPSILON = 1e-05
MASKED = -1e30
GELU_C = 0.7978845608028654
GELU_A = 0.044715
LOG2E = 1.4426950408889634
LN2 = 0.6931471805599453
SCALE = HEAD_DIM ** (-0.5)
AUG = 80
QB = 256
FWD_QB = 1024
FWD_HEADS = 4
FFN_TB = 512
TB = 256
VMEM_LIMIT = 63 * 2**20
SPARE = 20 * 2**20

bf16 = jnp.bfloat16
f32 = jnp.float32


def dg(a, b, ca, cb):
    return lax.dot_general(a, b, (((ca,), (cb,)), ((), ())), preferred_element_type=f32)


def column_of(row):
    return jnp.broadcast_to(row.astype(f32), (8, row.shape[1])).T[:, 0:1]


def three_parts(row):
    high = row.astype(bf16).astype(f32)
    rest = row - high
    middle = rest.astype(bf16).astype(f32)
    return high, middle, (rest - middle)


def tall(shape, rows):
    index = lax.broadcasted_iota(jnp.int32, shape, 0)
    block = jnp.zeros(shape, f32)
    for at, row in rows.items():
        block = jnp.where(index == at, jnp.broadcast_to(row, shape), block)
    return block


def norm_parts(y):
    centre = y - jnp.mean(y, axis=-1, keepdims=True)
    spread = lax.rsqrt(jnp.mean(centre * centre, axis=-1, keepdims=True) + EPSILON)
    return centre * spread, spread


def norm_back(xhat, spread, gain, e):
    a = e * gain
    dy = (a - jnp.mean(a, axis=-1, keepdims=True) - xhat * jnp.mean(a * xhat, axis=-1, keepdims=True)) * spread
    return dy, jnp.sum(e * xhat, axis=0, keepdims=True), jnp.sum(e, axis=0, keepdims=True)


ANY = pl.BlockSpec(memory_space=pl.ANY)
HBM = pl.BlockSpec(memory_space=pltpu.HBM)
VMEM = pl.BlockSpec(memory_space=pltpu.VMEM)
SMEM = pl.BlockSpec(memory_space=pltpu.SMEM)


class Staged:
    def __init__(self, far, near, sems, first, pick=None):
        self.far, self.near, self.sems, self.next, self.pending, self.pick = far, near, sems, first, [], pick

    def load(self):
        source = self.far if self.pick is None else self.far.at[self.pick]
        copy = pltpu.make_async_copy(source, self.near, self.sems.at[self.next])
        copy.start()
        self.pending.append(copy)

    def store(self, rows=None):
        near, far = (self.near, self.far) if rows is None else (self.near.at[rows], self.far.at[rows])
        copy = pltpu.make_async_copy(near, far, self.sems.at[self.next])
        self.next += 1
        copy.start()
        self.pending.append(copy)

    def wait(self):
        for copy in self.pending:
            copy.wait()
        self.pending = []
        return self.near


def staged_call(body, scalars, big_ins, small_ins, outs, small_outs=(), scratch=(), after=(), micros=10.0, pinned=False):
    def shape_of(a, part):
        if part is None:
            return a.shape
        return a.shape[1:] if part == "core" else (part.stop - part.start,) + a.shape[1:]

    def kernel(*refs):
        refs = list(refs)
        take = lambda n: [refs.pop(0) for _ in range(n)]
        (scalar_ref,) = take(1)
        far_in, smalls, _, far_out = take(len(big_ins)), take(len(small_ins)), take(len(after)), take(len(outs))
        short_out, buf_in, buf_out = take(len(small_outs)), take(len(big_ins)), take(len(outs))
        sem_in, sem_out = take(2)
        me = [scalar_ref[i] for i in range(scalars.shape[0])]
        ins = [
            Staged(far, near, sem_in, i, me[0] if part == "core" else part)
            for i, (far, near, (_, part)) in enumerate(zip(far_in, buf_in, big_ins))
        ]
        for one in ins:
            one.load()
        first = 0
        results = []
        for far, near, (_, _, n) in zip(far_out, buf_out, outs):
            results.append(Staged(far, near, sem_out, first))
            first += n
        body(me if len(me) > 1 else me[0], ins, smalls, results, short_out, refs)
        for one in ins + results:
            one.wait()

    held = [(shape_of(a, part), a.dtype) for a, part in big_ins] + [(s, d) for s, d, _ in outs]
    held += [(one.shape, one.dtype) for one in scratch]
    size = sum(math.prod(s) * jnp.dtype(d).itemsize for s, d in held)
    far = [pltpu.with_memory_space_constraint(a, pltpu.HBM) for a, _ in big_ins]
    if pinned:
        small_ins = [pltpu.with_memory_space_constraint(a, pltpu.HBM) for a in small_ins]
    return pl.pallas_call(
        kernel,
        out_shape=[pltpu.HBM(s, d) for s, d, _ in outs] + [jax.ShapeDtypeStruct(s, d) for s, d in small_outs],
        in_specs=[SMEM] + [HBM] * len(big_ins) + [VMEM] * len(small_ins) + [ANY] * len(after),
        out_specs=[HBM] * len(outs) + [VMEM] * len(small_outs),
        scratch_shapes=[pltpu.VMEM(shape_of(a, part), a.dtype) for a, part in big_ins]
        + [pltpu.VMEM(s, d) for s, d, _ in outs]
        + [pltpu.SemaphoreType.DMA((len(big_ins),)), pltpu.SemaphoreType.DMA((max(1, sum(o[2] for o in outs)),))]
        + list(scratch),
        compiler_params=pltpu.CompilerParams(vmem_limit_bytes=min(VMEM_LIMIT, size + SPARE)),
        cost_estimate=pl.CostEstimate(flops=int(micros * 1.1e9), bytes_accessed=1024, transcendentals=0),
    )(scalars, *far, *small_ins, *after)


def row_of(ref):
    return ref[...].astype(f32).reshape(1, ref.shape[0])


S_GAIN, S_SHIFT, S_SELF_OB, S_CROSS_OB, S_FFN_OB, S_SELF_B, S_CROSS_B, S_FFN_B, S_SLOT_B = 0, 3, 6, 7, 8, 9, 10, 11, 13


def own_first(row, core):
    half = row.shape[1] // 2
    return jnp.where(core == 0, row, jnp.concatenate([row[:, half:], row[:, :half]], axis=1))


def attend_forward(cross, core, ins, smalls, outs, _, scratch):
    qa_s, ka_s, va_s, ctx_s, y_s, h_s = outs
    qa, ka, va, ctx, y_out, h_out = [o.near for o in outs]
    if cross:
        src_s, k_m, k_t, w_m, w_t, wo_m, wo_t = ins
        bias_m, bias_t, out_bias, gains, shifts, seg_d, seg_e = smalls
    else:
        k_m, k_t, w_m, w_t, wo_m, wo_t = ins
        bias_m, bias_t, out_bias, gains, shifts, seg_d = smalls
        seg_e = seg_d
    heads, _, length = qa.shape
    half = length // 2
    hw = w_m.near.shape[2]
    heads_half = heads // 2
    seg_q = own_first(seg_d[pl.ds(core, 1), :], core)
    seg_k = own_first(seg_e[pl.ds(core, 1), :], core)
    shape16 = (16, length)
    index = lax.broadcasted_iota(jnp.int32, shape16, 0)
    same_q = index == jnp.broadcast_to(seg_q, shape16)
    same_k = index == jnp.broadcast_to(seg_k, shape16)
    q_extra = jnp.where(index < 4, jnp.where(same_q, 0.0, MASKED), 0.0).astype(bf16)
    k_extra = jnp.where(index < 4, jnp.where(same_k, 1.0, 0.0), jnp.where(index < 7, 1.0, 0.0)).astype(bf16)
    v_extra = jnp.where(index < 3, 1.0, 0.0).astype(bf16)
    for h in range(heads):
        qa[h, 64:80, :] = q_extra
        ka[h, 64:80, :] = k_extra
        va[h, 64:80, :] = v_extra
    src_k = [k_m.wait(), k_t.wait()]
    if cross:
        src = src_s.wait()
        src_q = [src.at[0:half], src.at[half:length]]
    else:
        src_q = src_k
    for side, (w_s, short) in enumerate(((w_m, bias_m), (w_t, bias_t))):
        w = w_s.wait()
        bias_q = column_of(short[0:1, :])
        bias_v = column_of(short[1:2, :])
        for piece in range(2):
            at = slice(piece * half, (piece + 1) * half)
            q = ((dg(w[0], src_q[piece][...], 0, 1) + bias_q) * (SCALE * LOG2E)).astype(bf16)
            k = dg(w[1], src_k[piece][...], 0, 1).astype(bf16)
            v = (dg(w[2], src_k[piece][...], 0, 1) + bias_v).astype(bf16)
            for i in range(heads_half):
                h = side * heads_half + i
                rows = slice(i * HEAD_DIM, (i + 1) * HEAD_DIM)
                qa[h, 0:64, at] = q[rows]
                ka[h, 0:64, at] = k[rows]
                va[h, 0:64, at] = v[rows]
    ka_s.store()
    va_s.store()

    def some_heads(step, _):
        items = [(step * FWD_HEADS + j, slice(i, i + FWD_QB)) for j in range(FWD_HEADS) for i in range(0, length, FWD_QB)]

        def scores_of(item):
            h, at = item
            return dg(ka[h], qa[h, :, at], 0, 0)

        scores = scores_of(items[0])
        for n, (h, at) in enumerate(items):
            following = scores_of(items[n + 1]) if n + 1 < len(items) else None
            top = jnp.max(scores, axis=0, keepdims=True)
            weights = jnp.exp2(scores - top).astype(bf16)
            out = dg(va[h], weights, 1, 0)
            total = out[64:65, :]
            ctx[pl.ds(pl.multiple_of(h * HEAD_DIM, HEAD_DIM), HEAD_DIM), at] = (out[0:64, :] * (1.0 / total)).astype(bf16)
            high, middle, low = three_parts(-(top + jnp.log2(total)))
            extra = tall((16, FWD_QB), {4: high, 5: middle, 6: low})
            qa[h, 64:80, at] = qa[h, 64:80, at] + extra.astype(bf16)
            scores = following
        return 0

    lax.fori_loop(0, heads // FWD_HEADS, some_heads, 0)
    qa_s.store()
    ctx_s.store()
    norm = 1 if cross else 0
    bias = row_of(out_bias)
    gain = gains[norm : norm + 1, :].astype(f32)
    shift = shifts[norm : norm + 1, :].astype(f32)
    wo = [wo_m.wait(), wo_t.wait()]
    for i in range(length // TB):
        at = slice(i * TB, (i + 1) * TB)
        y = dg(ctx[0:hw, at], wo[0][...], 0, 0) + dg(ctx[hw:, at], wo[1][...], 0, 0) + bias
        piece, inner = divmod(i * TB, half)
        y = y + src_q[piece][inner : inner + TB, :].astype(f32)
        y_out[at, :] = y
        y_s.store(at)
        xhat, _ = norm_parts(y)
        h_out[at, :] = (xhat * gain + shift).astype(bf16)
        h_s.store(at)


def back_heads(count, qa, ka, va, da, ctx, dq, dk, dv):
    length = qa.shape[2]

    def one_head(h, _):
        rows = pl.ds(pl.multiple_of(h * HEAD_DIM, HEAD_DIM), HEAD_DIM)
        keys = ka[h]
        values = va[h]
        inner = jnp.sum(da[h, 0:64, :].astype(f32) * ctx[rows, :].astype(f32), axis=0, keepdims=True)
        high, middle, low = three_parts(-inner)
        da[h, 64:80, :] = tall((16, length), {0: high, 1: middle, 2: low}).astype(bf16)
        cuts = [slice(i * QB, (i + 1) * QB) for i in range(length // QB)]

        def products(at):
            return dg(qa[h, :, at], keys, 0, 0), dg(da[h, :, at], values, 0, 0)

        ahead = products(cuts[0])
        for n, at in enumerate(cuts):
            scores, spread = ahead
            if n + 1 < len(cuts):
                ahead = products(cuts[n + 1])
            weights = jnp.exp2(scores)
            ds = (weights * spread).astype(bf16)
            dv_part = dg(da[h, 0:64, at], weights.astype(bf16), 1, 0)
            dk_part = dg(qa[h, 0:64, at], ds, 1, 0)
            dv_sum = dv_part if n == 0 else dv_sum + dv_part
            dk_sum = dk_part if n == 0 else dk_sum + dk_part
            dq[rows, at] = (dg(keys[0:64], ds, 1, 1) * SCALE).astype(bf16)
        dk[rows, :] = (dk_sum * LN2).astype(bf16)
        dv[rows, :] = dv_sum.astype(bf16)
        return 0

    lax.fori_loop(0, count, one_head, 0)


def weight_rows(g, grads, sources):
    for j, (grad, pair) in enumerate(zip(grads, sources)):
        hw, length = grad.shape
        half = length // 2
        total = dg(pair[0][...], grad[:, 0:half], 0, 1) + dg(pair[1][...], grad[:, half:length], 0, 1)
        put = slice(j * hw, (j + 1) * hw)
        inner = total.shape[0] // 2
        g.near[put, 0:hw] = total[0:inner].astype(bf16)
        g.near[put, hw : 2 * hw] = total[inner:].astype(bf16)
        g.store(put)


def position_sums(dq, dv):
    ones = jnp.ones((8, dq.shape[1]), bf16)
    return dg(ones, dq[...], 1, 1)[0:1], dg(ones, dv[...], 1, 1)[0:1]


def heads_backward(ins, outs, da, dout):
    wo, ctx, va, qa, ka = ins
    dctx = dg(wo.wait()[...], dout[...], 1, 1).astype(bf16)
    for i in range(da.shape[0]):
        da[i, 0:64, :] = dctx[i * HEAD_DIM : (i + 1) * HEAD_DIM]
    ctx, va, qa, ka = ctx.wait(), va.wait(), qa.wait(), ka.wait()
    grads = [one.near for one in outs]
    back_heads(qa.shape[0], qa, ka, va, da, ctx, *grads)
    for one in outs:
        one.store()
    return grads


def halves_of(staged):
    if len(staged) == 2:
        return [one.wait() for one in staged]
    whole = staged[0].wait()
    half = whole.shape[0] // 2
    return [whole.at[0:half], whole.at[half : 2 * half]]


def out_rows(g, ctx, dout):
    hw = ctx.shape[0]
    put = slice(3 * hw, 4 * hw)
    g.near[put, :] = dg(ctx[...], dout[...], 1, 0).astype(bf16)
    g.store(put)


def cross_backward_first(core, ins, smalls, outs, _, scratch):
    do_s, src_s, k_m, k_t = ins[0:4]
    short, = smalls
    g, ns = outs[0:2]
    dout = do_s.wait()
    grads = heads_backward(ins[4:9], outs[2:5], scratch[0], dout)
    out_rows(g, ins[5].near, dout)
    src_k = [k_m.wait(), k_t.wait()]
    weight_rows(g, grads, [halves_of([src_s]), src_k, src_k])
    q_sum, v_sum = position_sums(grads[0], grads[2])
    ns.near[...] = short[...]
    ns.near[S_CROSS_B : S_CROSS_B + 1, :] = jnp.concatenate([q_sum, v_sum], axis=1)
    ns.store()


def cross_backward_second(core, ins, smalls, outs, _, scratch):
    do_s, src_s, k_m, k_t = ins[0:4]
    dy_s, y_s, dqt_s, wq_m, wq_t, ctx1_s = ins[9:15]
    gains, short_m, short_t = smalls
    g, ns_m, ns_t = outs[0:3]
    dprev_s, do1_s, so_t = outs[6:9]
    dout = do_s.wait()
    grads = heads_backward(ins[4:9], outs[3:6], scratch[0], dout)
    dq_m = grads[0]
    dq_t = dqt_s.wait()
    w = [wq_m.wait(), wq_t.wait()]
    y_prev = y_s.wait()
    dy = dy_s.wait()
    length, width = dy.shape
    hw = dq_m.shape[0]
    dprev = dprev_s.near
    dout1 = do1_s.near
    gain = gains[0:1, :].astype(f32)
    gain_sum = jnp.zeros((1, width), f32)
    shift_sum = jnp.zeros((1, width), f32)
    out_sum = jnp.zeros((1, width), f32)
    for i in range(length // TB):
        at = slice(i * TB, (i + 1) * TB)
        e = dy[at, :] + dg(dq_m[:, at], w[0][0], 0, 1) + dg(dq_t[:, at], w[1][0], 0, 1)
        xhat, spread = norm_parts(y_prev[at, :])
        back, d_gain, d_shift = norm_back(xhat, spread, gain, e)
        dprev[at, :] = back
        dprev_s.store(at)
        rounded = back.astype(bf16)
        dout1[at, :] = rounded
        gain_sum += d_gain
        shift_sum += d_shift
        out_sum += jnp.sum(rounded.astype(f32), axis=0, keepdims=True)
    do1_s.store()
    ctx1 = ctx1_s.wait()
    so_t.near[...] = dg(ctx1[hw : 2 * hw, :], dout1[...], 1, 0).astype(bf16)
    so_t.store()
    out_rows(g, ins[5].near, dout)
    put = slice(4 * hw, 5 * hw)
    g.near[put, :] = dg(ctx1[0:hw, :], dout1[...], 1, 0).astype(bf16)
    g.store(put)
    src_k = [k_m.wait(), k_t.wait()]
    weight_rows(g, grads, [halves_of([src_s]), src_k, src_k])
    q_sum, v_sum = position_sums(grads[0], grads[2])
    for short, ns in ((short_m, ns_m), (short_t, ns_t)):
        ns.near[...] = short[...]
        ns.near[S_GAIN : S_GAIN + 1, :] = gain_sum
        ns.near[S_SHIFT : S_SHIFT + 1, :] = shift_sum
        ns.near[S_SELF_OB : S_SELF_OB + 1, :] = out_sum
    ns_m.near[S_CROSS_B : S_CROSS_B + 1, :] = jnp.concatenate([q_sum, v_sum], axis=1)
    ns_m.store()
    ns_t.store()


def self_backward(core, ins, smalls, outs, _, scratch):
    do_s, x_m, x_t = ins[0:3]
    (short,) = smalls
    g = outs[0]
    grads = heads_backward(ins[3:8], outs[1:4], scratch[0], do_s.wait())
    src = [x_m.wait(), x_t.wait()]
    weight_rows(g, grads, [src] * 3)
    q_sum, v_sum = position_sums(grads[0], grads[2])
    own = jnp.concatenate([q_sum, v_sum], axis=1)
    index = lax.broadcasted_iota(jnp.int32, short.shape, 0)
    rows = jnp.where(index == S_SELF_B, jnp.broadcast_to(own, short.shape), short[...])
    start = 3 * grads[0].shape[0]
    stop, end = start + short.shape[0], g.near.shape[0]
    g.near[start:stop, :] = rows.astype(bf16)
    if stop < end:
        g.near[stop:end, :] = jnp.zeros((end - stop, g.near.shape[1]), bf16)
    g.store(slice(start, end))


def memory_gradient(core, ins, smalls, outs, _, scratch):
    out_m, out_t = outs
    sides = [[one.wait() for one in ins[0:3]], [one.wait() for one in ins[3:6]]]
    half = out_m.near.shape[0]
    for piece, out in ((1, out_t), (0, out_m)):
        at = slice(piece * half, (piece + 1) * half)
        total = None
        for dk, dv, w in sides:
            part = dg(dk[:, at], w[1], 0, 1) + dg(dv[:, at], w[2], 0, 1)
            total = part if total is None else total + part
        out.near[...] = total.astype(bf16)
        out.store()


def input_gradient(core, ins, smalls, outs, _, scratch):
    dy_s = ins[-1]
    out_m, out_t = outs
    sides = [[one.wait() for one in ins[0:4]], [one.wait() for one in ins[4:8]]]
    dy = dy_s.wait()
    half = out_m.near.shape[0]
    for piece, out in ((1, out_t), (0, out_m)):
        at = slice(piece * half, (piece + 1) * half)
        total = dy[at, :]
        for grads in sides:
            for j in range(3):
                total = total + dg(grads[j][:, at], grads[3][j], 0, 1)
        out.near[...] = total.astype(bf16)
        out.store()


def place_of(slot, core, length):
    place = slot[pl.ds(core, 1), :]
    half = length // 2
    return jnp.where(core == 0, place, jnp.where(place >= half, place - half, place + half))


def slot_matrix(slot, core, length):
    row = place_of(slot, core, length)
    shape = (length, row.shape[1])
    return jnp.where(lax.broadcasted_iota(jnp.int32, shape, 0) == jnp.broadcast_to(row, shape), 1.0, 0.0).astype(bf16)


def feed_forward(core, ins, smalls, outs, _, scratch):
    gs_m, gs_t, ws_m, ws_t, go_m, go_t, h2_s, wi_m, wi_t, wo_m, wo_t, y2_s = ins
    bi_m, bi_t, ob, gains, shifts, slot = smalls
    out_m, out_t, dy2_s, dc_s, g_m, g_t, small_m, small_t = outs
    onehot, tl, tr, e3, hid, dpre, slope, df_all, states = scratch
    length, width = h2_s.near.shape
    half = length // 2
    fw = wi_m.near.shape[1]
    sw = ws_m.near.shape[1]
    onehot[...] = slot_matrix(slot, core, length)
    for side, (gs, ws) in enumerate(((gs_m, ws_m), (gs_t, ws_t))):
        cols = slice(side * sw, (side + 1) * sw)
        left = dg(onehot[...], gs.wait()[...], 1, 0)
        tl[:, cols] = left.astype(bf16)
        tr[:, cols] = pltpu.roll(left, 1, 0).astype(bf16)
    ws = [ws_m.wait(), ws_t.wait()]
    go = [go_m.wait(), go_t.wait()]
    for i in range(length // TB):
        at = slice(i * TB, (i + 1) * TB)
        piece, inner = divmod(i * TB, half)
        total = go[piece][inner : inner + TB, :].astype(f32)
        for side in range(2):
            cols = slice(side * sw, (side + 1) * sw)
            total = total + dg(tl[at, cols], ws[side][0:width, :], 1, 1) + dg(tr[at, cols], ws[side][width : 2 * width, :], 1, 1)
        e3[at, :] = total
    h2, y2 = h2_s.wait(), y2_s.wait()
    wi = [wi_m.wait(), wi_t.wait()]
    wo = [wo_m.wait(), wo_t.wait()]
    dy2 = dy2_s.near
    dc = dc_s.near
    bias_in = [row_of(bi_m), row_of(bi_t)]
    bias_out = row_of(ob)
    gain2 = gains[1:2, :].astype(f32)
    gain3 = gains[2:3, :].astype(f32)
    shift3 = shifts[2:3, :].astype(f32)

    def one_block(i, sums):
        gain3_sum, shift3_sum, gain2_sum, shift2_sum, ffn_out_sum, cross_out_sum, in_m_sum, in_t_sum = sums
        at = pl.ds(pl.multiple_of(i * FFN_TB, FFN_TB), FFN_TB)
        hb = h2[at, :]
        y3 = hb.astype(f32) + bias_out
        for side in range(2):
            cols = slice(side * fw, (side + 1) * fw)
            pre = dg(hb, wi[side][...], 1, 0) + bias_in[side]
            square = pre * pre
            tanh = jnp.tanh(pre * (GELU_C + GELU_C * GELU_A * square))
            gate = 0.5 + 0.5 * tanh
            hidden = (pre * gate).astype(bf16)
            hid[at, cols] = hidden
            slope[:, cols] = gate + (0.5 * pre) * (1.0 - tanh * tanh) * (GELU_C + 3.0 * GELU_C * GELU_A * square)
            y3 = y3 + dg(hidden, wo[side][...], 1, 0)
        xhat, spread = norm_parts(y3)
        states[at, :] = (xhat * gain3 + shift3).astype(bf16)
        dy3, d_gain, d_shift = norm_back(xhat, spread, gain3, e3[at, :])
        gain3_sum += d_gain
        shift3_sum += d_shift
        df = dy3.astype(bf16)
        df_all[at, :] = df
        ffn_out_sum += jnp.sum(df.astype(f32), axis=0, keepdims=True)
        e2 = dy3
        in_sums = []
        for side, in_sum in enumerate((in_m_sum, in_t_sum)):
            cols = slice(side * fw, (side + 1) * fw)
            back = (dg(df, wo[side][...], 1, 1) * slope[:, cols]).astype(bf16)
            dpre[at, cols] = back
            in_sums.append(in_sum + jnp.sum(back.astype(f32), axis=0, keepdims=True))
            e2 = e2 + dg(back, wi[side][...], 1, 1)
        xhat, spread = norm_parts(y2[at, :])
        back2, d_gain, d_shift = norm_back(xhat, spread, gain2, e2)
        dy2[at, :] = back2
        rounded = back2.astype(bf16)
        dc[at, :] = rounded
        gain2_sum += d_gain
        shift2_sum += d_shift
        cross_out_sum += jnp.sum(rounded.astype(f32), axis=0, keepdims=True)
        return gain3_sum, shift3_sum, gain2_sum, shift2_sum, ffn_out_sum, cross_out_sum, in_sums[0], in_sums[1]

    row = jnp.zeros((1, width), f32)
    wide = jnp.zeros((1, fw), f32)
    sums = lax.fori_loop(0, length // FFN_TB, one_block, (row, row, row, row, row, row, wide, wide))
    dc_s.store()
    dy2_s.store()
    for piece, out in ((1, out_t), (0, out_m)):
        out.near[...] = states[piece * half : (piece + 1) * half, :]
        out.store()
    for side, g in ((1, g_t), (0, g_m)):
        for i in range(fw // width):
            block = slice(side * fw + i * width, side * fw + (i + 1) * width)
            rows = slice(width + i * width, 2 * width + i * width)
            g.near[rows, :] = dg(h2[...], dpre[:, block], 0, 0).astype(bf16)
            g.store(rows)
            rows = slice(width + fw + i * width, 2 * width + fw + i * width)
            g.near[rows, :] = dg(hid[:, block], df_all[...], 0, 0).astype(bf16)
            g.store(rows)
        cols = slice(side * sw, (side + 1) * sw)
        rows = slice(0, width)
        g.near[rows, 0:sw] = dg(states[...], tl[:, cols], 0, 0).astype(bf16)
        g.near[rows, sw : 2 * sw] = dg(states[...], tr[:, cols], 0, 0).astype(bf16)
        g.store(rows)
    for short, total, gs in ((small_m, sums[6], gs_m), (small_t, sums[7], gs_t)):
        short.near[...] = jnp.zeros(short.near.shape, f32)
        for at, one in ((S_GAIN + 2, 0), (S_SHIFT + 2, 1), (S_GAIN + 1, 2), (S_SHIFT + 1, 3), (S_FFN_OB, 4), (S_CROSS_OB, 5)):
            short.near[at : at + 1, :] = sums[one]
        for i in range(fw // width):
            short.near[S_FFN_B + i : S_FFN_B + i + 1, :] = total[:, i * width : (i + 1) * width]
        short.near[S_SLOT_B : S_SLOT_B + 1, 0:sw] = jnp.sum(gs.near[...].astype(f32), axis=0, keepdims=True)
        short.store()


def slot_forward(core, ins, smalls, outs, _, scratch):
    out_m, out_t, ws_m, ws_t = ins
    bs_m, bs_t, slot = smalls
    onehot, states = scratch
    length, width = states.shape
    half = length // 2
    onehot[...] = slot_matrix(slot, core, length)
    states[0:half, :] = out_m.wait()[...]
    states[half:length, :] = out_t.wait()[...]
    for ws_s, short, out in ((ws_t, bs_t, outs[1]), (ws_m, bs_m, outs[0])):
        ws = ws_s.wait()
        top = dg(states[...], ws[0:width, :], 1, 0)
        low = dg(states[...], ws[width : 2 * width, :], 1, 0)
        total = (top + pltpu.roll(low, length - 1, 0) + row_of(short)).astype(bf16)
        out.near[...] = dg(onehot[...], total, 0, 0).astype(bf16)
        out.store()


def joined(scalars, ins):
    bit = scalars[1]
    own, got = ins[0].wait(), ins[1].wait()
    return jnp.where(bit == 0, own[...], got[...]), jnp.where(bit == 0, got[...], own[...])


def put_qkv(out, buf, hw):
    for j in range(3):
        out.near[j, 0:hw, :] = buf[j * hw : (j + 1) * hw, 0:hw].astype(f32)
        out.near[j, hw : 2 * hw, :] = buf[j * hw : (j + 1) * hw, hw : 2 * hw].astype(f32)
    out.store()


def unpack_cross(scalars, ins, smalls, outs, small_outs, scratch):
    (buf,) = scratch
    count = buf.shape[0] // 2
    buf[0:count, :], buf[count:, :] = joined(scalars, ins)
    qkv, cross_out, self_out = outs
    hw = cross_out.near.shape[0]
    put_qkv(qkv, buf, hw)
    cross_out.near[...] = buf[3 * hw : 4 * hw, :].astype(f32)
    cross_out.store()
    self_out.near[...] = buf[4 * hw : 5 * hw, :].astype(f32)
    self_out.store()


def unpack_self(scalars, ins, smalls, outs, small_outs, scratch):
    (buf,) = scratch
    count = buf.shape[0] // 2
    buf[0:count, :], buf[count:, :] = joined(scalars, ins)
    (qkv,) = outs
    hw = qkv.near.shape[2]
    put_qkv(qkv, buf, hw)
    self_b, self_ob, cross_b, cross_ob, ffn_b, ffn_ob, gains, shifts, slot_b = small_outs
    short = buf[3 * hw : 3 * hw + 16, :].astype(f32)
    width = short.shape[1]
    for ref, at in ((self_b, S_SELF_B), (cross_b, S_CROSS_B)):
        ref[0:1, :] = short[at : at + 1, 0:hw]
        ref[1:2, :] = short[at : at + 1, hw : 2 * hw]
    for ref, at in ((self_ob, S_SELF_OB), (cross_ob, S_CROSS_OB), (ffn_ob, S_FFN_OB)):
        ref[...] = short[at : at + 1, :].reshape(width)
    wide = ffn_b.shape[0] // width
    ffn_b[...] = jnp.concatenate([short[S_FFN_B + i : S_FFN_B + i + 1, :] for i in range(wide)], axis=1).reshape(wide * width)
    gains[...] = short[S_GAIN : S_GAIN + 3, :]
    shifts[...] = short[S_SHIFT : S_SHIFT + 3, :]
    slot_b[...] = short[S_SLOT_B : S_SLOT_B + 1, 0 : slot_b.shape[0]].reshape(slot_b.shape[0])


def unpack_ffn(scalars, ins, smalls, outs, _, scratch):
    (buf,) = scratch
    count = buf.shape[0] // 2
    buf[0:count, :], buf[count:, :] = joined(scalars, ins)
    slot_w, ffn_in, ffn_out = outs
    width = buf.shape[1]
    sw = slot_w.near.shape[1]
    slot_w.near[0:width, :] = buf[0:width, 0:sw].astype(f32)
    slot_w.near[width:, :] = buf[0:width, sw : 2 * sw].astype(f32)
    slot_w.store()
    fw = ffn_in.near.shape[1]
    for i in range(fw // width):
        ffn_in.near[:, i * width : (i + 1) * width] = buf[(i + 1) * width : (i + 2) * width, :].astype(f32)
    ffn_in.store()
    ffn_out.near[...] = buf[width + fw :, :].astype(f32)
    ffn_out.store()


def swap(x):
    return lax.ppermute(x, "tensor", [(0, 1), (1, 0)])


class RowSum:
    def __init__(self, x, dp_size, dp_index, core):
        bits = dp_size.bit_length() - 1
        orders = [list(range(bits)), list(range(bits))]
        if bits > 2:
            orders[1] = [1, 2, 0] + list(range(3, bits))
        self.plan = []
        for step in range(bits):
            pairs = []
            for device in range(dp_size):
                for c in range(2):
                    pairs.append((device * 2 + c, (device ^ (1 << orders[c][step])) * 2 + c))
            bit = jnp.where(core == 0, (dp_index >> orders[0][step]) & 1, (dp_index >> orders[1][step]) & 1)
            self.plan.append((pairs, bit.astype(jnp.int32)))
        self.x = x
        self.step = 0
        self.done = False
        self.cut()

    def cut(self):
        if self.step >= len(self.plan) - 1:
            self.away = self.kept = self.x
            return
        bit = self.plan[self.step][1]
        count = self.x.shape[0] // 2
        self.away = lax.dynamic_slice_in_dim(self.x, (1 - bit) * count, count, 0)
        self.kept = lax.dynamic_slice_in_dim(self.x, bit * count, count, 0)

    def scatter(self, *beside):
        got = lax.ppermute(self.away, ("dp", "tensor"), self.plan[self.step][0])
        if beside:
            got = lax.optimization_barrier((got, *beside))[0]
        self.x = (self.kept.astype(f32) + got.astype(f32)).astype(bf16)
        self.step += 1
        self.done = self.step == len(self.plan)
        self.cut()
        if self.done:
            self.step -= 1

    def gather(self, last, *beside):
        while self.step > last:
            pairs, bit = self.plan[self.step - 1]
            got = lax.ppermute(self.x, ("dp", "tensor"), pairs)
            self.step -= 1
            if self.step == 0:
                return self.x, got
            if beside and self.step == last:
                got = lax.optimization_barrier((got, *beside))[0]
            first = lax.broadcasted_iota(jnp.int32, (2,) + self.x.shape, 0) == bit
            self.x = jnp.where(first, self.x[None], got[None]).reshape((2 * self.x.shape[0],) + self.x.shape[1:])


def shards(dp_size, *args):
    (tokens, memory, dec_segment, enc_segment, slot_left, self_qkv, self_bias, self_out, self_out_bias,
     cross_qkv, cross_bias, cross_out, cross_out_bias, ffn_in, ffn_in_bias, ffn_out, ffn_out_bias,
     norm_gain, norm_bias, slot_weight, slot_bias, grad_output, grad_slots) = args
    core_index = lax.axis_index("tensor")
    dp_index = lax.axis_index("dp")
    core = core_index.astype(jnp.int32).reshape(1)
    half, width = tokens.shape[1], tokens.shape[2]
    length = 2 * half
    hw = self_qkv.shape[2]
    heads = 2 * hw // HEAD_DIM
    fw = ffn_in.shape[1]
    wide = fw // width
    sw = slot_weight.shape[1]
    slots = slot_left.shape[1]

    tokens_t = swap(tokens)
    self_qkv_t = swap(self_qkv)
    self_bias_t = swap(self_bias)
    self_out_t = swap(self_out)
    memory_t = swap(memory)
    cross_qkv_t = swap(cross_qkv)
    cross_bias_t = swap(cross_bias)
    cross_out_t = swap(cross_out)
    grad_slots_t = swap(grad_slots)
    slot_weight_t = swap(slot_weight)
    grad_output_t = swap(grad_output)
    ffn_in_t = swap(ffn_in)
    ffn_in_bias_t = swap(ffn_in_bias)
    ffn_out_t = swap(ffn_out)
    slot_bias_t = swap(slot_bias)

    aug = (heads, AUG, length)
    blocks = length // TB
    forward_outs = [(aug, bf16, 1), (aug, bf16, 1), (aug, bf16, 1), ((2 * hw, length), bf16, 1),
                    ((length, width), f32, blocks), ((length, width), bf16, blocks)]
    qa, ka, va, ctx, y1, h1 = staged_call(
        functools.partial(attend_forward, False), core,
        [(tokens, "core"), (tokens_t, "core"), (self_qkv, None), (self_qkv_t, None), (self_out, None), (self_out_t, None)],
        [self_bias, self_bias_t, self_out_bias, norm_gain, norm_bias, dec_segment], forward_outs, micros=18, pinned=True)
    qa2, ka2, va2, ctx2, y2, h2 = staged_call(
        functools.partial(attend_forward, True), core,
        [(h1, None), (memory, "core"), (memory_t, "core"), (cross_qkv, None), (cross_qkv_t, None), (cross_out, None),
         (cross_out_t, None)],
        [cross_bias, cross_bias_t, cross_out_bias, norm_gain, norm_bias, dec_segment, enc_segment], forward_outs, micros=18)
    g1_rows = width + 2 * fw
    half_out = ((half, width), bf16, 1)
    out_m, out_t, dy2, dc, g1_m, g1_t, short1_m, short1_t = staged_call(
        feed_forward, core,
        [(grad_slots, "core"), (grad_slots_t, "core"), (slot_weight, None), (slot_weight_t, None), (grad_output, "core"),
         (grad_output_t, "core"), (h2, None), (ffn_in, None), (ffn_in_t, None), (ffn_out, None), (ffn_out_t, None),
         (y2, None)],
        [ffn_in_bias, ffn_in_bias_t, ffn_out_bias, norm_gain, norm_bias, slot_left],
        [half_out, half_out, ((length, width), f32, 1), ((length, width), bf16, 1), ((g1_rows, width), bf16, 1 + 2 * wide),
         ((g1_rows, width), bf16, 1 + 2 * wide), ((16, width), f32, 1), ((16, width), f32, 1)],
        scratch=[pltpu.VMEM((length, slots), bf16), pltpu.VMEM((length, 2 * sw), bf16), pltpu.VMEM((length, 2 * sw), bf16),
                 pltpu.VMEM((length, width), f32), pltpu.VMEM((length, 2 * fw), bf16), pltpu.VMEM((length, 2 * fw), bf16),
                 pltpu.VMEM((FFN_TB, 2 * fw), f32), pltpu.VMEM((length, width), bf16), pltpu.VMEM((length, width), bf16)],
        after=[slot_bias_t], micros=25)
    st_m, st_t = staged_call(
        slot_forward, core, [(out_m, None), (out_t, None), (slot_weight, None), (slot_weight_t, None)],
        [slot_bias, slot_bias_t, slot_left], [((slots, sw), bf16, 1), ((slots, sw), bf16, 1)],
        scratch=[pltpu.VMEM((length, slots), bf16), pltpu.VMEM((length, width), bf16)], micros=4)
    g1_got = lax.optimization_barrier((swap(g1_t), st_m))[0]
    g1 = (g1_m.astype(f32) + g1_got.astype(f32)).astype(bf16)

    def packed(total):
        return total.reshape(dp_size, total.shape[0] // dp_size, width)

    def added(kept, got):
        return (kept.astype(f32) + got.astype(f32)).astype(bf16)

    sum1 = RowSum(packed(g1), dp_size, dp_index, core_index)
    count = heads // 2
    grad_out = ((hw, length), bf16, 1)
    wide_f32 = ((length, width), f32, blocks)
    short_out = ((16, width), f32, 1)
    da_scratch = [pltpu.VMEM((count, AUG, length), bf16)]

    def head_inputs(side, wo, c, v, q, k):
        of = slice(side * count, (side + 1) * count)
        return [(wo[side], None), (c, slice(side * hw, (side + 1) * hw)), (v, of), (q, of), (k, of)]

    cross_inputs = [(dc, None), (h1, None), (memory, "core"), (memory_t, "core")]
    cross_wo = (cross_out, cross_out_t)
    g2_t, short_t, *cross_t = staged_call(
        cross_backward_first, core, cross_inputs + head_inputs(1, cross_wo, ctx2, va2, qa2, ka2), [short1_t],
        [((4 * hw, width), bf16, 4), short_out] + [grad_out] * 3, scratch=da_scratch, after=[sum1.away], micros=15)
    sum1.scatter()
    g2_m, short2_m, short2_t, *cross_m, dy1, do1, so_t = staged_call(
        cross_backward_second, core,
        cross_inputs + head_inputs(0, cross_wo, ctx2, va2, qa2, ka2)
        + [(dy2, None), (y1, None), (cross_t[0], None), (cross_qkv, slice(0, 1)), (cross_qkv_t, slice(0, 1)), (ctx, None)],
        [norm_gain, short1_m, short_t],
        [((5 * hw, width), bf16, 5), short_out, short_out] + [grad_out] * 3
        + [wide_f32, ((length, width), bf16, 1), ((hw, width), bf16, 1)],
        scratch=da_scratch, after=[sum1.away], micros=17)
    sum1.scatter()
    dmem_m, dmem_t = staged_call(
        memory_gradient, core,
        [(cross_m[1], None), (cross_m[2], None), (cross_qkv, None), (cross_t[1], None), (cross_t[2], None), (cross_qkv_t, None)],
        [], [half_out, half_out], after=[sum1.away], micros=4)
    so_got = lax.optimization_barrier((swap(so_t), dmem_m))[0]
    sum2 = RowSum(packed(added(g2_m, jnp.concatenate([swap(g2_t), so_got], axis=0))), dp_size, dp_index, core_index)
    sum1.scatter()
    g3_rows = 3 * hw + 16 + (-(3 * hw + 16)) % 128
    g3_rows += -g3_rows % dp_size
    sides = {}
    held = [dmem_m]
    for side in (1, 0):
        g3, *grads = staged_call(
            self_backward, core,
            [(do1, None), (tokens, "core"), (tokens_t, "core")] + head_inputs(side, (self_out, self_out_t), ctx, va, qa, ka),
            [(short2_m, short2_t)[side]], [((g3_rows, width), bf16, 4)] + [grad_out] * 3, scratch=da_scratch,
            after=held + [sum1.away, sum2.away], micros=15)
        if not sum1.done:
            sum1.scatter()
        sum2.scatter()
        held = []
        sides[side] = (g3, [(g, None) for g in grads] + [((self_qkv, self_qkv_t)[side], None)])
    while not sum1.done:
        sum1.scatter()
    sum1.gather(len(sum1.plan) - 2)

    def together(kept, sent):
        got = swap(sent)
        return jnp.where(lax.broadcasted_iota(jnp.int32, (2,) + kept.shape, 0) == core_index, kept[None], got[None])

    output = together(out_m, out_t)
    slot_states = together(st_m, st_t)
    grad_memory = together(dmem_m, dmem_t)
    g3_got = lax.optimization_barrier((swap(sides[1][0]), sum1.x, sum2.away))[0]
    sum3 = RowSum(packed(added(sides[0][0], g3_got)), dp_size, dp_index, core_index)
    dx_m, dx_t = staged_call(input_gradient, core, sides[0][1] + sides[1][1] + [(dy1, None)], [], [half_out, half_out],
                             after=[sum3.away], micros=5)
    sum2.scatter(sum3.away)
    sum3.scatter(dx_m)
    sum3.scatter(output, slot_states, grad_memory)
    while not sum2.done:
        sum2.scatter()
    while not sum3.done:
        sum3.scatter()
    grad_input = together(dx_m, dx_t)

    def ends(total):
        own, got = total.gather(0)
        flat = lambda x: x.reshape(-1, width)
        return jnp.stack([core_index.astype(jnp.int32), total.plan[0][1]]), [(flat(own), None), (flat(got), None)]

    qkv_out = ((3, 2 * hw, hw), f32, 1)
    scalars, halves = ends(sum1)
    grad_slot_weight, grad_ffn_in, grad_ffn_out = staged_call(
        unpack_ffn, scalars, halves, [], [((2 * width, sw), f32, 1), ((width, fw), f32, 1), ((fw, width), f32, 1)],
        scratch=[pltpu.VMEM((g1_rows, width), bf16)], micros=4)
    scalars, halves = ends(sum2)
    grad_cross_qkv, grad_cross_out, grad_self_out = staged_call(
        unpack_cross, scalars, halves, [], [qkv_out, ((hw, width), f32, 1), ((hw, width), f32, 1)],
        scratch=[pltpu.VMEM((5 * hw, width), bf16)], micros=3)
    sum3.gather(1, grad_ffn_out)
    scalars, halves = ends(sum3)
    (grad_self_qkv, grad_self_bias, grad_self_out_bias, grad_cross_bias, grad_cross_out_bias, grad_ffn_in_bias,
     grad_ffn_out_bias, grad_norm_gain, grad_norm_bias, grad_slot_bias) = staged_call(
        unpack_self, scalars, halves, [], [qkv_out],
        [((2, hw), f32), ((width,), f32), ((2, hw), f32), ((width,), f32), ((fw,), f32), ((width,), f32), ((3, width), f32),
         ((3, width), f32), ((sw,), f32)],
        scratch=[pltpu.VMEM((g3_rows, width), bf16)], micros=3)
    return (
        output, slot_states, grad_input, grad_memory, grad_self_qkv, grad_self_bias, grad_self_out, grad_self_out_bias,
        grad_cross_qkv, grad_cross_bias, grad_cross_out, grad_cross_out_bias, grad_ffn_in, grad_ffn_in_bias, grad_ffn_out,
        grad_ffn_out_bias, grad_norm_gain, grad_norm_bias, grad_slot_weight, grad_slot_bias,
    )


def solution(mesh):
    row3 = P("dp", "tensor", None)
    seg = P("dp", None)
    col3 = P(None, None, "tensor")
    col2 = P(None, "tensor")
    out2 = P("tensor", None)
    one = P("tensor")
    in_specs = (row3, row3, seg, seg, seg, col3, col2, out2, P(), col3, col2, out2, P(), col2, one, out2, P(), P(), P(),
                col2, one, row3, P("dp", None, "tensor"))
    out_specs = (row3, P("dp", None, "tensor"), row3, row3, col3, col2, out2, P(), col3, col2, out2, P(), col2, one, out2,
                 P(), P(), P(), col2, one)
    body = functools.partial(shards, mesh.shape["dp"])
    return jax.shard_map(body, mesh=mesh, in_specs=in_specs, out_specs=out_specs, check_vma=False)
```
